32 devices in a mesh: batch: 16 (over z, y, core), seq: 2 (over x).
Axes of the slice: x: 2, y: 2, z: 4, core: 2. Of those that a mesh axis runs over, the one named last changes fastest.
Arguments:
- inputs: bfloat16 [16, 1024, 512], P('batch', 'seq'), may hold values from -6 to 6
- memory: bfloat16 [16, 512, 512], P('batch'), may hold values from -6 to 6
- cotangent: bfloat16 [16, 1024, 512], P('batch', 'seq'), may hold values from -3 to 3
- labels: int32 [16, 1024], P('batch', 'seq'), may hold values from 0 to 1, as said below
- attention_gain: float32 [512], replicated, may hold values from 0.5 to 1.5
- query_weight: bfloat16 [512, 512], replicated, may hold values from -0.25 to 0.25
- key_weight: bfloat16 [512, 512], replicated, may hold values from -0.25 to 0.25
- value_weight: bfloat16 [512, 512], replicated, may hold values from -0.25 to 0.25
- out_weight: bfloat16 [512, 512], replicated, may hold values from -4 to 4
- forward_gain: float32 [512], replicated, may hold values from 0.5 to 1.5
- up_weight: bfloat16 [512, 2048], replicated, may hold values from -0.25 to 0.25
- down_weight: bfloat16 [2048, 512], replicated, may hold values from -0.125 to 0.125
- boundary_hidden: bfloat16 [512, 2048], replicated, may hold values from -0.25 to 0.25
- boundary_out: bfloat16 [2048], replicated, may hold values from -0.375 to 0.375
Outputs:
- outputs: bfloat16 [16, 1024, 512], P('batch', 'seq')
- input_grad: float32 [16, 1024, 512], P('batch', 'seq')
- attention_gain_grad: float32 [512], replicated
- query_weight_grad: float32 [512, 512], replicated
- key_weight_grad: float32 [512, 512], replicated
- value_weight_grad: float32 [512, 512], replicated
- out_weight_grad: float32 [512, 512], replicated
- forward_gain_grad: float32 [512], replicated
- up_weight_grad: float32 [512, 2048], replicated
- down_weight_grad: float32 [2048, 512], replicated
- boundary_hidden_grad: float32 [512, 2048], replicated
- boundary_out_grad: float32 [2048], replicated
The draws below stay inside these ranges and needn't reach their ends.
Inputs may be any that keep to these rules, and one draw needn't show every extreme that they name: `labels`: 1 marks the last byte of a segment; most segments are 2 to 6 bytes, a few are hundreds of bytes long.
All inputs are finite; a program needn't handle non-finite values.
Results may differ from the reference program's by a relative error of at most 0.014.
Values may be sent and summed in bfloat16 or wider, within the bound.
No kernel may reach another device: no remote copies, remote signals or barrier semaphores. Data moves between devices by JAX's collectives and lax.ppermute only.
A program may use at most 128 MiB of HBM per device.

```python
import math
import jax
import jax.numpy as jnp
from jax import lax

D = 512
HEADS = 8
FF = 2048
PH = 2048
BLK = 512
SEQS = 16
L = 1024


def draw_labels(key, part):
    key = jax.random.fold_in(key, 11)
    first_key, second_key, third_key = jax.random.split(key, 3)
    short_gaps = jax.random.randint(first_key, (SEQS, L), 2, 7)
    long_gaps = jax.random.randint(second_key, (SEQS, L), 100, 400)
    picked = jax.random.randint(third_key, (SEQS, L), 0, 64) == 0
    gaps = jnp.where(picked, long_gaps, short_gaps).astype(jnp.int32)
    ends = jnp.cumsum(gaps, axis=1).astype(jnp.int32) - 1
    sequence = jnp.broadcast_to(jnp.arange(SEQS, dtype=jnp.int32)[:, None], (SEQS, L))
    labels = jnp.zeros((SEQS, L), jnp.int32).at[sequence, ends].set(1, mode='drop')
    return labels


def block_levels(own_key, dims, shards, least, largest):
    level = 1.0
    for position, parts in shards:
        heights = jax.random.uniform(jax.random.fold_in(jax.random.fold_in(own_key, 6), position), (parts,), jnp.float32, least / len(shards), largest / len(shards))
        level = level * jnp.repeat(jnp.exp(heights), dims[position] // parts).reshape((-1,) + (1,) * (len(dims) - 1 - position))
    return level


def bell_draw(stream_key, shape, scale, limit, pieces=(), kind=jnp.bfloat16):
    result = jax.random.normal(stream_key, shape, jnp.float32) * scale
    if len(pieces) > 0:
        result = block_levels(stream_key, shape, pieces, -0.22, 0.18) * result
    return jnp.clip(result, min=-limit, max=limit).astype(kind)


def setup_inputs(seed: int = 0) -> dict:
    arg_keys = jax.random.split(jax.random.key(seed), 15)
    inputs = bell_draw(arg_keys[0], (SEQS, L, D), 1.0, 6.0, ((0, 16), (1, 2)))
    memory = bell_draw(arg_keys[1], (SEQS, BLK, D), 1.0, 6.0, ((0, 16),))
    cotangent = bell_draw(arg_keys[2], (SEQS, L, D), 0.5, 3.0, ((0, 16), (1, 2)))
    labels = draw_labels(jax.random.fold_in(arg_keys[14], 71), 0)
    attention_gain = jnp.clip(1.0 + 0.1 * jax.random.normal(arg_keys[4], (D,), jnp.float32), 0.5, 1.5)
    query_weight = bell_draw(arg_keys[5], (D, D), D ** -0.5, 0.25)
    key_weight = bell_draw(arg_keys[6], (D, D), D ** -0.5, 0.25)
    value_weight = bell_draw(arg_keys[7], (D, D), D ** -0.5, 0.25)
    out_weight = bell_draw(arg_keys[8], (D, D), (2 * D // BLK) ** -0.5, 4.0)
    forward_gain = jnp.clip(1.0 + 0.1 * jax.random.normal(arg_keys[9], (D,), jnp.float32), 0.5, 1.5)
    up_weight = bell_draw(arg_keys[10], (D, FF), D ** -0.5, 0.25)
    down_weight = bell_draw(arg_keys[11], (FF, D), FF ** -0.5, 0.125)
    boundary_hidden = bell_draw(arg_keys[12], (D, PH), D ** -0.5, 0.25)
    boundary_out = bell_draw(arg_keys[13], (PH,), (PH // 8) ** -0.5, 0.375)
    return {"inputs": inputs, "memory": memory, "cotangent": cotangent, "labels": labels, "attention_gain": attention_gain, "query_weight": query_weight, "key_weight": key_weight, "value_weight": value_weight, "out_weight": out_weight, "forward_gain": forward_gain, "up_weight": up_weight, "down_weight": down_weight, "boundary_hidden": boundary_hidden, "boundary_out": boundary_out}


EPS = 1e-05
BASE = 10000.0
HIGH = lax.Precision.HIGHEST

@jax.custom_vjp
def low(v):
    return lax.optimization_barrier(v.astype(jnp.bfloat16)).astype(jnp.float32)

@jax.custom_vjp
def low_back(v):
    return v

def low_keep(v):
    return (low(v), None)

def low_pass(kept, grad):
    return (grad,)

def back_keep(v):
    return (v, None)

def back_low(kept, grad):
    return (low(grad),)
low.defvjp(low_keep, low_pass)
low_back.defvjp(back_keep, back_low)

def layer_norm(values, gain):
    centre = values - lax.optimization_barrier(jnp.mean(values, axis=-1, keepdims=True))
    spread = lax.optimization_barrier(jnp.mean(centre * centre, axis=-1, keepdims=True))
    return centre * lax.rsqrt(spread + EPS) * gain

def rotary_tables(positions, width):
    half = width // 2
    freqs = BASE ** (-(jnp.arange(half, dtype=jnp.float32) * 2.0 / width))
    angles = positions[:, None] * freqs[None, :]
    return (jnp.cos(angles), jnp.sin(angles))

def rotate(values, cosine, sine):
    half = values.shape[-1] // 2
    front = values[..., :half]
    back = values[..., half:]
    cosine = cosine[:, None, :]
    sine = sine[:, None, :]
    return jnp.concatenate([front * cosine - back * sine, back * cosine + front * sine], axis=-1)

def window_mask(block):
    query = lax.broadcasted_iota(jnp.int32, (block, 2 * block), 0)
    column = lax.broadcasted_iota(jnp.int32, (block, 2 * block), 1)
    return jnp.where(column < block, column > query, column - block <= query)

def attend_block(blocks):
    queries, key_window, value_window = blocks
    scale = 1.0 / math.sqrt(queries.shape[-1])
    scores = low_back(scale * jnp.einsum('qhd,khd->hqk', queries, key_window, precision=HIGH))
    scores = jnp.where(window_mask(queries.shape[0])[None], scores, -1e+30)
    weights = jax.nn.softmax(scores, axis=-1)
    return jnp.einsum('hqk,khd->qhd', low(weights), value_window, precision=HIGH)

def layer(rows, memory_rows, attention_gain, query_weight, key_weight, value_weight, out_weight, forward_gain, up_weight, down_weight, boundary_hidden, boundary_out, cotangent, targets):
    group, length, width = rows.shape
    head_width = width // HEADS
    blocks = length // BLK

    def project(source, weight):
        return jnp.einsum('gld,de->gle', source, weight, precision=HIGH)
    normed = low(layer_norm(rows, attention_gain))
    remembered = low(layer_norm(memory_rows, attention_gain))
    own_cos, own_sin = rotary_tables(jnp.arange(length, dtype=jnp.float32), head_width)
    side_cos, side_sin = rotary_tables(jnp.arange(BLK, dtype=jnp.float32) - BLK, head_width)
    shape = (group, length, HEADS, head_width)
    side_shape = (group, BLK, HEADS, head_width)
    queries = low(rotate(low_back(project(normed, query_weight)).reshape(shape), own_cos, own_sin))
    keys = low(rotate(low_back(project(normed, key_weight)).reshape(shape), own_cos, own_sin))
    values = low(low_back(project(normed, value_weight))).reshape(shape)
    memory_keys = low(rotate(low_back(project(remembered, key_weight)).reshape(side_shape), side_cos, side_sin))
    memory_values = low(low_back(project(remembered, value_weight))).reshape(side_shape)

    def split_blocks(values_all):
        return values_all.reshape(group, blocks, BLK, HEADS, head_width)

    def flatten(values_all):
        return values_all.reshape((group * blocks,) + values_all.shape[2:])
    key_blocks = split_blocks(keys)
    value_blocks = split_blocks(values)
    key_window = jnp.concatenate([jnp.concatenate([memory_keys[:, None], key_blocks[:, :-1]], axis=1), key_blocks], axis=2)
    value_window = jnp.concatenate([jnp.concatenate([memory_values[:, None], value_blocks[:, :-1]], axis=1), value_blocks], axis=2)
    mixed = lax.map(jax.checkpoint(attend_block), (flatten(split_blocks(queries)), flatten(key_window), flatten(value_window)))
    mixed = low(low_back(mixed.reshape(group, length, width)))
    hidden = rows + low_back(project(mixed, out_weight))
    normed_hidden = low(layer_norm(hidden, forward_gain))
    gated = low(jax.nn.gelu(low_back(project(normed_hidden, up_weight))))
    final = hidden + low_back(project(gated, down_weight))
    probe = low(jax.nn.gelu(low_back(project(low(final), boundary_hidden))))
    logits = low_back(jnp.einsum('gld,d->gl', probe, boundary_out, precision=HIGH))
    entropy = jax.nn.softplus(logits) - targets * logits
    objective = jnp.sum(final * cotangent) + jnp.sum(entropy)
    return (objective, final)

def reference(inputs, memory, cotangent, labels, attention_gain, query_weight, key_weight, value_weight, out_weight, forward_gain, up_weight, down_weight, boundary_hidden, boundary_out):
    group = 4 if SEQS % 4 == 0 else 1
    count = SEQS // group
    params = (attention_gain.astype(jnp.float32), query_weight.astype(jnp.float32), key_weight.astype(jnp.float32), value_weight.astype(jnp.float32), out_weight.astype(jnp.float32), forward_gain.astype(jnp.float32), up_weight.astype(jnp.float32), down_weight.astype(jnp.float32), boundary_hidden.astype(jnp.float32), boundary_out.astype(jnp.float32))

    def regroup(array):
        return array.reshape((count, group) + array.shape[1:])

    def accumulate(totals, piece):
        batch_rows, memory_rows, cotangent_rows, label_rows = piece

        def objective(rows, *weights):
            return layer(rows, memory_rows.astype(jnp.float32), *weights, cotangent_rows.astype(jnp.float32), label_rows.astype(jnp.float32))
        value, backward, final = jax.vjp(objective, batch_rows.astype(jnp.float32), *params, has_aux=True)
        grads = backward(jnp.ones_like(value))
        summed = tuple((total + grad for total, grad in zip(totals, grads[1:])))
        return (summed, (final.astype(jnp.bfloat16), grads[0]))
    zeros = tuple((jnp.zeros(weight.shape, jnp.float32) for weight in params))
    totals, (outputs, input_grad) = lax.scan(accumulate, zeros, (regroup(inputs), regroup(memory), regroup(cotangent), regroup(labels)))
    return (outputs.reshape(SEQS, L, D), input_grad.reshape(SEQS, L, D), totals[0], totals[1], totals[2], totals[3], totals[4], totals[5], totals[6], totals[7], totals[8], totals[9])
```

```python
import math

import jax
import jax.numpy as jnp
from jax import lax
from jax.sharding import PartitionSpec as P

HEADS = 8


EPS = 1e-05
BASE = 10000.0


def passed_along(array, axis, by):
    length = lax.axis_size(axis)
    pairs = [(i, i + by) for i in range(length) if 0 <= i + by < length]
    return lax.ppermute(array, axis, pairs)


def matmul(left, right):
    return jnp.dot(left, right, preferred_element_type=jnp.float32)


def inner_rows(left, right):
    return lax.dot_general(
        left, right, (((0,), (0,)), ((), ())), preferred_element_type=jnp.float32
    )


def outer_rows(left, right):
    return lax.dot_general(
        left, right, (((1,), (1,)), ((), ())), preferred_element_type=jnp.float32
    )


def exchange_steps(batches, blocks):
    number = batches * blocks

    def pairs(partner):
        return [
            (d, p[0] * blocks + p[1])
            for d in range(number)
            for p in [partner(d // blocks, d % blocks)]
        ]

    steps = [(pairs(lambda b, s: (b ^ 1, s)), lambda b, s: b % 2)]
    steps.append(
        (
            pairs(lambda b, s: (b, s ^ 1) if b % 2 == 0 else (b ^ 2, s)),
            lambda b, s: jnp.where(b % 2 == 0, s, (b // 2) % 2),
        )
    )
    steps.append(
        (
            pairs(lambda b, s: (b ^ 2, s) if b % 2 == 0 else (b, s ^ 1)),
            lambda b, s: jnp.where(b % 2 == 0, (b // 2) % 2, s),
        )
    )
    place = 4
    while place < batches:
        steps.append(
            (
                pairs(lambda b, s, place=place: (b ^ place, s)),
                lambda b, s, place=place: (b // place) % 2,
            )
        )
        place *= 2
    return steps


AXES = ("batch", "seq")


def total_of(array, steps, halved):
    row, column = (lax.axis_index("batch"), lax.axis_index("seq"))
    for pairs, bit in steps[:halved]:
        half = array.shape[0] // 2
        mine = bit(row, column)
        sent = lax.dynamic_slice_in_dim(array, (1 - mine) * half, half)
        kept = lax.dynamic_slice_in_dim(array, mine * half, half)
        array = kept + lax.ppermute(sent, AXES, pairs)
    for pairs, bit in steps[halved:]:
        array = array + lax.ppermute(array, AXES, pairs)
    for pairs, bit in reversed(steps[:halved]):
        mine = bit(row, column)
        other = lax.ppermute(array, AXES, pairs)
        array = jnp.concatenate(
            [jnp.where(mine == 0, array, other), jnp.where(mine == 0, other, array)], axis=0
        )
    return array


def layer_norm(values, gain):
    centre = values - jnp.mean(values, axis=-1, keepdims=True)
    spread = jnp.mean(centre * centre, axis=-1, keepdims=True)
    return centre * lax.rsqrt(spread + EPS) * gain


def rotary_tables(positions, width):
    half = width // 2
    freqs = BASE ** (-(jnp.arange(half, dtype=jnp.float32) * 2.0 / width))
    angles = positions[:, None] * freqs[None, :]
    return (jnp.cos(angles), jnp.sin(angles))


def rotate(values, cosine, sine):
    half = values.shape[-1] // 2
    front = values[..., :half]
    back = values[..., half:]
    cosine = cosine[:, None, :]
    sine = sine[:, None, :]
    return jnp.concatenate([front * cosine - back * sine, back * cosine + front * sine], axis=-1)


def window_mask(block):
    query = lax.broadcasted_iota(jnp.int32, (block, 2 * block), 0)
    column = lax.broadcasted_iota(jnp.int32, (block, 2 * block), 1)
    return jnp.where(column < block, column > query, column - block <= query)


def body(
    inputs,
    memory,
    cotangent,
    labels,
    attention_gain,
    query_weight,
    key_weight,
    value_weight,
    out_weight,
    forward_gain,
    up_weight,
    down_weight,
    boundary_hidden,
    boundary_out,
):
    group, block, width = inputs.shape
    head_width = width // HEADS
    total = group * block
    scale = 1.0 / math.sqrt(head_width)
    first = lax.axis_index("seq") == 0
    position = (lax.axis_index("seq") * block + jnp.arange(block, dtype=jnp.int32)).astype(
        jnp.float32
    )
    own_cos, own_sin = rotary_tables(position, head_width)
    side_cos, side_sin = rotary_tables(position - block, head_width)
    mask = window_mask(block)[None]

    def split_heads(values_all):
        return values_all.reshape(group, block, HEADS, head_width)

    def join_heads(values_all):
        return values_all.reshape(total, width)

    rows = inputs.reshape(total, width).astype(jnp.float32)
    normed, normed_back = jax.vjp(layer_norm, rows, attention_gain)
    normed_low = normed.astype(jnp.bfloat16)
    memory_rows = memory.reshape(total, width).astype(jnp.float32)
    remembered, remembered_back = jax.vjp(layer_norm, memory_rows, attention_gain)
    remembered_low = remembered.astype(jnp.bfloat16)

    def side_pairs(source):
        side_keys = rotate(split_heads(matmul(source, key_weight)), side_cos, side_sin).astype(
            jnp.bfloat16
        )
        side_values = split_heads(matmul(source, value_weight).astype(jnp.bfloat16))
        return (side_keys, side_values)

    queries = rotate(split_heads(matmul(normed_low, query_weight)), own_cos, own_sin).astype(
        jnp.bfloat16
    )
    keys = rotate(split_heads(matmul(normed_low, key_weight)), own_cos, own_sin).astype(
        jnp.bfloat16
    )
    values = split_heads(matmul(normed_low, value_weight).astype(jnp.bfloat16))
    sent_keys, sent_values = passed_along((keys, values), "seq", 1)

    def from_memory():
        return side_pairs(remembered_low)

    def from_neighbour():
        return (sent_keys, sent_values)

    halo_keys, halo_values = lax.cond(first, from_memory, from_neighbour)

    def window_scores(query_block, key_window):
        scores = (
            jnp.einsum("qhd,khd->hqk", query_block, key_window, preferred_element_type=jnp.float32)
            * scale
        )
        return jnp.where(mask, scores, -1e30)

    def attend(items):
        query_block, side_key, side_value, own_key, own_value = items
        key_window = jnp.concatenate([side_key, own_key], axis=0)
        value_window = jnp.concatenate([side_value, own_value], axis=0)
        scores = window_scores(query_block, key_window)
        peak = jnp.max(scores, axis=-1, keepdims=True)
        raised = jnp.exp(scores - peak)
        weight_sum = jnp.sum(raised, axis=-1, keepdims=True)
        attention_weights = raised / weight_sum
        mixed = jnp.einsum(
            "hqk,khd->qhd",
            attention_weights.astype(jnp.bfloat16),
            value_window,
            preferred_element_type=jnp.float32,
        )
        return (mixed.astype(jnp.bfloat16), (peak + jnp.log(weight_sum))[..., 0])

    mixed_heads, log_totals = lax.map(attend, (queries, halo_keys, halo_values, keys, values))
    mixed_low = join_heads(mixed_heads)
    hidden = rows + matmul(mixed_low, out_weight)
    normed_hidden, hidden_back = jax.vjp(layer_norm, hidden, forward_gain)
    normed_hidden_low = normed_hidden.astype(jnp.bfloat16)
    gated, gelu_back = jax.vjp(jax.nn.gelu, matmul(normed_hidden_low, up_weight))
    gated_low = gated.astype(jnp.bfloat16)
    final = hidden + matmul(gated_low, down_weight)
    outputs_low = final.astype(jnp.bfloat16)
    probe, probe_back = jax.vjp(jax.nn.gelu, matmul(outputs_low, boundary_hidden))
    probe_low = probe.astype(jnp.bfloat16)
    logits = matmul(probe_low, boundary_out)
    targets = labels.reshape(total).astype(jnp.float32)
    logit_grad = (jax.nn.sigmoid(logits) - targets).astype(jnp.bfloat16)
    boundary_out_grad = matmul(logit_grad, probe_low)
    (probe_pre_grad,) = probe_back(
        logit_grad.astype(jnp.float32)[:, None] * boundary_out.astype(jnp.float32)[None, :]
    )
    probe_grad_low = probe_pre_grad.astype(jnp.bfloat16)
    boundary_hidden_grad = inner_rows(outputs_low, probe_grad_low)
    final_grad = cotangent.reshape(total, width).astype(jnp.float32) + outer_rows(
        probe_grad_low, boundary_hidden
    )
    down_low = final_grad.astype(jnp.bfloat16)
    down_weight_grad = inner_rows(gated_low, down_low)
    (up_grad,) = gelu_back(outer_rows(down_low, down_weight))
    up_low = up_grad.astype(jnp.bfloat16)
    up_weight_grad = inner_rows(normed_hidden_low, up_low)
    hidden_part, forward_gain_grad = hidden_back(outer_rows(up_low, up_weight))
    hidden_grad = final_grad + hidden_part
    mixed_in = hidden_grad.astype(jnp.bfloat16)
    out_weight_grad = inner_rows(mixed_low, mixed_in)
    mixed_grad = split_heads(outer_rows(mixed_in, out_weight).astype(jnp.bfloat16))

    def attend_back(items):
        query_block, side_key, side_value, own_key, own_value, log_total, upstream = items
        key_window = jnp.concatenate([side_key, own_key], axis=0)
        value_window = jnp.concatenate([side_value, own_value], axis=0)
        attention_weights = jnp.exp(window_scores(query_block, key_window) - log_total[..., None])
        weights_low = attention_weights.astype(jnp.bfloat16)
        prob_grad = jnp.einsum(
            "qhd,khd->hqk", upstream, value_window, preferred_element_type=jnp.float32
        )
        centred = jnp.sum(attention_weights * prob_grad, axis=-1, keepdims=True)
        score_grad = (attention_weights * (prob_grad - centred)).astype(jnp.bfloat16)
        query_grad = (
            jnp.einsum("hqk,khd->qhd", score_grad, key_window, preferred_element_type=jnp.float32)
            * scale
        )
        key_grad = (
            jnp.einsum("hqk,qhd->khd", score_grad, query_block, preferred_element_type=jnp.float32)
            * scale
        )
        value_grad = jnp.einsum(
            "hqk,qhd->khd", weights_low, upstream, preferred_element_type=jnp.float32
        )
        return (
            query_grad,
            key_grad[:block],
            value_grad[:block],
            key_grad[block:],
            value_grad[block:],
        )

    query_grad, side_key_grad, side_value_grad, own_key_grad, own_value_grad = lax.map(
        attend_back, (queries, halo_keys, halo_values, keys, values, log_totals, mixed_grad)
    )
    returned_keys, returned_values = passed_along((side_key_grad, side_value_grad), "seq", -1)
    query_low = join_heads(rotate(query_grad, own_cos, -own_sin)).astype(jnp.bfloat16)
    key_low = join_heads(rotate(own_key_grad + returned_keys, own_cos, -own_sin)).astype(
        jnp.bfloat16
    )
    value_low = join_heads(own_value_grad + returned_values).astype(jnp.bfloat16)
    query_weight_grad = inner_rows(normed_low, query_low)
    key_weight_grad = inner_rows(normed_low, key_low)
    value_weight_grad = inner_rows(normed_low, value_low)
    normed_grad = (
        outer_rows(query_low, query_weight)
        + outer_rows(key_low, key_weight)
        + outer_rows(value_low, value_weight)
    )
    rows_part, attention_gain_grad = normed_back(normed_grad)
    input_grad = hidden_grad + rows_part

    def memory_terms():
        side_key_low = join_heads(rotate(side_key_grad, side_cos, -side_sin)).astype(jnp.bfloat16)
        side_value_low = join_heads(side_value_grad).astype(jnp.bfloat16)
        memory_grad = outer_rows(side_key_low, key_weight) + outer_rows(
            side_value_low, value_weight
        )
        ignored, gain_part = remembered_back(memory_grad)
        return (
            inner_rows(remembered_low, side_key_low),
            inner_rows(remembered_low, side_value_low),
            gain_part,
        )

    def no_terms():
        return (
            jnp.zeros_like(key_weight_grad),
            jnp.zeros_like(value_weight_grad),
            jnp.zeros_like(attention_gain_grad),
        )

    memory_key, memory_value, memory_gain = lax.cond(first, memory_terms, no_terms)
    key_weight_grad = key_weight_grad + memory_key
    value_weight_grad = value_weight_grad + memory_value
    attention_gain_grad = attention_gain_grad + memory_gain
    batches, blocks = (lax.axis_size("batch"), lax.axis_size("seq"))
    steps = exchange_steps(batches, blocks)

    def reduced(pieces):
        stacked = jnp.concatenate([p.reshape(-1, 512).astype(jnp.bfloat16) for p in pieces], axis=0)
        return total_of(stacked, steps, 5).astype(jnp.float32)

    hidden_total = reduced([boundary_hidden_grad])
    down_total = reduced([down_weight_grad])
    up_total = reduced([up_weight_grad])
    small = jnp.concatenate([attention_gain_grad, forward_gain_grad, boundary_out_grad])
    small = jnp.pad(small, (0, 512 * 512 - small.shape[0]))
    rest = reduced([query_weight_grad, key_weight_grad, value_weight_grad, out_weight_grad, small])
    small = rest[4 * width : 4 * width + 6].reshape(-1)
    everything = (
        small[:width],
        rest[:width],
        rest[width : 2 * width],
        rest[2 * width : 3 * width],
        rest[3 * width : 4 * width],
        small[width : 2 * width],
        up_total.reshape(up_weight_grad.shape),
        down_total.reshape(down_weight_grad.shape),
        hidden_total.reshape(boundary_hidden_grad.shape),
        small[2 * width :],
    )
    gain_sum, query_sum, key_sum, value_sum, out_sum = (
        everything[0],
        everything[1],
        everything[2],
        everything[3],
        everything[4],
    )
    forward_sum, up_sum, down_sum, boundary_hidden_sum, boundary_out_sum = (
        everything[5],
        everything[6],
        everything[7],
        everything[8],
        everything[9],
    )
    return (
        outputs_low.reshape(group, block, width),
        input_grad.reshape(group, block, width),
        gain_sum,
        query_sum,
        key_sum,
        value_sum,
        out_sum,
        forward_sum,
        up_sum,
        down_sum,
        boundary_hidden_sum,
        boundary_out_sum,
    )


def solution(mesh):
    placed = (
        P("batch", "seq", None),
        P("batch", None, None),
        P("batch", "seq", None),
        P("batch", "seq"),
        P(),
        P(),
        P(),
        P(),
        P(),
        P(),
        P(),
        P(),
        P(),
        P(),
    )
    return jax.shard_map(
        body,
        mesh=mesh,
        in_specs=placed,
        out_specs=(
            P("batch", "seq", None),
            P("batch", "seq", None),
            P(),
            P(),
            P(),
            P(),
            P(),
            P(),
            P(),
            P(),
            P(),
            P(),
        ),
        check_vma=False,
    )
```

```python
import functools
import math

import jax
import jax.numpy as jnp
import numpy as np
from jax import lax
from jax.experimental import pallas as pl
from jax.experimental.pallas import tpu as pltpu
from jax.sharding import PartitionSpec as P

HEADS = 8
HEAD = 64
PAIR = 2 * HEAD
TILE = 256
EPS = 1e-05
BASE = 10000.0
AXES = ("batch", "seq")
F32, BF16 = jnp.float32, jnp.bfloat16
VMEM = pl.BlockSpec(memory_space=pltpu.VMEM)
LIMIT = 56 * 1024 * 1024


def dot(left, right):
    return jnp.dot(left, right, preferred_element_type=F32)


def dot_t(left, right):
    return lax.dot_general(left, right, (((1,), (1,)), ((), ())), preferred_element_type=F32)


def t_dot(left, right):
    return lax.dot_general(left, right, (((0,), (0,)), ((), ())), preferred_element_type=F32)


def normalised(values):
    centre = values - jnp.mean(values, axis=-1, keepdims=True)
    spread = jnp.mean(centre * centre, axis=-1, keepdims=True)
    scale = lax.rsqrt(spread + EPS)
    return centre * scale, scale


def norm_back(unit, scale, gain, upstream):
    product = upstream * unit
    inner = upstream * gain
    mean = jnp.mean(inner, axis=-1, keepdims=True)
    along = jnp.mean(inner * unit, axis=-1, keepdims=True)
    return scale * (inner - mean - unit * along), jnp.sum(product, axis=0, keepdims=True)


def gelu_both(value):
    factor = math.sqrt(2.0 / math.pi)
    square = value * value
    slope = jnp.tanh(value * (factor + (factor * 0.044715) * square))
    half = 0.5 + 0.5 * slope
    bend = (0.5 * value) * (1.0 - slope * slope)
    return value * half, half + bend * (factor + (3.0 * factor * 0.044715) * square)


def turned(values, cosine, sine):
    front = lax.broadcasted_iota(jnp.int32, (values.shape[0], PAIR), 1) % HEAD < HEAD // 2
    parts = []
    for at in range(0, values.shape[1], PAIR):
        part = values[:, at : at + PAIR]
        other = jnp.where(
            front, pltpu.roll(part, PAIR - HEAD // 2, 1), pltpu.roll(part, HEAD // 2, 1)
        )
        parts.append(part * cosine + other * sine)
    return jnp.concatenate(parts, axis=1)


def rotary_tables(first, count):
    positions = np.arange(first, first + count, dtype=np.float32)
    half = HEAD // 2
    freqs = np.float32(BASE) ** (-(np.arange(half, dtype=np.float32) * np.float32(2.0 / HEAD)))
    angles = (positions[:, None] * freqs[None, :].astype(np.float32)).astype(np.float64)
    cosine, sine = (np.cos(angles), np.sin(angles))
    return (
        np.concatenate([cosine] * 4, axis=1).astype(np.float32),
        np.concatenate([-sine, sine] * 2, axis=1).astype(np.float32),
    )


def own_kernel(x_ref, gain_ref, wq_ref, wk_ref, wv_ref, cos_ref, sin_ref, n_ref, q_ref, k_ref, v_ref):
    unit, _ = normalised(x_ref[...].astype(F32))
    low = (unit * gain_ref[...]).astype(BF16)
    n_ref[...] = low
    block = low.shape[0]
    cosine, sine = cos_ref[block:], sin_ref[block:]
    scale = 1.0 / math.sqrt(HEAD)
    q_ref[...] = (turned(dot(low, wq_ref[...]), cosine, sine).astype(BF16).astype(F32) * scale).astype(BF16)
    k_ref[...] = turned(dot(low, wk_ref[...]), cosine, sine).astype(BF16)
    v_ref[...] = dot(low, wv_ref[...]).astype(BF16)


def merged(scores, below):
    return jnp.where(below, scores[:, 2 * TILE :], scores[:, :TILE]), scores[:, TILE : 2 * TILE]


def spread_out(edge, middle, below):
    edge, middle = edge.astype(BF16), middle.astype(BF16)
    none = jnp.zeros_like(edge)
    return jnp.concatenate(
        [jnp.where(below, none, edge), middle, jnp.where(below, edge, none)], axis=1
    )


def below_diagonal():
    row = lax.broadcasted_iota(jnp.int32, (TILE, TILE), 0)
    return lax.broadcasted_iota(jnp.int32, (TILE, TILE), 1) <= row


def forward_kernel(
    x_ref, side_ref, gain_ref, wk_ref, wv_ref, cos_ref, sin_ref, q_ref, k_ref, v_ref,
    wo_ref, fgain_ref, up_ref, down_ref, bh_ref, bo_ref, labels_ref,
    sn_ref, kw_ref, vw_ref, mixed_ref, lse_ref, hidden_ref, nh_ref, gated_ref, slope_ref,
    out_ref, pg_ref, sent_ref, kept_ref, bog_ref,
    probe_ref, pslope_ref, turn_ref,
):
    block, width = x_ref.shape
    unit, _ = normalised(side_ref[...].astype(F32))
    low = (unit * gain_ref[...]).astype(BF16)
    sn_ref[...] = low
    kw_ref[:block] = turned(dot(low, wk_ref[...]), cos_ref[:block], sin_ref[:block]).astype(BF16)
    vw_ref[:block] = dot(low, wv_ref[...]).astype(BF16)
    kw_ref[block:] = k_ref[...]
    vw_ref[block:] = v_ref[...]
    pairs = width // PAIR

    def attend(step, carry):
        pair, tile = step // (block // TILE), step % (block // TILE)
        rows = pl.ds(pl.multiple_of(tile * TILE, TILE), TILE)
        window = pl.ds(pl.multiple_of(tile * TILE, TILE), 3 * TILE)
        lanes = pl.ds(pl.multiple_of(pair * PAIR, PAIR), PAIR)
        query, keys, values = q_ref[rows, lanes], kw_ref[window, lanes], vw_ref[window, lanes]
        lane = lax.broadcasted_iota(jnp.int32, (TILE, PAIR), 1)
        below = below_diagonal()
        mixes, totals = [], lse_ref[rows]
        for head in range(2):
            one = jnp.where(lane // HEAD == head, query, jnp.zeros_like(query))
            edge, middle = merged(dot_t(one, keys), below)
            peak = jnp.maximum(
                jnp.max(edge, axis=-1, keepdims=True), jnp.max(middle, axis=-1, keepdims=True)
            )
            edge, middle = jnp.exp(edge - peak), jnp.exp(middle - peak)
            total = jnp.sum(edge + middle, axis=-1, keepdims=True)
            mixes.append(dot(spread_out(edge, middle, below), values) / total)
            totals = jnp.where(lane == 2 * pair + head, peak + jnp.log(total), totals)
        lse_ref[rows] = totals
        mixed_ref[rows, lanes] = jnp.where(lane < HEAD, mixes[0], mixes[1]).astype(BF16)
        return carry

    lse_ref[...] = jnp.zeros_like(lse_ref)
    lax.fori_loop(0, pairs * (block // TILE), attend, 0)

    hidden = x_ref[...].astype(F32) + dot(mixed_ref[...], wo_ref[...])
    hidden_ref[...] = hidden
    unit, _ = normalised(hidden)
    low = (unit * fgain_ref[...]).astype(BF16)
    nh_ref[...] = low
    final = hidden
    step = 512
    for at in range(0, up_ref.shape[1], step):
        gated, slope = gelu_both(dot(low, up_ref[:, at : at + step]))
        gated = gated.astype(BF16)
        gated_ref[:, at : at + step] = gated
        slope_ref[:, at : at + step] = slope.astype(BF16)
        final = final + dot(gated, down_ref[at : at + step])
    out = final.astype(BF16)
    out_ref[...] = out
    logits = jnp.zeros((block, 1), F32)
    for at in range(0, bh_ref.shape[1], step):
        probe, slope = gelu_both(dot(out, bh_ref[:, at : at + step]))
        probe = probe.astype(BF16)
        probe_ref[:, at : at + step] = probe
        pslope_ref[:, at : at + step] = slope.astype(BF16)
        logits = logits + jnp.sum(
            probe.astype(F32) * bo_ref[:, at : at + step].astype(F32), axis=-1, keepdims=True
        )
    targets = jnp.transpose(jnp.broadcast_to(labels_ref[...].astype(F32), (PAIR, block)))[:, :1]
    signal = (jax.nn.sigmoid(logits) - targets).astype(BF16).astype(F32)
    turn_ref[...] = jnp.transpose(out)
    half = width // 2
    core = lax.axis_index("batch") % 2
    mine = pl.ds(pl.multiple_of(core * half, half), half)
    other = pl.ds(pl.multiple_of((1 - core) * half, half), half)
    for at in range(0, bh_ref.shape[1], step):
        bog_ref[:, at : at + step] = jnp.sum(
            signal * probe_ref[:, at : at + step].astype(F32), axis=0, keepdims=True
        )
        grad = pslope_ref[:, at : at + step].astype(F32) * (
            signal * bo_ref[:, at : at + step].astype(F32)
        )
        grad = grad.astype(BF16)
        pg_ref[:, at : at + step] = grad
        sent_ref[:, at : at + step] = dot(turn_ref[other], grad).astype(BF16)
        kept_ref[:, at : at + step] = dot(turn_ref[mine], grad).astype(BF16)


def down_kernel(pg_ref, bh_ref, cot_ref, gated_ref, slope_ref, down_ref, grad_ref, upg_ref, sent_ref, kept_ref):
    final = cot_ref[...].astype(F32) + dot_t(pg_ref[...], bh_ref[...])
    grad_ref[...] = final
    low = final.astype(BF16)
    step = 512
    half = down_ref.shape[0] // 2
    core = lax.axis_index("batch") % 2
    for at in range(0, half, step):
        rows = pl.ds(pl.multiple_of((1 - core) * half + at, step), step)
        sent_ref[at : at + step] = t_dot(gated_ref[:, rows], low).astype(BF16)
    for at in range(0, half, step):
        rows = pl.ds(pl.multiple_of(core * half + at, step), step)
        kept_ref[at : at + step] = t_dot(gated_ref[:, rows], low).astype(BF16)
    for at in range(0, down_ref.shape[0], step):
        part = slope_ref[:, at : at + step].astype(F32) * dot_t(low, down_ref[at : at + step])
        upg_ref[:, at : at + step] = part.astype(BF16)


def up_kernel(
    nh_ref, upg_ref, up_ref, hidden_ref, fgain_ref, grad_ref, mixed_ref, wo_ref,
    hg_ref, mg_ref, og_ref, fgg_ref, sent_ref, kept_ref, turn_ref,
):
    width = nh_ref.shape[1]
    step = 512
    turn_ref[...] = jnp.transpose(nh_ref[...])
    half = width // 2
    core = lax.axis_index("batch") % 2
    mine = pl.ds(pl.multiple_of(core * half, half), half)
    other = pl.ds(pl.multiple_of((1 - core) * half, half), half)
    upstream = jnp.zeros(nh_ref.shape, F32)
    for at in range(0, up_ref.shape[1], step):
        grad = upg_ref[:, at : at + step]
        sent_ref[:, at : at + step] = dot(turn_ref[other], grad).astype(BF16)
        kept_ref[:, at : at + step] = dot(turn_ref[mine], grad).astype(BF16)
        upstream = upstream + dot_t(grad, up_ref[:, at : at + step])
    unit, scale = normalised(hidden_ref[...])
    part, gain_part = norm_back(unit, scale, fgain_ref[...], upstream)
    fgg_ref[...] = gain_part
    total = grad_ref[...] + part
    hg_ref[...] = total
    low = total.astype(BF16)
    og_ref[...] = t_dot(mixed_ref[...], low).astype(BF16)
    mg_ref[...] = dot_t(low, wo_ref[...]).astype(BF16)


def attention_kernel(
    q_ref, kw_ref, vw_ref, lse_ref, mg_ref, cos_ref, sin_ref, x_ref, side_ref, n_ref, sn_ref,
    gain_ref, wq_ref, wk_ref, wv_ref, hg_ref,
    ig_ref, sg_ref, qg_ref, kg_ref, vg_ref, gg_ref,
    dq_ref, dk_ref, dv_ref,
):
    block, width = x_ref.shape
    pairs = width // PAIR
    dk_ref[...] = jnp.zeros_like(dk_ref)
    dv_ref[...] = jnp.zeros_like(dv_ref)

    def attend(step, carry):
        pair, tile = step // (block // TILE), step % (block // TILE)
        rows = pl.ds(pl.multiple_of(tile * TILE, TILE), TILE)
        window = pl.ds(pl.multiple_of(tile * TILE, TILE), 3 * TILE)
        lanes = pl.ds(pl.multiple_of(pair * PAIR, PAIR), PAIR)
        query, keys, values = q_ref[rows, lanes], kw_ref[window, lanes], vw_ref[window, lanes]
        upstream = mg_ref[rows, lanes]
        totals = lse_ref[rows]
        lane = lax.broadcasted_iota(jnp.int32, (TILE, PAIR), 1)
        below = below_diagonal()
        dqs, dks, dvs = [], 0.0, 0.0
        for head in range(2):
            chosen = lane // HEAD == head
            one = jnp.where(chosen, query, jnp.zeros_like(query))
            above = jnp.where(chosen, upstream, jnp.zeros_like(upstream))
            total = jnp.sum(
                jnp.where(lane == 2 * pair + head, totals, 0.0), axis=-1, keepdims=True
            )
            edge, middle = merged(dot_t(one, keys), below)
            edge, middle = jnp.exp(edge - total), jnp.exp(middle - total)
            edge_grad, middle_grad = merged(dot_t(above, values), below)
            centred = jnp.sum(edge * edge_grad + middle * middle_grad, axis=-1, keepdims=True)
            weights = spread_out(edge, middle, below)
            grads = spread_out(edge * (edge_grad - centred), middle * (middle_grad - centred), below)
            dqs.append(dot(grads, keys))
            dks = dks + t_dot(grads, one)
            dvs = dvs + t_dot(weights, above)
        dq_ref[rows, lanes] = jnp.where(lane < HEAD, dqs[0], dqs[1])
        dk_ref[window, lanes] += dks
        dv_ref[window, lanes] += dvs
        return carry

    lax.fori_loop(0, pairs * (block // TILE), attend, 0)

    scale = 1.0 / math.sqrt(HEAD)
    own_cos, own_sin = cos_ref[block:], -sin_ref[block:]
    dq = turned(dq_ref[...] * scale, own_cos, own_sin).astype(BF16)
    dk = turned(dk_ref[block:], own_cos, own_sin).astype(BF16)
    dv = dv_ref[block:].astype(BF16)
    sdk = turned(dk_ref[:block], cos_ref[:block], -sin_ref[:block]).astype(BF16)
    sdv = dv_ref[:block].astype(BF16)
    turned_rows = jnp.transpose(n_ref[...])
    turned_side = jnp.transpose(sn_ref[...])
    qg_ref[...] = dot(turned_rows, dq).astype(BF16)
    kg_ref[...] = (dot(turned_rows, dk) + dot(turned_side, sdk)).astype(BF16)
    vg_ref[...] = (dot(turned_rows, dv) + dot(turned_side, sdv)).astype(BF16)
    wk, wv = wk_ref[...], wv_ref[...]
    upstream = dot_t(dq, wq_ref[...]) + dot_t(dk, wk) + dot_t(dv, wv)
    unit, spread = normalised(x_ref[...].astype(F32))
    part, gain_part = norm_back(unit, spread, gain_ref[...], upstream)
    ig_ref[...] = hg_ref[...] + part
    unit, spread = normalised(side_ref[...].astype(F32))
    part, side_gain = norm_back(unit, spread, gain_ref[...], dot_t(sdk, wk) + dot_t(sdv, wv))
    sg_ref[...] = part.astype(BF16)
    gg_ref[...] = gain_part + side_gain


def call(kernel, operands, results, scratch=(), flops=0):
    nbytes = sum(a.size * a.dtype.itemsize for a in operands) + sum(
        math.prod(s) * jnp.dtype(d).itemsize for s, d in results
    )
    return pl.pallas_call(
        kernel,
        out_shape=tuple(jax.ShapeDtypeStruct(s, d) for s, d in results),
        in_specs=[VMEM] * len(operands),
        out_specs=tuple(VMEM for _ in results),
        scratch_shapes=list(scratch),
        compiler_params=pltpu.CompilerParams(vmem_limit_bytes=LIMIT),
        cost_estimate=pl.CostEstimate(flops=flops, bytes_accessed=nbytes, transcendentals=0),
    )(*operands)


def exchange_steps(batches, blocks):
    number = batches * blocks

    def pairs(partner):
        return [
            (d, p[0] * blocks + p[1])
            for d in range(number)
            for p in [partner(d // blocks, d % blocks)]
        ]

    steps = [(pairs(lambda b, s: (b ^ 1, s)), lambda b, s: b % 2)]
    steps.append(
        (
            pairs(lambda b, s: (b, s ^ 1) if b % 2 == 0 else (b ^ 2, s)),
            lambda b, s: jnp.where(b % 2 == 0, s, (b // 2) % 2),
        )
    )
    steps.append(
        (
            pairs(lambda b, s: (b ^ 2, s) if b % 2 == 0 else (b, s ^ 1)),
            lambda b, s: jnp.where(b % 2 == 0, (b // 2) % 2, s),
        )
    )
    place = 4
    while place < batches:
        steps.append(
            (
                pairs(lambda b, s, place=place: (b ^ place, s)),
                lambda b, s, place=place: (b // place) % 2,
            )
        )
        place *= 2
    return steps


def total_of(sent, kept, steps, halved):
    row, column = (lax.axis_index("batch"), lax.axis_index("seq"))
    array = kept + lax.ppermute(sent, AXES, steps[0][0])
    for pairs, bit in steps[1:halved]:
        half = array.shape[0] // 2
        mine = bit(row, column)
        sent = lax.dynamic_slice_in_dim(array, (1 - mine) * half, half)
        kept = lax.dynamic_slice_in_dim(array, mine * half, half)
        array = kept + lax.ppermute(sent, AXES, pairs)
    for pairs, bit in steps[halved:]:
        array = array + lax.ppermute(array, AXES, pairs)
    for pairs, bit in reversed(steps[:halved]):
        mine = bit(row, column)
        other = lax.ppermute(array, AXES, pairs)
        array = jnp.concatenate(
            [jnp.where(mine == 0, array, other), jnp.where(mine == 0, other, array)], axis=0
        )
    return array


def body(
    inputs,
    memory,
    cotangent,
    labels,
    attention_gain,
    query_weight,
    key_weight,
    value_weight,
    out_weight,
    forward_gain,
    up_weight,
    down_weight,
    boundary_hidden,
    boundary_out,
):
    group, block, width = inputs.shape
    wide, hidden_wide = up_weight.shape[1], boundary_hidden.shape[1]
    batches, blocks = (lax.axis_size("batch"), lax.axis_size("seq"))
    steps = exchange_steps(batches, blocks)
    column = lax.axis_index("seq")
    rows = inputs.reshape(block, width)
    received = lax.ppermute(rows, "seq", [(i, i + 1) for i in range(blocks - 1)])
    tables = rotary_tables(-block, (blocks + 1) * block)
    cosine, sine = (
        lax.dynamic_slice_in_dim(jnp.asarray(t), column * block, 2 * block) for t in tables
    )
    gain = attention_gain.reshape(1, width)
    square = (block, width)
    normed, queries, keys, values = call(
        own_kernel,
        (rows, gain, query_weight, key_weight, value_weight, cosine, sine),
        [(square, BF16)] * 4,
        flops=6 * block * width * width,
    )
    side = jnp.where(column == 0, memory.reshape(block, width), received)
    window = (2 * block, width)
    (
        side_normed, key_window, value_window, mixed, totals, hidden, normed_hidden, gated, slope,
        outputs, probe_grad, hidden_sent, hidden_kept, boundary_out_grad,
    ) = call(
        forward_kernel,
        (
            rows, side, gain, key_weight, value_weight, cosine, sine, queries, keys, values,
            out_weight, forward_gain.reshape(1, width), up_weight, down_weight, boundary_hidden,
            boundary_out.reshape(1, hidden_wide), labels,
        ),
        [
            (square, BF16), (window, BF16), (window, BF16), (square, BF16), ((block, PAIR), F32),
            (square, F32), (square, BF16), ((block, wide), BF16), ((block, wide), BF16),
            (square, BF16), ((block, hidden_wide), BF16), ((width // 2, hidden_wide), BF16),
            ((width // 2, hidden_wide), BF16), ((1, hidden_wide), F32),
        ],
        [
            pltpu.VMEM((block, hidden_wide), BF16),
            pltpu.VMEM((block, hidden_wide), BF16),
            pltpu.VMEM((width, block), BF16),
        ],
        flops=2 * block * width * (3 * width + 2 * wide + 2 * hidden_wide + 4 * block),
    )
    final_grad, up_grad, down_sent, down_kept = call(
        down_kernel,
        (probe_grad, boundary_hidden, cotangent.reshape(square), gated, slope, down_weight),
        [(square, F32), ((block, wide), BF16), ((wide // 2, width), BF16), ((wide // 2, width), BF16)],
        flops=2 * block * width * (2 * wide + hidden_wide),
    )
    hidden_grad, mixed_grad, out_grad, forward_gain_grad, up_sent, up_kept = call(
        up_kernel,
        (
            normed_hidden, up_grad, up_weight, hidden, forward_gain.reshape(1, width), final_grad,
            mixed, out_weight,
        ),
        [
            (square, F32), (square, BF16), ((width, width), BF16), ((1, width), F32),
            ((width // 2, wide), BF16), ((width // 2, wide), BF16),
        ],
        [pltpu.VMEM((width, block), BF16)],
        flops=2 * block * width * (2 * wide + 2 * width),
    )
    input_part, side_grad, query_grad, key_grad, value_grad, gain_grad = call(
        attention_kernel,
        (
            queries, key_window, value_window, totals, mixed_grad, cosine, sine, rows, side, normed,
            side_normed, gain, query_weight, key_weight, value_weight, hidden_grad,
        ),
        [
            (square, F32), (square, BF16), ((width, width), BF16), ((width, width), BF16),
            ((width, width), BF16), ((1, width), F32),
        ],
        [pltpu.VMEM(square, F32), pltpu.VMEM(window, F32), pltpu.VMEM(window, F32)],
        flops=2 * block * width * (10 * width + 6 * block),
    )
    hidden_total = total_of(hidden_sent, hidden_kept, steps, 5)
    down_total = total_of(down_sent, down_kept, steps, 5)
    up_total = total_of(up_sent, up_kept, steps, 5)
    small = jnp.concatenate([gain_grad, forward_gain_grad, boundary_out_grad], axis=1)
    small = jnp.pad(small.reshape(-1).astype(BF16), (0, width * width - small.size))
    rest = jnp.concatenate(
        [query_grad, key_grad, value_grad, out_grad, small.reshape(width, width)], axis=0
    )
    half = rest.shape[0] // 2
    core = lax.axis_index("batch") % 2
    rest = total_of(
        lax.dynamic_slice_in_dim(rest, (1 - core) * half, half),
        lax.dynamic_slice_in_dim(rest, core * half, half),
        steps,
        5,
    ).astype(F32)
    returned = lax.ppermute(side_grad, "seq", [(i + 1, i) for i in range(blocks - 1)])
    input_grad = input_part + returned.astype(F32)
    small = rest[4 * width :].reshape(-1)
    return (
        outputs.reshape(inputs.shape),
        input_grad.reshape(inputs.shape),
        small[:width],
        rest[:width],
        rest[width : 2 * width],
        rest[2 * width : 3 * width],
        rest[3 * width : 4 * width],
        small[width : 2 * width],
        up_total.astype(F32),
        down_total.astype(F32),
        hidden_total.astype(F32),
        small[2 * width : 2 * width + hidden_wide],
    )


def solution(mesh):
    placed = (
        P("batch", "seq", None),
        P("batch", None, None),
        P("batch", "seq", None),
        P("batch", "seq"),
        P(),
        P(),
        P(),
        P(),
        P(),
        P(),
        P(),
        P(),
        P(),
        P(),
    )
    return jax.shard_map(
        body,
        mesh=mesh,
        in_specs=placed,
        out_specs=(
            P("batch", "seq", None),
            P("batch", "seq", None),
            P(),
            P(),
            P(),
            P(),
            P(),
            P(),
            P(),
            P(),
            P(),
            P(),
        ),
        check_vma=False,
    )
```

```python
import functools
import math

import jax
import jax.numpy as jnp
import numpy as np
from jax import lax
from jax.experimental import pallas as pl
from jax.experimental.pallas import tpu as pltpu
from jax.sharding import PartitionSpec as P

HEADS = 8
HEAD = 64
PAIR = 2 * HEAD
TILE = 256
EPS = 1e-05
BASE = 10000.0
AXES = ("batch", "seq")
F32, BF16 = jnp.float32, jnp.bfloat16
VMEM = pl.BlockSpec(memory_space=pltpu.VMEM)
MEGA = 1024 * 1024


def dot(left, right):
    return jnp.dot(left, right, preferred_element_type=F32)


def dot_t(left, right):
    return lax.dot_general(left, right, (((1,), (1,)), ((), ())), preferred_element_type=F32)


def t_dot(left, right):
    return lax.dot_general(left, right, (((0,), (0,)), ((), ())), preferred_element_type=F32)


def normalised(values):
    centre = values - jnp.mean(values, axis=-1, keepdims=True)
    spread = jnp.mean(centre * centre, axis=-1, keepdims=True)
    scale = lax.rsqrt(spread + EPS)
    return centre * scale, scale


def norm_back(unit, scale, gain, upstream):
    product = upstream * unit
    inner = upstream * gain
    mean = jnp.mean(inner, axis=-1, keepdims=True)
    along = jnp.mean(inner * unit, axis=-1, keepdims=True)
    return scale * (inner - mean - unit * along), jnp.sum(product, axis=0, keepdims=True)


def gelu_both(value):
    factor = math.sqrt(2.0 / math.pi)
    square = value * value
    half = 0.5 + 0.5 * jnp.tanh(value * (factor + (factor * 0.044715) * square))
    result = value * half
    bend = (result - result * half) * (2.0 * factor + (6.0 * factor * 0.044715) * square)
    return result, half + bend


def turned(values, cosine, sine):
    front = lax.broadcasted_iota(jnp.int32, (values.shape[0], PAIR), 1) % HEAD < HEAD // 2
    parts = []
    for at in range(0, values.shape[1], PAIR):
        part = values[:, at : at + PAIR]
        other = jnp.where(
            front, pltpu.roll(part, PAIR - HEAD // 2, 1), pltpu.roll(part, HEAD // 2, 1)
        )
        parts.append(part * cosine + other * sine)
    return jnp.concatenate(parts, axis=1)


def rotary_tables(first, count):
    positions = np.arange(first, first + count, dtype=np.float32)
    half = HEAD // 2
    freqs = np.float32(BASE) ** (-(np.arange(half, dtype=np.float32) * np.float32(2.0 / HEAD)))
    angles = (positions[:, None] * freqs[None, :].astype(np.float32)).astype(np.float64)
    cosine, sine = (np.cos(angles), np.sin(angles))
    return (
        np.concatenate([cosine] * 4, axis=1).astype(np.float32),
        np.concatenate([-sine, sine] * 2, axis=1).astype(np.float32),
    )


def own_kernel(
    x_ref, gain_ref, wq_ref, wk_ref, wv_ref, cos_ref, sin_ref,
    nt_ref, q_ref, qt_ref, k_ref, kt_ref, v_ref, vt_ref,
):
    unit, _ = normalised(x_ref[...].astype(F32))
    low = (unit * gain_ref[...]).astype(BF16)
    nt_ref[...] = jnp.transpose(low)
    block = low.shape[0]
    cosine, sine = cos_ref[block:], sin_ref[block:]
    scale = 1.0 / math.sqrt(HEAD)
    query = turned(dot(low, wq_ref[...]), cosine, sine).astype(BF16).astype(F32) * scale
    query = query.astype(BF16)
    q_ref[...] = query
    qt_ref[...] = jnp.transpose(query)
    key = turned(dot(low, wk_ref[...]), cosine, sine).astype(BF16)
    k_ref[...] = key
    kt_ref[...] = jnp.transpose(key)
    value = dot(low, wv_ref[...]).astype(BF16)
    v_ref[...] = value
    vt_ref[...] = jnp.transpose(value)


def before_diagonal():
    key = lax.broadcasted_iota(jnp.int32, (TILE, TILE), 0)
    return key <= lax.broadcasted_iota(jnp.int32, (TILE, TILE), 1)


def halves(array, seen):
    none = jnp.zeros_like(array)
    return jnp.where(seen, none, array), jnp.where(seen, array, none)


def attend(q_t, keys, values_t, w_ref, mix_ref):
    seen = before_diagonal()
    pairs = mix_ref.shape[0] // PAIR

    def one_pair(pair, carry):
        lanes = pl.ds(pl.multiple_of(pair * PAIR, PAIR), PAIR)
        both = q_t(lanes)
        row = lax.broadcasted_iota(jnp.int32, both.shape, 0)
        for head in range(2):
            query = jnp.where(row // HEAD == head, both, jnp.zeros_like(both))
            first, middle, last = [dot(block(lanes), query) for block in keys]
            edge = jnp.where(seen, last, first)
            peak = jnp.maximum(
                jnp.max(edge, axis=0, keepdims=True), jnp.max(middle, axis=0, keepdims=True)
            )
            edge, middle = jnp.exp(edge - peak), jnp.exp(middle - peak)
            total = jnp.sum(edge + middle, axis=0, keepdims=True)
            edge, middle = (edge / total).astype(BF16), (middle / total).astype(BF16)
            w_ref[2 * pair + head, :TILE] = edge
            w_ref[2 * pair + head, TILE:] = middle
            own = pl.ds(pl.multiple_of(pair * PAIR + head * HEAD, HEAD), HEAD)
            left, right = halves(edge, seen)
            mix = dot(values_t[0](own), left) + dot(values_t[1](own), middle)
            mix_ref[own] = (mix + dot(values_t[2](own), right)).astype(BF16)
        return carry

    lax.fori_loop(0, pairs, one_pair, 0)


def side_rows(memory_ref, received_ref):
    return jnp.where(lax.axis_index("seq") == 0, memory_ref[...], received_ref[...]).astype(F32)


def side_part(memory_ref, received_ref, gain_ref, wk_ref, wv_ref, cos_ref, sin_ref, snt_ref, k_ref, kt_ref, v_ref, vt_ref):
    unit, _ = normalised(side_rows(memory_ref, received_ref))
    low = (unit * gain_ref[...]).astype(BF16)
    snt_ref[...] = jnp.transpose(low)
    key = turned(dot(low, wk_ref[...]), cos_ref[...], sin_ref[...]).astype(BF16)
    k_ref[...] = key
    kt_ref[...] = jnp.transpose(key)
    value = dot(low, wv_ref[...]).astype(BF16)
    v_ref[...] = value
    vt_ref[...] = jnp.transpose(value)


def late_kernel(
    memory_ref, received_ref, gain_ref, wk_ref, wv_ref, cos_ref, sin_ref, qt_ref, ok_ref, ovt_ref,
    snt_ref, k_ref, kt_ref, v_ref, vt_ref, w_ref, mix_ref,
):
    side_part(
        memory_ref.at[TILE:], received_ref, gain_ref, wk_ref, wv_ref, cos_ref.at[TILE : 2 * TILE], sin_ref.at[TILE : 2 * TILE],
        snt_ref, k_ref, kt_ref, v_ref, vt_ref,
    )
    attend(
        lambda at: qt_ref[at, TILE:],
        (lambda at: k_ref[:, at], lambda at: ok_ref[:TILE, at], lambda at: ok_ref[TILE:, at]),
        (lambda at: vt_ref[at], lambda at: ovt_ref[at, :TILE], lambda at: ovt_ref[at, TILE:]),
        w_ref,
        mix_ref,
    )


def early_kernel(
    memory_ref, received_ref, gain_ref, wk_ref, wv_ref, cos_ref, sin_ref, qt_ref, ok_ref, ovt_ref, sk_ref, svt_ref,
    snt_ref, k_ref, kt_ref, v_ref, vt_ref, w_ref, mix_ref,
):
    side_part(
        memory_ref.at[:TILE], received_ref, gain_ref, wk_ref, wv_ref, cos_ref.at[:TILE], sin_ref.at[:TILE],
        snt_ref, k_ref, kt_ref, v_ref, vt_ref,
    )
    attend(
        lambda at: qt_ref[at, :TILE],
        (lambda at: k_ref[:, at], lambda at: sk_ref[:, at], lambda at: ok_ref[:TILE, at]),
        (lambda at: vt_ref[at], lambda at: svt_ref[at], lambda at: ovt_ref[at, :TILE]),
        w_ref,
        mix_ref,
    )


def forward_kernel(
    x_ref, mix0_ref, mix1_ref, wo_ref, fgain_ref, up_ref, down_ref, bh_ref, bo_ref, labels_ref,
    mixt_ref, hidden_ref, nht_ref, gated_ref, slope_ref, out_ref, pg_ref, sent_ref, kept_ref, bog_ref,
    probe_ref, pslope_ref, turn_ref,
):
    block, width = x_ref.shape
    mixt_ref[:, :TILE] = mix0_ref[...]
    mixt_ref[:, TILE:] = mix1_ref[...]
    mixed = jnp.transpose(mixt_ref[...])
    hidden = x_ref[...].astype(F32) + dot(mixed, wo_ref[...])
    hidden_ref[...] = hidden
    unit, _ = normalised(hidden)
    low = (unit * fgain_ref[...]).astype(BF16)
    nht_ref[...] = jnp.transpose(low)
    final = hidden
    step = 512
    for at in range(0, up_ref.shape[1], step):
        gated, slope = gelu_both(dot(low, up_ref[:, at : at + step]))
        gated = gated.astype(BF16)
        gated_ref[:, at : at + step] = gated
        slope_ref[:, at : at + step] = slope.astype(BF16)
        final = final + dot(gated, down_ref[at : at + step])
    out = final.astype(BF16)
    out_ref[...] = out
    turn_ref[...] = jnp.transpose(out)
    logits = jnp.zeros((block, 1), F32)
    for at in range(0, bh_ref.shape[1], step):
        probe, slope = gelu_both(dot(out, bh_ref[:, at : at + step]))
        probe = probe.astype(BF16)
        probe_ref[:, at : at + step] = probe
        pslope_ref[:, at : at + step] = slope.astype(BF16)
        logits = logits + jnp.sum(
            probe.astype(F32) * bo_ref[:, at : at + step].astype(F32), axis=-1, keepdims=True
        )
    targets = jnp.transpose(jnp.broadcast_to(labels_ref[...].astype(F32), (PAIR, block)))[:, :1]
    signal = (jax.nn.sigmoid(logits) - targets).astype(BF16).astype(F32)
    half = bh_ref.shape[1] // 2
    core = lax.axis_index("batch") & 1
    for at in range(0, bh_ref.shape[1], step):
        grad = pslope_ref[:, at : at + step].astype(F32) * (
            signal * bo_ref[:, at : at + step].astype(F32)
        )
        pg_ref[:, at : at + step] = grad.astype(BF16)
    for place, ref in ((1 - core, sent_ref), (core, kept_ref)):
        for at in range(0, half, step):
            grad = pg_ref[:, pl.ds(pl.multiple_of(place * half + at, step), step)]
            ref[at * width // step : (at + step) * width // step] = dot(turn_ref[...], grad).astype(BF16)
    for at in range(0, bh_ref.shape[1], step):
        bog_ref[:, at : at + step] = jnp.sum(
            signal * probe_ref[:, at : at + step].astype(F32), axis=0, keepdims=True
        )


def down_kernel(pg_ref, bh_ref, cot_ref, gated_ref, slope_ref, down_ref, grad_ref, upg_ref, sent_ref, kept_ref):
    final = cot_ref[...].astype(F32) + dot_t(pg_ref[...], bh_ref[...])
    grad_ref[...] = final
    low = final.astype(BF16)
    step = 512
    half = down_ref.shape[0] // 2
    core = lax.axis_index("batch") & 1
    for at in range(0, half, step):
        rows = pl.ds(pl.multiple_of((1 - core) * half + at, step), step)
        sent_ref[at : at + step] = t_dot(gated_ref[:, rows], low).astype(BF16)
    for at in range(0, half, step):
        rows = pl.ds(pl.multiple_of(core * half + at, step), step)
        kept_ref[at : at + step] = t_dot(gated_ref[:, rows], low).astype(BF16)
    for at in range(0, down_ref.shape[0], step):
        part = slope_ref[:, at : at + step].astype(F32) * dot_t(low, down_ref[at : at + step])
        upg_ref[:, at : at + step] = part.astype(BF16)


def up_kernel(
    nht_ref, upg_ref, up_ref, hidden_ref, fgain_ref, grad_ref, mixt_ref, wo_ref,
    hg_ref, mg_ref, mgt_ref, fgg_ref, sent_ref, kept_ref,
):
    width, wide = up_ref.shape
    upstream = dot_t(upg_ref[...], up_ref[...])
    unit, scale = normalised(hidden_ref[...])
    part, gain_part = norm_back(unit, scale, fgain_ref[...], upstream)
    fgg_ref[...] = gain_part
    total = grad_ref[...] + part
    hg_ref[...] = total
    low = total.astype(BF16)
    mixed_grad = dot_t(low, wo_ref[...]).astype(BF16)
    mg_ref[...] = mixed_grad
    mgt_ref[...] = jnp.transpose(mixed_grad)
    core = lax.axis_index("batch") & 1
    half, step = wide // 2, 512
    for place, ref in ((1 - core, sent_ref), (core, kept_ref)):
        for at in range(0, half, step):
            grad = upg_ref[:, pl.ds(pl.multiple_of(place * half + at, step), step)]
            ref[at * width // step : (at + step) * width // step] = dot(nht_ref[...], grad).astype(BF16)
        rows = pl.ds(pl.multiple_of(place * (width // 2), width // 2), width // 2)
        ref[half * width // step :] = dot(mixt_ref[rows], low).astype(BF16)


def attend_back(pair, tile, w_ref, mg_ref, mgt_ref, q_ref, values, keys_t, dq_ref, dks, dvs):
    seen = before_diagonal()
    lanes = slice(pair * PAIR, (pair + 1) * PAIR)
    rows = slice(tile * TILE, (tile + 1) * TILE)
    upstream_t, upstream, query = mgt_ref[lanes, rows], mg_ref[rows, lanes], q_ref[rows, lanes]
    row = lax.broadcasted_iota(jnp.int32, (PAIR, TILE), 0)
    lane = lax.broadcasted_iota(jnp.int32, (TILE, PAIR), 1)
    none, none_t = jnp.zeros_like(upstream), jnp.zeros_like(upstream_t)
    for head in range(2):
        above_t = jnp.where(row // HEAD == head, upstream_t, none_t)
        first, middle_grad, last = [dot(block[:, lanes], above_t) for block in values]
        edge_grad = jnp.where(seen, last, first)
        weights = w_ref[2 * pair + head]
        edge, middle = weights[:TILE].astype(F32), weights[TILE:].astype(F32)
        centred = jnp.sum(edge * edge_grad + middle * middle_grad, axis=0, keepdims=True)
        edge = (edge * (edge_grad - centred)).astype(BF16)
        middle = (middle * (middle_grad - centred)).astype(BF16)
        left, right = halves(edge, seen)
        above = jnp.where(lane // HEAD == head, upstream, none)
        one = jnp.where(lane // HEAD == head, query, none)
        own = slice(pair * PAIR + head * HEAD, pair * PAIR + (head + 1) * HEAD)
        grad = dot(keys_t[0][own], left) + dot(keys_t[1][own], middle) + dot(keys_t[2][own], right)
        inside = (pair * PAIR + head * HEAD) % dq_ref.shape[0]
        dq_ref[inside : inside + HEAD, rows] = grad
        w_left, w_right = halves(weights[:TILE], seen)
        for place, part in enumerate((left, middle, right)):
            dks[place] = dks[place] + dot(part, one)
        for place, part in enumerate((w_left, weights[TILE:], w_right)):
            dvs[place] = dvs[place] + dot(part, above)


def rows_of(*smalls):
    rows = [s[:, at : at + TILE] for s in smalls for at in range(0, s.shape[1], TILE)]
    rows.append(jnp.zeros((128 - len(rows), TILE), F32))
    return jnp.concatenate(rows, axis=0).astype(BF16)


def attention_kernel(
    part, final, w0_ref, w1_ref, mg_ref, mgt_ref, q_ref, sv0_ref, sv1_ref, v_ref, skt0_ref, skt1_ref, kt_ref,
    cos_ref, sin_ref, nt_ref, snt0_ref, snt1_ref, wq_ref, wk_ref, wv_ref, *rest,
):
    if final:
        x_ref, memory_ref, side0_ref, side1_ref, gain_ref, hg_ref, up_ref, sup_ref, ig_ref, sg_ref, grads_ref, dq_ref = rest
    else:
        bog_ref, fgg_ref, nup_ref, nsup_ref, grads_ref, dq_ref = rest
    block, width = q_ref.shape
    pairs = width // PAIR // 2
    values = (sv0_ref, sv1_ref, v_ref.at[:TILE], v_ref.at[TILE:])
    keys_t = (skt0_ref, skt1_ref, kt_ref.at[:, :TILE], kt_ref.at[:, TILE:])
    dk_parts, dv_parts = [[] for _ in range(4)], [[] for _ in range(4)]
    for pair in range(part * pairs, (part + 1) * pairs):
        dk, dv = [0.0] * 4, [0.0] * 4
        for tile, w_ref in ((1, w1_ref), (0, w0_ref)):
            dks, dvs = dk[tile : tile + 3], dv[tile : tile + 3]
            attend_back(
                pair, tile, w_ref, mg_ref, mgt_ref, q_ref, values[tile : tile + 3], keys_t[tile : tile + 3],
                dq_ref, dks, dvs,
            )
            dk[tile : tile + 3], dv[tile : tile + 3] = dks, dvs
        for place in range(4):
            dk_parts[place].append(dk[place])
            dv_parts[place].append(dv[place])
    dk = [jnp.concatenate(p, axis=1) for p in dk_parts]
    dv = [jnp.concatenate(p, axis=1).astype(BF16) for p in dv_parts]
    lanes = slice(part * (width // 2), (part + 1) * (width // 2))
    scale = 1.0 / math.sqrt(HEAD)
    cosine, sine = cos_ref[...], -sin_ref[...]
    dq = turned(jnp.transpose(dq_ref[...]) * scale, cosine[block:], sine[block:]).astype(BF16)
    dk = [
        turned(p, cosine[i * TILE : (i + 1) * TILE], sine[i * TILE : (i + 1) * TILE]).astype(BF16)
        for i, p in enumerate(dk)
    ]
    own_k, own_v = jnp.concatenate(dk[2:], axis=0), jnp.concatenate(dv[2:], axis=0)
    side_k, side_v = jnp.concatenate(dk[:2], axis=0), jnp.concatenate(dv[:2], axis=0)
    rows_t = nt_ref[...]
    side_t = jnp.concatenate([snt0_ref[...], snt1_ref[...]], axis=1)
    grads_ref[:width] = dot(rows_t, dq).astype(BF16)
    grads_ref[width : 2 * width] = (dot(rows_t, own_k) + dot(side_t, side_k)).astype(BF16)
    grads_ref[2 * width : 3 * width] = (dot(rows_t, own_v) + dot(side_t, side_v)).astype(BF16)
    wk, wv = wk_ref[:, lanes], wv_ref[:, lanes]
    upstream = dot_t(dq, wq_ref[:, lanes]) + dot_t(own_k, wk) + dot_t(own_v, wv)
    side_up = dot_t(side_k, wk) + dot_t(side_v, wv)
    if not final:
        grads_ref[3 * width :] = rows_of(bog_ref[...], fgg_ref[...])
        nup_ref[...] = upstream
        nsup_ref[...] = side_up
        return
    upstream = upstream + up_ref[...]
    side_up = side_up + sup_ref[...]
    unit, spread = normalised(x_ref[...].astype(F32))
    back, gain_part = norm_back(unit, spread, gain_ref[...], upstream)
    ig_ref[...] = hg_ref[...] + back
    for i, ref in enumerate((side0_ref, side1_ref)):
        at = slice(i * TILE, (i + 1) * TILE)
        unit, spread = normalised(side_rows(memory_ref.at[at], ref))
        back, side_gain = norm_back(unit, spread, gain_ref[...], side_up[at])
        sg_ref[at] = back.astype(BF16)
        gain_part = gain_part + side_gain
    grads_ref[3 * width :] = rows_of(gain_part)


def places(own_ref, other_ref):
    core = lax.axis_index("batch") & 1
    return ((core, own_ref), (1 - core, other_ref))


def tall_final(own_ref, other_ref, out_ref):
    half = own_ref.shape[0]
    for place, ref in places(own_ref, other_ref):
        out_ref[pl.ds(pl.multiple_of(place * half, half), half)] = ref[...].astype(F32)


def wide_final(own_ref, other_ref, out_ref, *more):
    width, wide = out_ref.shape
    step = own_ref.shape[1]
    for place, ref in places(own_ref, other_ref):
        for at in range(wide // 2 // step):
            lanes = pl.ds(pl.multiple_of(place * (wide // 2) + at * step, step), step)
            out_ref[:, lanes] = ref[at * width : (at + 1) * width].astype(F32)
        for extra in more:
            half = extra.shape[0] // 2
            extra[pl.ds(pl.multiple_of(place * half, half), half)] = ref[wide // 2 // step * width :].astype(F32)


def rest_final(own_ref, other_ref, q_ref, k_ref, v_ref, small_ref):
    width = q_ref.shape[0]
    half = width // 2
    for place, ref in places(own_ref, other_ref):
        lanes = pl.ds(pl.multiple_of(place * half, half), half)
        for at, out in enumerate((q_ref, k_ref, v_ref)):
            out[:, lanes] = ref[at * width : (at + 1) * width].astype(F32)
        small_ref[pl.ds(pl.multiple_of(place * 16, 16), 16)] = ref[3 * width : 3 * width + 16].astype(F32)


def call(kernel, operands, results, scratch=(), flops=0, limit=6):
    nbytes = sum(a.size * a.dtype.itemsize for a in operands) + sum(
        math.prod(s) * jnp.dtype(d).itemsize for s, d in results
    )
    return pl.pallas_call(
        kernel,
        out_shape=tuple(jax.ShapeDtypeStruct(s, d) for s, d in results),
        in_specs=[VMEM] * len(operands),
        out_specs=tuple(VMEM for _ in results),
        scratch_shapes=list(scratch),
        compiler_params=pltpu.CompilerParams(vmem_limit_bytes=limit * MEGA),
        cost_estimate=pl.CostEstimate(flops=flops, bytes_accessed=nbytes, transcendentals=0),
    )(*operands)


def exchange_steps(batches, blocks):
    number = batches * blocks

    def pairs(partner):
        return [
            (d, p[0] * blocks + p[1])
            for d in range(number)
            for p in [partner(d // blocks, d % blocks)]
        ]

    steps = [(pairs(lambda b, s: (b ^ 1, s)), lambda b, s: b & 1)]
    steps.append(
        (
            pairs(lambda b, s: (b, s ^ 1) if b % 2 == 0 else (b ^ 2, s)),
            lambda b, s: jnp.where(b & 1 == 0, s, (b >> 1) & 1),
        )
    )
    steps.append(
        (
            pairs(lambda b, s: (b ^ 2, s) if b % 2 == 0 else (b, s ^ 1)),
            lambda b, s: jnp.where(b & 1 == 0, (b >> 1) & 1, s),
        )
    )
    place = 4
    while place < batches:
        steps.append(
            (
                pairs(lambda b, s, place=place: (b ^ place, s)),
                lambda b, s, place=place: (b & place) // place,
            )
        )
        place *= 2
    return steps


def added(left, right, rows):
    return (left[rows].astype(F32) + right[rows].astype(F32)).astype(BF16)


def halve_kernel(bit, kept_ref, arrived_ref, sent_ref, left_ref):
    half, mine = sent_ref.shape[0], bit(lax.axis_index("batch"), lax.axis_index("seq"))
    step = 16 * math.gcd(half // 16, 8)
    for place, ref in ((1 - mine, sent_ref), (mine, left_ref)):
        for at in range(0, half, step):
            rows = pl.ds(pl.multiple_of(place * half + at, 16), step)
            ref[at : at + step] = added(kept_ref, arrived_ref, rows)


def add_kernel(kept_ref, arrived_ref, out_ref):
    half = out_ref.shape[0]
    step = 16 * math.gcd(half // 16, 8)
    for at in range(0, half, step):
        out_ref[at : at + step] = added(kept_ref, arrived_ref, slice(at, at + step))


def double_kernel(bit, kept_ref, arrived_ref, out_ref):
    half, mine = kept_ref.shape[0], bit(lax.axis_index("batch"), lax.axis_index("seq"))
    for place, ref in ((mine, kept_ref), (1 - mine, arrived_ref)):
        out_ref[pl.ds(pl.multiple_of(place * half, 16), half)] = ref[...]


def choose_kernel(bit, kept0_ref, arrived0_ref, kept1_ref, arrived1_ref, sent_ref, left_ref):
    mine = bit(lax.axis_index("batch"), lax.axis_index("seq"))
    step = 128
    for at in range(0, sent_ref.shape[0], step):
        rows = slice(at, at + step)
        zero, one = added(kept0_ref, arrived0_ref, rows), added(kept1_ref, arrived1_ref, rows)
        left_ref[rows] = jnp.where(mine == 0, zero, one)
        sent_ref[rows] = jnp.where(mine == 0, one, zero)


def pick_kernel(bit, zero_ref, one_ref, sent_ref, left_ref):
    mine = bit(lax.axis_index("batch"), lax.axis_index("seq"))

    @pl.when(mine == 0)
    def _():
        left_ref[...] = zero_ref[...]
        sent_ref[...] = one_ref[...]

    @pl.when(mine != 0)
    def _():
        left_ref[...] = one_ref[...]
        sent_ref[...] = zero_ref[...]


class Sum:
    def __init__(self, steps, sent, kept):
        self.steps, self.sent, self.kept, self.arrived = steps, sent, kept, None

    def start(self, number):
        self.arrived = lax.ppermute(self.sent, AXES, self.steps[number][0])

    def halve(self, number):
        shape = ((self.kept.shape[0] // 2, self.kept.shape[1]), BF16)
        self.sent, self.kept = call(
            functools.partial(halve_kernel, self.steps[number][1]), (self.kept, self.arrived), [shape] * 2
        )

    def add(self):
        (self.kept,) = call(add_kernel, (self.kept, self.arrived), [(self.kept.shape, BF16)])
        self.sent = self.kept

    def double(self, number):
        shape = ((self.kept.shape[0] * 2, self.kept.shape[1]), BF16)
        (self.kept,) = call(
            functools.partial(double_kernel, self.steps[number][1]), (self.kept, self.arrived), [shape]
        )
        self.sent = self.kept

    def pair(self, number):
        shape = (self.kept.shape, BF16)
        return call(
            functools.partial(pick_kernel, self.steps[number][1]), (self.kept, self.arrived), [shape] * 2
        )[::-1]


def fence(*arrays):
    return lax.optimization_barrier(arrays)


def body(
    inputs,
    memory,
    cotangent,
    labels,
    attention_gain,
    query_weight,
    key_weight,
    value_weight,
    out_weight,
    forward_gain,
    up_weight,
    down_weight,
    boundary_hidden,
    boundary_out,
):
    group, block, width = inputs.shape
    wide, hidden_wide = up_weight.shape[1], boundary_hidden.shape[1]
    batches, blocks = (lax.axis_size("batch"), lax.axis_size("seq"))
    steps = exchange_steps(batches, blocks)
    column = lax.axis_index("seq")
    core = lax.axis_index("batch") % 2
    rows = inputs.reshape(block, width)
    memory_rows = memory.reshape(block, width)
    onward = [(i, i + 1) for i in range(blocks - 1)]
    side1 = lax.ppermute(rows[TILE:], "seq", onward)
    side0 = lax.ppermute(rows[:TILE], "seq", onward)
    tables = rotary_tables(-block, (blocks + 1) * block)
    cosine, sine = (
        lax.dynamic_slice_in_dim(jnp.asarray(t), column * block, 2 * block) for t in tables
    )
    gain = attention_gain.reshape(1, width)
    square, side_shape = (block, width), (TILE, width)
    turned_square, turned_side = (width, block), (width, TILE)
    normed_t, queries, queries_t, keys, keys_t, values, values_t = call(
        own_kernel,
        (rows, gain, query_weight, key_weight, value_weight, cosine, sine),
        [(turned_square, BF16), (square, BF16), (turned_square, BF16)]
        + [(square, BF16), (turned_square, BF16)] * 2,
        flops=6 * block * width * width,
    )
    side_results = [
        (turned_side, BF16), (side_shape, BF16), (turned_side, BF16), (side_shape, BF16), (turned_side, BF16),
        ((HEADS, 2 * TILE, TILE), BF16), (turned_side, BF16),
    ]
    sn_t1, sk1, sk_t1, sv1, sv_t1, weights1, mix1 = call(
        late_kernel,
        (memory_rows, side1, gain, key_weight, value_weight, cosine, sine, queries_t, keys, values_t),
        side_results,
        flops=4 * TILE * width * (width + 3 * TILE),
    )
    sn_t0, sk0, sk_t0, sv0, sv_t0, weights0, mix0 = call(
        early_kernel,
        (memory_rows, side0, gain, key_weight, value_weight, cosine, sine, queries_t, keys, values_t, sk1, sv_t1),
        side_results,
        flops=4 * TILE * width * (width + 3 * TILE),
    )
    bh_half = (hidden_wide // 2 * width // 512, 512)
    (
        mixed_t, hidden, normed_hidden_t, gated, slope, outputs, probe_grad, hidden_sent, hidden_kept,
        boundary_out_grad,
    ) = call(
        forward_kernel,
        (
            rows, mix0, mix1, out_weight, forward_gain.reshape(1, width), up_weight, down_weight,
            boundary_hidden, boundary_out.reshape(1, hidden_wide), labels,
        ),
        [
            (turned_square, BF16), (square, F32), (turned_square, BF16), ((block, wide), BF16),
            ((block, wide), BF16), (square, BF16), ((block, hidden_wide), BF16),
            (bh_half, BF16), (bh_half, BF16), ((1, hidden_wide), F32),
        ],
        [
            pltpu.VMEM((block, hidden_wide), BF16),
            pltpu.VMEM((block, hidden_wide), BF16),
            pltpu.VMEM((width, block), BF16),
        ],
        flops=2 * block * width * (width + 2 * wide + 2 * hidden_wide),
        limit=18,
    )
    bh = Sum(steps, hidden_sent, hidden_kept)
    bh.start(0)
    final_grad, up_grad, down_sent, down_kept = call(
        down_kernel,
        (probe_grad, boundary_hidden, cotangent.reshape(square), gated, slope, down_weight),
        [(square, F32), ((block, wide), BF16), ((wide // 2, width), BF16), ((wide // 2, width), BF16)],
        flops=2 * block * width * (2 * wide + hidden_wide),
    )
    bh.arrived, up_grad, down_sent = fence(bh.arrived, up_grad, down_sent)
    bh.halve(1)
    bh.start(1)
    dn = Sum(steps, down_sent, down_kept)
    dn.start(0)
    up_half = (wide // 2 * width // 512 + width // 2, 512)
    hidden_grad, mixed_grad, mixed_grad_t, forward_gain_grad, up_sent, up_kept = call(
        up_kernel,
        (
            normed_hidden_t, up_grad, up_weight, hidden, forward_gain.reshape(1, width), final_grad,
            mixed_t, out_weight,
        ),
        [
            (square, F32), (square, BF16), (turned_square, BF16), ((1, width), F32),
            (up_half, BF16), (up_half, BF16),
        ],
        flops=2 * block * width * (2 * wide + 2 * width),
    )
    dn.arrived, mixed_grad, up_sent = fence(dn.arrived, mixed_grad, up_sent)
    dn.halve(1)
    dn.start(1)
    up = Sum(steps, up_sent, up_kept)
    up.start(0)
    shared = (
        weights0, weights1, mixed_grad, mixed_grad_t, queries, sv0, sv1, values, sk_t0, sk_t1, keys_t,
        cosine, sine, normed_t, sn_t0, sn_t1, query_weight, key_weight, value_weight,
    )
    grads_shape = ((3 * width + 128, width // 2), BF16)
    work = [pltpu.VMEM((width // 2, block), F32)]
    flops = 2 * block * width * (5 * width + 4 * block)
    upstream, side_upstream, grads0 = call(
        functools.partial(attention_kernel, 0, False),
        shared + (boundary_out_grad, forward_gain_grad),
        [(square, F32), (square, F32), grads_shape],
        work,
        flops=flops,
        limit=10,
    )
    bh.arrived, up.arrived, upstream = fence(bh.arrived, up.arrived, upstream)
    up.halve(1)
    up.start(1)
    input_part, side_grad, grads1 = call(
        functools.partial(attention_kernel, 1, True),
        shared + (rows, memory_rows, side0, side1, gain, hidden_grad, upstream, side_upstream),
        [(square, F32), (square, BF16), grads_shape],
        work,
        flops=flops,
        limit=10,
    )
    bh.arrived, dn.arrived, grads0, grads1, side_grad = fence(bh.arrived, dn.arrived, grads0, grads1, side_grad)
    rest = Sum(
        steps, *call(functools.partial(pick_kernel, steps[0][1]), (grads0, grads1), [grads_shape] * 2)
    )
    rest.start(0)
    both_shape = (bh.kept.shape, BF16)
    both = Sum(
        steps,
        *call(
            functools.partial(choose_kernel, steps[2][1]),
            (bh.kept, bh.arrived, dn.kept, dn.arrived),
            [both_shape] * 2,
        ),
    )
    both.start(2)
    up.halve(2)
    up.start(2)
    rest.halve(1)
    rest.start(1)
    both.halve(3)
    both.start(3)
    up.halve(3)
    up.start(3)
    rest.halve(2)
    rest.start(2)

    def across(total):
        for number in range(4, len(steps)):
            total.add()
            total.start(number)
        total.add()

    across(both)
    both.start(3)
    across(up)
    up.start(3)
    rest.halve(3)
    rest.start(3)
    across(rest)
    rest.start(3)
    for total in (both, up, rest):
        total.double(3)
        total.start(2)
    bh.sent, dn.sent = both.pair(2)
    bh.kept, dn.kept = bh.sent, dn.sent
    for total in (up, rest):
        total.double(2)
        total.start(1)
    for total in (bh, dn):
        total.start(1)
    for total in (up, rest, bh, dn):
        total.double(1)
        total.start(0)
    returned = lax.ppermute(side_grad, "seq", [(i + 1, i) for i in range(blocks - 1)])
    input_grad = input_part + returned.astype(F32)
    (hidden_total,) = call(wide_final, (bh.kept, bh.arrived), [((width, hidden_wide), F32)])
    (down_total,) = call(tall_final, (dn.kept, dn.arrived), [((wide, width), F32)])
    up_total, out_total = call(wide_final, (up.kept, up.arrived), [((width, wide), F32), ((width, width), F32)])
    query_total, key_total, value_total, small = call(
        rest_final, (rest.kept, rest.arrived), [((width, width), F32)] * 3 + [((32, width // 2), F32)]
    )
    small0, small1 = (small[:16].reshape(-1), small[16:].reshape(-1))
    return (
        outputs.reshape(inputs.shape),
        input_grad.reshape(inputs.shape),
        small1[:width],
        query_total,
        key_total,
        value_total,
        out_total,
        small0[hidden_wide : hidden_wide + width],
        up_total,
        down_total,
        hidden_total,
        small0[:hidden_wide],
    )


def solution(mesh):
    placed = (
        P("batch", "seq", None),
        P("batch", None, None),
        P("batch", "seq", None),
        P("batch", "seq"),
        P(),
        P(),
        P(),
        P(),
        P(),
        P(),
        P(),
        P(),
        P(),
        P(),
    )
    return jax.shard_map(
        body,
        mesh=mesh,
        in_specs=placed,
        out_specs=(
            P("batch", "seq", None),
            P("batch", "seq", None),
            P(),
            P(),
            P(),
            P(),
            P(),
            P(),
            P(),
            P(),
            P(),
            P(),
        ),
        check_vma=False,
    )
```

```python
import functools
import math

import jax
import jax.numpy as jnp
import numpy as np
from jax import lax
from jax.experimental import pallas as pl
from jax.experimental.pallas import tpu as pltpu
from jax.sharding import PartitionSpec as P

HEADS = 8
HEAD = 64
PAIR = 2 * HEAD
TILE = 256
EPS = 1e-05
BASE = 10000.0
AXES = ("batch", "seq")
F32, BF16 = jnp.float32, jnp.bfloat16
VMEM = pl.BlockSpec(memory_space=pltpu.VMEM)
STEP_FLOPS = int(4e9)
MEGA = 1024 * 1024
ORDER = "HaDHbDUcHUdDHTUDTHUDrTHUsHTDHTUDHTUDTHUTDUDTUT"


def dot(left, right):
    return jnp.dot(left, right, preferred_element_type=F32)


def dot_t(left, right):
    return lax.dot_general(left, right, (((1,), (1,)), ((), ())), preferred_element_type=F32)


def t_dot(left, right):
    return lax.dot_general(left, right, (((0,), (0,)), ((), ())), preferred_element_type=F32)


def normalised(values):
    centre = values - jnp.mean(values, axis=-1, keepdims=True)
    spread = jnp.mean(centre * centre, axis=-1, keepdims=True)
    scale = lax.rsqrt(spread + EPS)
    return centre * scale, scale


def norm_back(unit, scale, gain, upstream):
    product = upstream * unit
    inner = upstream * gain
    mean = jnp.mean(inner, axis=-1, keepdims=True)
    along = jnp.mean(inner * unit, axis=-1, keepdims=True)
    return scale * (inner - mean - unit * along), jnp.sum(product, axis=0, keepdims=True)


def gelu_both(value):
    factor = math.sqrt(2.0 / math.pi)
    square = value * value
    half = 0.5 + 0.5 * jnp.tanh(value * (factor + (factor * 0.044715) * square))
    result = value * half
    bend = (result - result * half) * (2.0 * factor + (6.0 * factor * 0.044715) * square)
    return result, half + bend


def turned(values, cosine, sine):
    front = lax.broadcasted_iota(jnp.int32, (values.shape[0], PAIR), 1) % HEAD < HEAD // 2
    parts = []
    for at in range(0, values.shape[1], PAIR):
        part = values[:, at : at + PAIR]
        other = jnp.where(
            front, pltpu.roll(part, PAIR - HEAD // 2, 1), pltpu.roll(part, HEAD // 2, 1)
        )
        parts.append(part * cosine + other * sine)
    return jnp.concatenate(parts, axis=1)


def rotary_tables(first, count):
    positions = np.arange(first, first + count, dtype=np.float32)
    half = HEAD // 2
    freqs = np.float32(BASE) ** (-(np.arange(half, dtype=np.float32) * np.float32(2.0 / HEAD)))
    angles = (positions[:, None] * freqs[None, :].astype(np.float32)).astype(np.float64)
    cosine, sine = (np.cos(angles), np.sin(angles))
    return (
        np.concatenate([cosine] * 4, axis=1).astype(np.float32),
        np.concatenate([-sine, sine] * 2, axis=1).astype(np.float32),
    )


def own_kernel(
    x_ref, gain_ref, wq_ref, wk_ref, wv_ref, cos_ref, sin_ref,
    nt_ref, q_ref, qt_ref, k_ref, kt_ref, v_ref, vt_ref,
):
    unit, _ = normalised(x_ref[...].astype(F32))
    low = (unit * gain_ref[...]).astype(BF16)
    nt_ref[...] = jnp.transpose(low)
    block = low.shape[0]
    cosine, sine = cos_ref[block:], sin_ref[block:]
    scale = 1.0 / math.sqrt(HEAD)
    query = turned(dot(low, wq_ref[...]), cosine, sine).astype(BF16).astype(F32) * scale
    query = query.astype(BF16)
    q_ref[...] = query
    qt_ref[...] = jnp.transpose(query)
    key = turned(dot(low, wk_ref[...]), cosine, sine).astype(BF16)
    k_ref[...] = key
    kt_ref[...] = jnp.transpose(key)
    value = dot(low, wv_ref[...]).astype(BF16)
    v_ref[...] = value
    vt_ref[...] = jnp.transpose(value)


def before_diagonal():
    key = lax.broadcasted_iota(jnp.int32, (TILE, TILE), 0)
    return key <= lax.broadcasted_iota(jnp.int32, (TILE, TILE), 1)


def halves(array, seen):
    none = jnp.zeros_like(array)
    return jnp.where(seen, none, array), jnp.where(seen, array, none)


def attend(q_t, keys, values_t, w_ref, mix_ref):
    seen = before_diagonal()
    pairs = mix_ref.shape[0] // PAIR

    def one_pair(pair, carry):
        lanes = pl.ds(pl.multiple_of(pair * PAIR, PAIR), PAIR)
        both = q_t(lanes)
        row = lax.broadcasted_iota(jnp.int32, both.shape, 0)
        for head in range(2):
            query = jnp.where(row // HEAD == head, both, jnp.zeros_like(both))
            first, middle, last = [dot(block(lanes), query) for block in keys]
            edge = jnp.where(seen, last, first)
            peak = jnp.maximum(
                jnp.max(edge, axis=0, keepdims=True), jnp.max(middle, axis=0, keepdims=True)
            )
            edge, middle = jnp.exp(edge - peak), jnp.exp(middle - peak)
            total = jnp.sum(edge + middle, axis=0, keepdims=True)
            edge, middle = (edge / total).astype(BF16), (middle / total).astype(BF16)
            w_ref[2 * pair + head, :TILE] = edge
            w_ref[2 * pair + head, TILE:] = middle
            own = pl.ds(pl.multiple_of(pair * PAIR + head * HEAD, HEAD), HEAD)
            left, right = halves(edge, seen)
            mix = dot(values_t[0](own), left) + dot(values_t[1](own), middle)
            mix_ref[own] = (mix + dot(values_t[2](own), right)).astype(BF16)
        return carry

    lax.fori_loop(0, pairs, one_pair, 0)


def side_rows(memory_ref, received_ref):
    return jnp.where(lax.axis_index("seq") == 0, memory_ref[...], received_ref[...]).astype(F32)


def side_part(memory_ref, received_ref, gain_ref, wk_ref, wv_ref, cos_ref, sin_ref, snt_ref, k_ref, kt_ref, v_ref, vt_ref):
    unit, _ = normalised(side_rows(memory_ref, received_ref))
    low = (unit * gain_ref[...]).astype(BF16)
    snt_ref[...] = jnp.transpose(low)
    key = turned(dot(low, wk_ref[...]), cos_ref[...], sin_ref[...]).astype(BF16)
    k_ref[...] = key
    kt_ref[...] = jnp.transpose(key)
    value = dot(low, wv_ref[...]).astype(BF16)
    v_ref[...] = value
    vt_ref[...] = jnp.transpose(value)


def late_kernel(
    memory_ref, received_ref, gain_ref, wk_ref, wv_ref, cos_ref, sin_ref, qt_ref, ok_ref, ovt_ref,
    snt_ref, k_ref, kt_ref, v_ref, vt_ref, w_ref, mix_ref,
):
    side_part(
        memory_ref.at[TILE:], received_ref, gain_ref, wk_ref, wv_ref, cos_ref.at[TILE : 2 * TILE], sin_ref.at[TILE : 2 * TILE],
        snt_ref, k_ref, kt_ref, v_ref, vt_ref,
    )
    attend(
        lambda at: qt_ref[at, TILE:],
        (lambda at: k_ref[:, at], lambda at: ok_ref[:TILE, at], lambda at: ok_ref[TILE:, at]),
        (lambda at: vt_ref[at], lambda at: ovt_ref[at, :TILE], lambda at: ovt_ref[at, TILE:]),
        w_ref,
        mix_ref,
    )


def early_kernel(
    memory_ref, received_ref, gain_ref, wk_ref, wv_ref, cos_ref, sin_ref, qt_ref, ok_ref, ovt_ref, sk_ref, svt_ref,
    snt_ref, k_ref, kt_ref, v_ref, vt_ref, w_ref, mix_ref,
):
    side_part(
        memory_ref.at[:TILE], received_ref, gain_ref, wk_ref, wv_ref, cos_ref.at[:TILE], sin_ref.at[:TILE],
        snt_ref, k_ref, kt_ref, v_ref, vt_ref,
    )
    attend(
        lambda at: qt_ref[at, :TILE],
        (lambda at: k_ref[:, at], lambda at: sk_ref[:, at], lambda at: ok_ref[:TILE, at]),
        (lambda at: vt_ref[at], lambda at: svt_ref[at], lambda at: ovt_ref[at, :TILE]),
        w_ref,
        mix_ref,
    )


def forward_kernel(
    x_ref, mix0_ref, mix1_ref, wo_ref, fgain_ref, up_ref, down_ref, bh_ref, bo_ref, labels_ref,
    mixt_ref, hidden_ref, nht_ref, gated_ref, slope_ref, out_ref, pg_ref, sent_ref, kept_ref, bog_ref,
    probe_ref, pslope_ref, turn_ref,
):
    block, width = x_ref.shape
    mixt_ref[:, :TILE] = mix0_ref[...]
    mixt_ref[:, TILE:] = mix1_ref[...]
    mixed = jnp.transpose(mixt_ref[...])
    hidden = x_ref[...].astype(F32) + dot(mixed, wo_ref[...])
    hidden_ref[...] = hidden
    unit, _ = normalised(hidden)
    low = (unit * fgain_ref[...]).astype(BF16)
    nht_ref[...] = jnp.transpose(low)
    final = hidden
    step = 512
    for at in range(0, up_ref.shape[1], step):
        gated, slope = gelu_both(dot(low, up_ref[:, at : at + step]))
        gated = gated.astype(BF16)
        gated_ref[:, at : at + step] = gated
        slope_ref[:, at : at + step] = slope.astype(BF16)
        final = final + dot(gated, down_ref[at : at + step])
    out = final.astype(BF16)
    out_ref[...] = out
    turn_ref[...] = jnp.transpose(out)
    logits = jnp.zeros((block, 1), F32)
    for at in range(0, bh_ref.shape[1], step):
        probe, slope = gelu_both(dot(out, bh_ref[:, at : at + step]))
        probe = probe.astype(BF16)
        probe_ref[:, at : at + step] = probe
        pslope_ref[:, at : at + step] = slope.astype(BF16)
        logits = logits + jnp.sum(
            probe.astype(F32) * bo_ref[:, at : at + step].astype(F32), axis=-1, keepdims=True
        )
    targets = jnp.transpose(jnp.broadcast_to(labels_ref[...].astype(F32), (PAIR, block)))[:, :1]
    signal = (jax.nn.sigmoid(logits) - targets).astype(BF16).astype(F32)
    half = bh_ref.shape[1] // 2
    core = lax.axis_index("batch") & 1
    for at in range(0, bh_ref.shape[1], step):
        grad = pslope_ref[:, at : at + step].astype(F32) * (
            signal * bo_ref[:, at : at + step].astype(F32)
        )
        pg_ref[:, at : at + step] = grad.astype(BF16)
    for place, ref in ((1 - core, sent_ref), (core, kept_ref)):
        for at in range(0, half, step):
            grad = pg_ref[:, pl.ds(pl.multiple_of(place * half + at, step), step)]
            ref[at * width // step : (at + step) * width // step] = dot(turn_ref[...], grad).astype(BF16)
    for at in range(0, bh_ref.shape[1], step):
        bog_ref[:, at : at + step] = jnp.sum(
            signal * probe_ref[:, at : at + step].astype(F32), axis=0, keepdims=True
        )


def down_kernel(pg_ref, bh_ref, cot_ref, gated_ref, slope_ref, down_ref, grad_ref, upg_ref, sent_ref, kept_ref):
    final = cot_ref[...].astype(F32) + dot_t(pg_ref[...], bh_ref[...])
    grad_ref[...] = final
    low = final.astype(BF16)
    step = 512
    half = down_ref.shape[0] // 2
    core = lax.axis_index("batch") & 1
    for at in range(0, half, step):
        rows = pl.ds(pl.multiple_of((1 - core) * half + at, step), step)
        sent_ref[at : at + step] = t_dot(gated_ref[:, rows], low).astype(BF16)
    for at in range(0, half, step):
        rows = pl.ds(pl.multiple_of(core * half + at, step), step)
        kept_ref[at : at + step] = t_dot(gated_ref[:, rows], low).astype(BF16)
    for at in range(0, down_ref.shape[0], step):
        part = slope_ref[:, at : at + step].astype(F32) * dot_t(low, down_ref[at : at + step])
        upg_ref[:, at : at + step] = part.astype(BF16)


def up_kernel(
    nht_ref, upg_ref, up_ref, hidden_ref, fgain_ref, grad_ref, mixt_ref, wo_ref,
    hg_ref, mg_ref, mgt_ref, fgg_ref, sent_ref, kept_ref,
):
    width, wide = up_ref.shape
    upstream = dot_t(upg_ref[...], up_ref[...])
    unit, scale = normalised(hidden_ref[...])
    part, gain_part = norm_back(unit, scale, fgain_ref[...], upstream)
    fgg_ref[...] = gain_part
    total = grad_ref[...] + part
    hg_ref[...] = total
    low = total.astype(BF16)
    mixed_grad = dot_t(low, wo_ref[...]).astype(BF16)
    mg_ref[...] = mixed_grad
    mgt_ref[...] = jnp.transpose(mixed_grad)
    core = lax.axis_index("batch") & 1
    half, step = wide // 2, 512
    for place, ref in ((1 - core, sent_ref), (core, kept_ref)):
        for at in range(0, half, step):
            grad = upg_ref[:, pl.ds(pl.multiple_of(place * half + at, step), step)]
            ref[at * width // step : (at + step) * width // step] = dot(nht_ref[...], grad).astype(BF16)
        rows = pl.ds(pl.multiple_of(place * (width // 2), width // 2), width // 2)
        ref[half * width // step :] = dot(mixt_ref[rows], low).astype(BF16)


def attend_back(pair, tile, w_ref, mg_ref, mgt_ref, q_ref, values, keys_t, dq_ref, dks, dvs):
    seen = before_diagonal()
    lanes = slice(pair * PAIR, (pair + 1) * PAIR)
    rows = slice(tile * TILE, (tile + 1) * TILE)
    upstream_t, upstream, query = mgt_ref[lanes, rows], mg_ref[rows, lanes], q_ref[rows, lanes]
    row = lax.broadcasted_iota(jnp.int32, (PAIR, TILE), 0)
    lane = lax.broadcasted_iota(jnp.int32, (TILE, PAIR), 1)
    none, none_t = jnp.zeros_like(upstream), jnp.zeros_like(upstream_t)
    for head in range(2):
        above_t = jnp.where(row // HEAD == head, upstream_t, none_t)
        first, middle_grad, last = [dot(block[:, lanes], above_t) for block in values]
        edge_grad = jnp.where(seen, last, first)
        weights = w_ref[2 * pair + head]
        edge, middle = weights[:TILE].astype(F32), weights[TILE:].astype(F32)
        centred = jnp.sum(edge * edge_grad + middle * middle_grad, axis=0, keepdims=True)
        edge = (edge * (edge_grad - centred)).astype(BF16)
        middle = (middle * (middle_grad - centred)).astype(BF16)
        left, right = halves(edge, seen)
        above = jnp.where(lane // HEAD == head, upstream, none)
        one = jnp.where(lane // HEAD == head, query, none)
        own = slice(pair * PAIR + head * HEAD, pair * PAIR + (head + 1) * HEAD)
        grad = dot(keys_t[0][own], left) + dot(keys_t[1][own], middle) + dot(keys_t[2][own], right)
        inside = (pair * PAIR + head * HEAD) % dq_ref.shape[0]
        dq_ref[inside : inside + HEAD, rows] = grad
        w_left, w_right = halves(weights[:TILE], seen)
        for place, part in enumerate((left, middle, right)):
            dks[place] = dks[place] + dot(part, one)
        for place, part in enumerate((w_left, weights[TILE:], w_right)):
            dvs[place] = dvs[place] + dot(part, above)


def rows_of(*smalls):
    rows = [s[:, at : at + TILE] for s in smalls for at in range(0, s.shape[1], TILE)]
    rows.append(jnp.zeros((128 - len(rows), TILE), F32))
    return jnp.concatenate(rows, axis=0).astype(BF16)


def attention_kernel(
    part, final, w0_ref, w1_ref, mg_ref, mgt_ref, q_ref, sv0_ref, sv1_ref, v_ref, skt0_ref, skt1_ref, kt_ref,
    cos_ref, sin_ref, nt_ref, snt0_ref, snt1_ref, wq_ref, wk_ref, wv_ref, *rest,
):
    if final:
        x_ref, memory_ref, side0_ref, side1_ref, gain_ref, hg_ref, up_ref, sup_ref, ig_ref, sg_ref, grads_ref, dq_ref = rest
    else:
        bog_ref, fgg_ref, nup_ref, nsup_ref, grads_ref, dq_ref = rest
    block, width = q_ref.shape
    pairs = width // PAIR // 2
    values = (sv0_ref, sv1_ref, v_ref.at[:TILE], v_ref.at[TILE:])
    keys_t = (skt0_ref, skt1_ref, kt_ref.at[:, :TILE], kt_ref.at[:, TILE:])
    dk_parts, dv_parts = [[] for _ in range(4)], [[] for _ in range(4)]
    for pair in range(part * pairs, (part + 1) * pairs):
        dk, dv = [0.0] * 4, [0.0] * 4
        for tile, w_ref in ((1, w1_ref), (0, w0_ref)):
            dks, dvs = dk[tile : tile + 3], dv[tile : tile + 3]
            attend_back(
                pair, tile, w_ref, mg_ref, mgt_ref, q_ref, values[tile : tile + 3], keys_t[tile : tile + 3],
                dq_ref, dks, dvs,
            )
            dk[tile : tile + 3], dv[tile : tile + 3] = dks, dvs
        for place in range(4):
            dk_parts[place].append(dk[place])
            dv_parts[place].append(dv[place])
    dk = [jnp.concatenate(p, axis=1) for p in dk_parts]
    dv = [jnp.concatenate(p, axis=1).astype(BF16) for p in dv_parts]
    lanes = slice(part * (width // 2), (part + 1) * (width // 2))
    scale = 1.0 / math.sqrt(HEAD)
    cosine, sine = cos_ref[...], -sin_ref[...]
    dq = turned(jnp.transpose(dq_ref[...]) * scale, cosine[block:], sine[block:]).astype(BF16)
    dk = [
        turned(p, cosine[i * TILE : (i + 1) * TILE], sine[i * TILE : (i + 1) * TILE]).astype(BF16)
        for i, p in enumerate(dk)
    ]
    own_k, own_v = jnp.concatenate(dk[2:], axis=0), jnp.concatenate(dv[2:], axis=0)
    side_k, side_v = jnp.concatenate(dk[:2], axis=0), jnp.concatenate(dv[:2], axis=0)
    rows_t = nt_ref[...]
    side_t = jnp.concatenate([snt0_ref[...], snt1_ref[...]], axis=1)
    grads_ref[:width] = dot(rows_t, dq).astype(BF16)
    grads_ref[width : 2 * width] = (dot(rows_t, own_k) + dot(side_t, side_k)).astype(BF16)
    grads_ref[2 * width : 3 * width] = (dot(rows_t, own_v) + dot(side_t, side_v)).astype(BF16)
    wk, wv = wk_ref[:, lanes], wv_ref[:, lanes]
    upstream = dot_t(dq, wq_ref[:, lanes]) + dot_t(own_k, wk) + dot_t(own_v, wv)
    side_up = dot_t(side_k, wk) + dot_t(side_v, wv)
    if not final:
        grads_ref[3 * width :] = rows_of(bog_ref[...], fgg_ref[...])
        nup_ref[...] = upstream
        nsup_ref[...] = side_up
        return
    upstream = upstream + up_ref[...]
    side_up = side_up + sup_ref[...]
    unit, spread = normalised(x_ref[...].astype(F32))
    back, gain_part = norm_back(unit, spread, gain_ref[...], upstream)
    ig_ref[...] = hg_ref[...] + back
    for i, ref in enumerate((side0_ref, side1_ref)):
        at = slice(i * TILE, (i + 1) * TILE)
        unit, spread = normalised(side_rows(memory_ref.at[at], ref))
        back, side_gain = norm_back(unit, spread, gain_ref[...], side_up[at])
        sg_ref[at] = back.astype(BF16)
        gain_part = gain_part + side_gain
    grads_ref[3 * width :] = rows_of(gain_part)


def places(own_ref, other_ref):
    core = lax.axis_index("batch") & 1
    return ((core, own_ref), (1 - core, other_ref))


def tall_final(own_ref, other_ref, out_ref):
    half = own_ref.shape[0]
    for place, ref in places(own_ref, other_ref):
        out_ref[pl.ds(pl.multiple_of(place * half, half), half)] = ref[...].astype(F32)


def wide_final(own_ref, other_ref, out_ref, *more):
    width, wide = out_ref.shape
    step = own_ref.shape[1]
    for place, ref in places(own_ref, other_ref):
        for at in range(wide // 2 // step):
            lanes = pl.ds(pl.multiple_of(place * (wide // 2) + at * step, step), step)
            out_ref[:, lanes] = ref[at * width : (at + 1) * width].astype(F32)
        for extra in more:
            half = extra.shape[0] // 2
            extra[pl.ds(pl.multiple_of(place * half, half), half)] = ref[wide // 2 // step * width :].astype(F32)


def rest_final(own_ref, other_ref, q_ref, k_ref, v_ref, small_ref):
    width = q_ref.shape[0]
    half = width // 2
    for place, ref in places(own_ref, other_ref):
        lanes = pl.ds(pl.multiple_of(place * half, half), half)
        for at, out in enumerate((q_ref, k_ref, v_ref)):
            out[:, lanes] = ref[at * width : (at + 1) * width].astype(F32)
        small_ref[pl.ds(pl.multiple_of(place * 16, 16), 16)] = ref[3 * width : 3 * width + 16].astype(F32)


def add_back_kernel(part_ref, returned_ref, out_ref):
    out_ref[...] = part_ref[...] + returned_ref[...].astype(F32)


def call(kernel, operands, results, scratch=(), limit=6):
    nbytes = sum(a.size * a.dtype.itemsize for a in operands) + sum(
        math.prod(s) * jnp.dtype(d).itemsize for s, d in results
    )
    return pl.pallas_call(
        kernel,
        out_shape=tuple(jax.ShapeDtypeStruct(s, d) for s, d in results),
        in_specs=[VMEM] * len(operands),
        out_specs=tuple(VMEM for _ in results),
        scratch_shapes=list(scratch),
        compiler_params=pltpu.CompilerParams(vmem_limit_bytes=limit * MEGA),
        cost_estimate=pl.CostEstimate(flops=STEP_FLOPS, bytes_accessed=nbytes, transcendentals=0),
    )(*operands)


def exchanges(batches, blocks):
    number = batches * blocks

    def pairs(partner):
        return [
            (d, p[0] * blocks + p[1])
            for d in range(number)
            for p in [partner(d // blocks, d % blocks)]
        ]

    def flip(place):
        return (pairs(lambda b, s: (b ^ place, s)), lambda b, s: (b & place) // place)

    found = {
        "core": flip(1),
        "across": (
            pairs(lambda b, s: (b, s ^ 1) if b % 2 == 0 else (b ^ 2, s)),
            lambda b, s: jnp.where(b & 1 == 0, s, (b >> 1) & 1),
        ),
        "along": (
            pairs(lambda b, s: (b ^ 2, s) if b % 2 == 0 else (b, s ^ 1)),
            lambda b, s: jnp.where(b & 1 == 0, (b >> 1) & 1, s),
        ),
        "up": flip(4),
    }
    rest = []
    place = 8
    while place < batches:
        rest.append(flip(place))
        place *= 2
    return found, rest


def added(left, right, rows):
    return (left[rows].astype(F32) + right[rows].astype(F32)).astype(BF16)


def halve_kernel(bit, kept_ref, arrived_ref, sent_ref, left_ref):
    half, mine = sent_ref.shape[0], bit(lax.axis_index("batch"), lax.axis_index("seq"))
    step = 16 * math.gcd(half // 16, 8)
    for place, ref in ((1 - mine, sent_ref), (mine, left_ref)):
        for at in range(0, half, step):
            rows = pl.ds(pl.multiple_of(place * half + at, 16), step)
            ref[at : at + step] = added(kept_ref, arrived_ref, rows)


def add_kernel(kept_ref, arrived_ref, out_ref):
    half = out_ref.shape[0]
    step = 16 * math.gcd(half // 16, 8)
    for at in range(0, half, step):
        out_ref[at : at + step] = added(kept_ref, arrived_ref, slice(at, at + step))


def double_kernel(bit, kept_ref, arrived_ref, out_ref):
    half, mine = kept_ref.shape[0], bit(lax.axis_index("batch"), lax.axis_index("seq"))
    for place, ref in ((mine, kept_ref), (1 - mine, arrived_ref)):
        out_ref[pl.ds(pl.multiple_of(place * half, 16), half)] = ref[...]


def choose_kernel(bit, kept0_ref, arrived0_ref, kept1_ref, arrived1_ref, sent_ref, left_ref):
    mine = bit(lax.axis_index("batch"), lax.axis_index("seq"))
    step = 128
    for at in range(0, sent_ref.shape[0], step):
        rows = slice(at, at + step)
        zero, one = added(kept0_ref, arrived0_ref, rows), added(kept1_ref, arrived1_ref, rows)
        left_ref[rows] = jnp.where(mine == 0, zero, one)
        sent_ref[rows] = jnp.where(mine == 0, one, zero)


def pick_kernel(bit, zero_ref, one_ref, sent_ref, left_ref):
    mine = bit(lax.axis_index("batch"), lax.axis_index("seq"))

    @pl.when(mine == 0)
    def _():
        left_ref[...] = zero_ref[...]
        sent_ref[...] = one_ref[...]

    @pl.when(mine != 0)
    def _():
        left_ref[...] = one_ref[...]
        sent_ref[...] = zero_ref[...]


class Sum:
    def __init__(self, halvings, fulls, sent, kept, finish):
        self.halvings, self.fulls, self.finish = halvings, fulls, finish
        self.sent, self.kept, self.arrived, self.at = sent, kept, None, 0

    def start(self, exchange):
        self.arrived = lax.ppermute(self.sent, AXES, exchange[0])

    def add(self):
        (self.kept,) = call(add_kernel, (self.kept, self.arrived), [(self.kept.shape, BF16)])
        self.sent = self.kept

    def advance(self, *after):
        count, at = len(self.halvings), self.at
        self.at += 1
        if at == 0:
            self.sent = fence(self.sent, *after)[0]
            self.start(self.halvings[0])
            return self.sent
        self.kept = fence(self.kept, *after)[0]
        rows, columns = self.kept.shape
        if at < count:
            self.sent, self.kept = call(
                functools.partial(halve_kernel, self.halvings[at][1]),
                (self.kept, self.arrived),
                [((rows // 2, columns), BF16)] * 2,
            )
            self.start(self.halvings[at])
        elif at == count:
            self.add()
            self.start(self.fulls[0])
        elif at == count + 1:
            for exchange in self.fulls[1:]:
                self.add()
                self.start(exchange)
            self.add()
            self.start(self.halvings[-1])
        elif at <= 2 * count:
            (self.kept,) = call(
                functools.partial(double_kernel, self.halvings[2 * count + 1 - at + 0][1]),
                (self.kept, self.arrived),
                [((rows * 2, columns), BF16)],
            )
            self.sent = self.kept
            self.start(self.halvings[2 * count - at])
        else:
            self.result = self.finish(self.kept, self.arrived)
            return self.result[0]
        return self.sent


def fence(*arrays):
    return lax.optimization_barrier(arrays)


def body(
    inputs,
    memory,
    cotangent,
    labels,
    attention_gain,
    query_weight,
    key_weight,
    value_weight,
    out_weight,
    forward_gain,
    up_weight,
    down_weight,
    boundary_hidden,
    boundary_out,
):
    group, block, width = inputs.shape
    wide, hidden_wide = up_weight.shape[1], boundary_hidden.shape[1]
    batches, blocks = (lax.axis_size("batch"), lax.axis_size("seq"))
    found, fulls = exchanges(batches, blocks)
    column = lax.axis_index("seq")
    core = lax.axis_index("batch") % 2
    rows = inputs.reshape(block, width)
    memory_rows = memory.reshape(block, width)
    onward = [(i, i + 1) for i in range(blocks - 1)]
    side1 = lax.ppermute(rows[TILE:], "seq", onward)
    side0 = lax.ppermute(rows[:TILE], "seq", onward)
    tables = rotary_tables(-block, (blocks + 1) * block)
    cosine, sine = (
        lax.dynamic_slice_in_dim(jnp.asarray(t), column * block, 2 * block) for t in tables
    )
    gain = attention_gain.reshape(1, width)
    square, side_shape = (block, width), (TILE, width)
    turned_square, turned_side = (width, block), (width, TILE)
    normed_t, queries, queries_t, keys, keys_t, values, values_t = call(
        own_kernel,
        (rows, gain, query_weight, key_weight, value_weight, cosine, sine),
        [(turned_square, BF16), (square, BF16), (turned_square, BF16)]
        + [(square, BF16), (turned_square, BF16)] * 2,
    )
    side_results = [
        (turned_side, BF16), (side_shape, BF16), (turned_side, BF16), (side_shape, BF16), (turned_side, BF16),
        ((HEADS, 2 * TILE, TILE), BF16), (turned_side, BF16),
    ]
    sn_t1, sk1, sk_t1, sv1, sv_t1, weights1, mix1 = call(
        late_kernel,
        (memory_rows, side1, gain, key_weight, value_weight, cosine, sine, queries_t, keys, values_t),
        side_results,
    )
    sn_t0, sk0, sk_t0, sv0, sv_t0, weights0, mix0 = call(
        early_kernel,
        (memory_rows, side0, gain, key_weight, value_weight, cosine, sine, queries_t, keys, values_t, sk1, sv_t1),
        side_results,
    )
    bh_half = (hidden_wide // 2 * width // 512, 512)
    (
        mixed_t, hidden, normed_hidden_t, gated, slope, outputs, probe_grad, hidden_sent, hidden_kept,
        boundary_out_grad,
    ) = call(
        forward_kernel,
        (
            rows, mix0, mix1, out_weight, forward_gain.reshape(1, width), up_weight, down_weight,
            boundary_hidden, boundary_out.reshape(1, hidden_wide), labels,
        ),
        [
            (turned_square, BF16), (square, F32), (turned_square, BF16), ((block, wide), BF16),
            ((block, wide), BF16), (square, BF16), ((block, hidden_wide), BF16),
            (bh_half, BF16), (bh_half, BF16), ((1, hidden_wide), F32),
        ],
        [
            pltpu.VMEM((block, hidden_wide), BF16),
            pltpu.VMEM((block, hidden_wide), BF16),
            pltpu.VMEM((width, block), BF16),
        ],
        limit=18,
    )
    sums, made = {}, {}

    def add_sum(name, way, sent, kept, finish):
        sums[name] = Sum([found[w] for w in way], fulls, sent, kept, finish)

    add_sum(
        "hidden", ("core", "across", "along", "up"), hidden_sent, hidden_kept,
        lambda own, other: call(wide_final, (own, other), [((width, hidden_wide), F32)]),
    )
    up_half = (wide // 2 * width // 512 + width // 2, 512)
    grads_shape = ((3 * width + 128, width // 2), BF16)
    work = [pltpu.VMEM((width // 2, block), F32)]
    shared = (
        queries, sv0, sv1, values, sk_t0, sk_t1, keys_t,
        cosine, sine, normed_t, sn_t0, sn_t1, query_weight, key_weight, value_weight,
    )

    def down_part(*after):
        grad = fence(probe_grad, *after)[0]
        final_grad, up_grad, sent, kept = call(
            down_kernel,
            (grad, boundary_hidden, cotangent.reshape(square), gated, slope, down_weight),
            [(square, F32), ((block, wide), BF16), ((wide // 2, width), BF16), ((wide // 2, width), BF16)],
        )
        made["down"] = (final_grad, up_grad)
        add_sum(
            "down", ("core", "up", "across", "along"), sent, kept,
            lambda own, other: call(tall_final, (own, other), [((wide, width), F32)]),
        )
        return up_grad

    def up_part(*after):
        final_grad, up_grad = made["down"]
        up_grad = fence(up_grad, *after)[0]
        hidden_grad, mixed_grad, mixed_grad_t, gain_part, sent, kept = call(
            up_kernel,
            (
                normed_hidden_t, up_grad, up_weight, hidden, forward_gain.reshape(1, width), final_grad,
                mixed_t, out_weight,
            ),
            [
                (square, F32), (square, BF16), (turned_square, BF16), ((1, width), F32),
                (up_half, BF16), (up_half, BF16),
            ],
        )
        made["up"] = (hidden_grad, (weights0, weights1, mixed_grad, mixed_grad_t) + shared, gain_part)
        add_sum(
            "up", ("core", "across", "along", "up"), sent, kept,
            lambda own, other: call(
                wide_final, (own, other), [((width, wide), F32), ((width, width), F32)]
            ),
        )
        return mixed_grad

    def attention0(*after):
        hidden_grad, operands, gain_part = made["up"]
        operands = (fence(weights0, *after)[0],) + operands[1:]
        made["attention"] = call(
            functools.partial(attention_kernel, 0, False),
            operands + (boundary_out_grad, gain_part),
            [(square, F32), (square, F32), grads_shape],
            work,
            limit=10,
        )
        return made["attention"][0]

    def attention1(*after):
        hidden_grad, operands, _ = made["up"]
        upstream, side_upstream, grads0 = made["attention"]
        upstream = fence(upstream, *after)[0]
        input_part, side_grad, grads1 = call(
            functools.partial(attention_kernel, 1, True),
            operands + (rows, memory_rows, side0, side1, gain, hidden_grad, upstream, side_upstream),
            [(square, F32), (square, BF16), grads_shape],
            work,
            limit=10,
        )
        made["input"] = (input_part, side_grad)
        picked = call(
            functools.partial(pick_kernel, found["core"][1]), (grads0, grads1), [grads_shape] * 2
        )
        add_sum(
            "rest", ("core", "across", "along", "up"), *picked,
            lambda own, other: call(
                rest_final, (own, other), [((width, width), F32)] * 3 + [((32, width // 2), F32)]
            ),
        )
        return picked[0]

    def send_back(*after):
        input_part, side_grad = made["input"]
        side_grad = fence(side_grad, *after)[0]
        made["returned"] = lax.ppermute(side_grad, "seq", [(i + 1, i) for i in range(blocks - 1)])
        return side_grad

    def add_back(*after):
        input_part = fence(made["input"][0], *after)[0]
        (made["input_grad"],) = call(add_back_kernel, (input_part, made["returned"]), [(square, F32)])
        return made["input_grad"]

    parts = {
        "a": down_part, "b": up_part, "c": attention0, "d": attention1, "r": send_back, "s": add_back,
    }
    names = {"H": "hidden", "D": "down", "U": "up", "T": "rest"}
    token = hidden_kept
    for letter in ORDER:
        token = parts[letter](token) if letter in parts else sums[names[letter]].advance(token)
    (hidden_total,), (down_total,) = (sums["hidden"].result, sums["down"].result)
    up_total, out_total = sums["up"].result
    query_total, key_total, value_total, small = sums["rest"].result
    input_grad = made["input_grad"]
    small0, small1 = (small[:16].reshape(-1), small[16:].reshape(-1))
    return (
        outputs.reshape(inputs.shape),
        input_grad.reshape(inputs.shape),
        small1[:width],
        query_total,
        key_total,
        value_total,
        out_total,
        small0[hidden_wide : hidden_wide + width],
        up_total,
        down_total,
        hidden_total,
        small0[:hidden_wide],
    )


def solution(mesh):
    placed = (
        P("batch", "seq", None),
        P("batch", None, None),
        P("batch", "seq", None),
        P("batch", "seq"),
        P(),
        P(),
        P(),
        P(),
        P(),
        P(),
        P(),
        P(),
        P(),
        P(),
    )
    return jax.shard_map(
        body,
        mesh=mesh,
        in_specs=placed,
        out_specs=(
            P("batch", "seq", None),
            P("batch", "seq", None),
            P(),
            P(),
            P(),
            P(),
            P(),
            P(),
            P(),
            P(),
            P(),
            P(),
        ),
        check_vma=False,
    )
```

```python
import functools
import math

import jax
import jax.numpy as jnp
import numpy as np
from jax import lax
from jax.experimental import pallas as pl
from jax.experimental.pallas import tpu as pltpu
from jax.sharding import PartitionSpec as P

HEADS = 8
HEAD = 64
PAIR = 2 * HEAD
TILE = 256
EPS = 1e-05
BASE = 10000.0
AXES = ("batch", "seq")
F32, BF16 = jnp.float32, jnp.bfloat16
VMEM = pl.BlockSpec(memory_space=pltpu.VMEM)
STEP_FLOPS = int(2e10)
MEGA = 1024 * 1024
ORDER = "HaDHbDUcHUDdTHUDTHrDUTHDUsHTDHTUDHTUHDTUDTUTUT"


def dot(left, right):
    return jnp.dot(left, right, preferred_element_type=F32)


def dot_t(left, right):
    return lax.dot_general(left, right, (((1,), (1,)), ((), ())), preferred_element_type=F32)


def t_dot(left, right):
    return lax.dot_general(left, right, (((0,), (0,)), ((), ())), preferred_element_type=F32)


def normalised(values):
    centre = values - jnp.mean(values, axis=-1, keepdims=True)
    spread = jnp.mean(centre * centre, axis=-1, keepdims=True)
    scale = lax.rsqrt(spread + EPS)
    return centre * scale, scale


def norm_back(unit, scale, gain, upstream):
    product = upstream * unit
    inner = upstream * gain
    mean = jnp.mean(inner, axis=-1, keepdims=True)
    along = jnp.mean(inner * unit, axis=-1, keepdims=True)
    return scale * (inner - mean - unit * along), jnp.sum(product, axis=0, keepdims=True)


def gelu_both(value):
    factor = math.sqrt(2.0 / math.pi)
    square = value * value
    half = 0.5 + 0.5 * jnp.tanh(value * (factor + (factor * 0.044715) * square))
    result = value * half
    bend = (result - result * half) * (2.0 * factor + (6.0 * factor * 0.044715) * square)
    return result, half + bend


def turned(values, cosine, sine):
    front = lax.broadcasted_iota(jnp.int32, (values.shape[0], PAIR), 1) % HEAD < HEAD // 2
    parts = []
    for at in range(0, values.shape[1], PAIR):
        part = values[:, at : at + PAIR]
        other = jnp.where(
            front, pltpu.roll(part, PAIR - HEAD // 2, 1), pltpu.roll(part, HEAD // 2, 1)
        )
        parts.append(part * cosine + other * sine)
    return jnp.concatenate(parts, axis=1)


def rotary_tables(first, count):
    positions = np.arange(first, first + count, dtype=np.float32)
    half = HEAD // 2
    freqs = np.float32(BASE) ** (-(np.arange(half, dtype=np.float32) * np.float32(2.0 / HEAD)))
    angles = (positions[:, None] * freqs[None, :].astype(np.float32)).astype(np.float64)
    cosine, sine = (np.cos(angles), np.sin(angles))
    return (
        np.concatenate([cosine] * 4, axis=1).astype(np.float32),
        np.concatenate([-sine, sine] * 2, axis=1).astype(np.float32),
    )


def own_kernel(
    x_ref, gain_ref, wq_ref, wk_ref, wv_ref, cos_ref, sin_ref,
    nt_ref, q_ref, qt_ref, k_ref, kt_ref, v_ref, vt_ref,
):
    unit, _ = normalised(x_ref[...].astype(F32))
    low = (unit * gain_ref[...]).astype(BF16)
    nt_ref[...] = jnp.transpose(low)
    block = low.shape[0]
    cosine, sine = cos_ref[block:], sin_ref[block:]
    scale = 1.0 / math.sqrt(HEAD)
    query = turned(dot(low, wq_ref[...]), cosine, sine).astype(BF16).astype(F32) * scale
    query = query.astype(BF16)
    q_ref[...] = query
    qt_ref[...] = jnp.transpose(query)
    key = turned(dot(low, wk_ref[...]), cosine, sine).astype(BF16)
    k_ref[...] = key
    kt_ref[...] = jnp.transpose(key)
    value = dot(low, wv_ref[...]).astype(BF16)
    v_ref[...] = value
    vt_ref[...] = jnp.transpose(value)


def before_diagonal():
    key = lax.broadcasted_iota(jnp.int32, (TILE, TILE), 0)
    return key <= lax.broadcasted_iota(jnp.int32, (TILE, TILE), 1)


def halves(array, seen):
    none = jnp.zeros_like(array)
    return jnp.where(seen, none, array), jnp.where(seen, array, none)


def attend(q_t, keys, values_t, w_ref, mix_ref):
    seen = before_diagonal()
    pairs = mix_ref.shape[0] // PAIR

    def one_pair(pair, carry):
        lanes = pl.ds(pl.multiple_of(pair * PAIR, PAIR), PAIR)
        both = q_t(lanes)
        row = lax.broadcasted_iota(jnp.int32, both.shape, 0)
        for head in range(2):
            query = jnp.where(row // HEAD == head, both, jnp.zeros_like(both))
            first, middle, last = [dot(block(lanes), query) for block in keys]
            edge = jnp.where(seen, last, first)
            peak = jnp.maximum(
                jnp.max(edge, axis=0, keepdims=True), jnp.max(middle, axis=0, keepdims=True)
            )
            edge, middle = jnp.exp(edge - peak), jnp.exp(middle - peak)
            total = jnp.sum(edge + middle, axis=0, keepdims=True)
            edge, middle = (edge / total).astype(BF16), (middle / total).astype(BF16)
            w_ref[2 * pair + head, :TILE] = edge
            w_ref[2 * pair + head, TILE:] = middle
            own = pl.ds(pl.multiple_of(pair * PAIR + head * HEAD, HEAD), HEAD)
            left, right = halves(edge, seen)
            mix = dot(values_t[0](own), left) + dot(values_t[1](own), middle)
            mix_ref[own] = (mix + dot(values_t[2](own), right)).astype(BF16)
        return carry

    lax.fori_loop(0, pairs, one_pair, 0, unroll=pairs)


def side_rows(memory_ref, received_ref):
    return jnp.where(lax.axis_index("seq") == 0, memory_ref[...], received_ref[...]).astype(F32)


def side_part(memory_ref, received_ref, gain_ref, wk_ref, wv_ref, cos_ref, sin_ref, snt_ref, k_ref, kt_ref, v_ref, vt_ref):
    unit, _ = normalised(side_rows(memory_ref, received_ref))
    low = (unit * gain_ref[...]).astype(BF16)
    snt_ref[...] = jnp.transpose(low)
    key = turned(dot(low, wk_ref[...]), cos_ref[...], sin_ref[...]).astype(BF16)
    k_ref[...] = key
    kt_ref[...] = jnp.transpose(key)
    value = dot(low, wv_ref[...]).astype(BF16)
    v_ref[...] = value
    vt_ref[...] = jnp.transpose(value)


def late_kernel(
    memory_ref, received_ref, gain_ref, wk_ref, wv_ref, cos_ref, sin_ref, qt_ref, ok_ref, ovt_ref,
    snt_ref, k_ref, kt_ref, v_ref, vt_ref, w_ref, mix_ref,
):
    side_part(
        memory_ref.at[TILE:], received_ref, gain_ref, wk_ref, wv_ref, cos_ref.at[TILE : 2 * TILE], sin_ref.at[TILE : 2 * TILE],
        snt_ref, k_ref, kt_ref, v_ref, vt_ref,
    )
    attend(
        lambda at: qt_ref[at, TILE:],
        (lambda at: k_ref[:, at], lambda at: ok_ref[:TILE, at], lambda at: ok_ref[TILE:, at]),
        (lambda at: vt_ref[at], lambda at: ovt_ref[at, :TILE], lambda at: ovt_ref[at, TILE:]),
        w_ref,
        mix_ref,
    )


def early_kernel(
    memory_ref, received_ref, gain_ref, wk_ref, wv_ref, cos_ref, sin_ref, qt_ref, ok_ref, ovt_ref, sk_ref, svt_ref,
    snt_ref, k_ref, kt_ref, v_ref, vt_ref, w_ref, mix_ref,
):
    side_part(
        memory_ref.at[:TILE], received_ref, gain_ref, wk_ref, wv_ref, cos_ref.at[:TILE], sin_ref.at[:TILE],
        snt_ref, k_ref, kt_ref, v_ref, vt_ref,
    )
    attend(
        lambda at: qt_ref[at, :TILE],
        (lambda at: k_ref[:, at], lambda at: sk_ref[:, at], lambda at: ok_ref[:TILE, at]),
        (lambda at: vt_ref[at], lambda at: svt_ref[at], lambda at: ovt_ref[at, :TILE]),
        w_ref,
        mix_ref,
    )


def forward_kernel(
    x_ref, mix0_ref, mix1_ref, wo_ref, fgain_ref, up_ref, down_ref, bh_ref, bo_ref, labels_ref,
    mixt_ref, hidden_ref, nht_ref, gated_ref, slope_ref, out_ref, pg_ref, sent_ref, kept_ref, bog_ref,
    probe_ref, pslope_ref, turn_ref,
):
    block, width = x_ref.shape
    mixt_ref[:, :TILE] = mix0_ref[...]
    mixt_ref[:, TILE:] = mix1_ref[...]
    mixed = jnp.transpose(mixt_ref[...])
    hidden = x_ref[...].astype(F32) + dot(mixed, wo_ref[...])
    hidden_ref[...] = hidden
    unit, _ = normalised(hidden)
    low = (unit * fgain_ref[...]).astype(BF16)
    nht_ref[...] = jnp.transpose(low)
    step = 1024
    tops = [slice(top, top + TILE) for top in range(0, block, TILE)]
    for part_rows in tops:
        part = hidden[part_rows]
        for at in range(0, up_ref.shape[1], step):
            gated, slope = gelu_both(dot(low[part_rows], up_ref[:, at : at + step]))
            gated = gated.astype(BF16)
            gated_ref[part_rows, at : at + step] = gated
            slope_ref[part_rows, at : at + step] = slope.astype(BF16)
            part = part + dot(gated, down_ref[at : at + step])
        out_ref[part_rows] = part.astype(BF16)
    out = out_ref[...]
    turn_ref[...] = jnp.transpose(out)
    logits = []
    for part_rows in tops:
        logit = jnp.zeros((TILE, 1), F32)
        for at in range(0, bh_ref.shape[1], step):
            probe, slope = gelu_both(dot(out[part_rows], bh_ref[:, at : at + step]))
            probe = probe.astype(BF16)
            probe_ref[part_rows, at : at + step] = probe
            pslope_ref[part_rows, at : at + step] = slope.astype(BF16)
            logit = logit + jnp.sum(
                probe.astype(F32) * bo_ref[:, at : at + step].astype(F32), axis=-1, keepdims=True
            )
        logits.append(logit)
    logits = jnp.concatenate(logits, axis=0)
    targets = jnp.transpose(jnp.broadcast_to(labels_ref[...].astype(F32), (PAIR, block)))[:, :1]
    signal = (jax.nn.sigmoid(logits) - targets).astype(BF16).astype(F32)
    step = 512
    half = bh_ref.shape[1] // 2
    core = lax.axis_index("batch") & 1
    for at in range(0, bh_ref.shape[1], step):
        grad = pslope_ref[:, at : at + step].astype(F32) * (
            signal * bo_ref[:, at : at + step].astype(F32)
        )
        pg_ref[:, at : at + step] = grad.astype(BF16)
    for place, ref in ((1 - core, sent_ref), (core, kept_ref)):
        for at in range(0, half, step):
            grad = pg_ref[:, pl.ds(pl.multiple_of(place * half + at, step), step)]
            ref[at * width // step : (at + step) * width // step] = dot(turn_ref[...], grad).astype(BF16)
    for at in range(0, bh_ref.shape[1], step):
        bog_ref[:, at : at + step] = jnp.sum(
            signal * probe_ref[:, at : at + step].astype(F32), axis=0, keepdims=True
        )


def down_kernel(pg_ref, bh_ref, cot_ref, gated_ref, slope_ref, down_ref, grad_ref, upg_ref, sent_ref, kept_ref):
    final = cot_ref[...].astype(F32) + dot_t(pg_ref[...], bh_ref[...])
    grad_ref[...] = final
    low = final.astype(BF16)
    step = 512
    half = down_ref.shape[0] // 2
    core = lax.axis_index("batch") & 1
    for at in range(0, half, step):
        rows = pl.ds(pl.multiple_of((1 - core) * half + at, step), step)
        sent_ref[at : at + step] = t_dot(gated_ref[:, rows], low).astype(BF16)
    for at in range(0, half, step):
        rows = pl.ds(pl.multiple_of(core * half + at, step), step)
        kept_ref[at : at + step] = t_dot(gated_ref[:, rows], low).astype(BF16)
    for at in range(0, down_ref.shape[0], step):
        part = slope_ref[:, at : at + step].astype(F32) * dot_t(low, down_ref[at : at + step])
        upg_ref[:, at : at + step] = part.astype(BF16)


def up_kernel(
    nht_ref, upg_ref, up_ref, hidden_ref, fgain_ref, grad_ref, mixt_ref, wo_ref,
    hg_ref, mg_ref, mgt_ref, fgg_ref, sent_ref, kept_ref,
):
    width, wide = up_ref.shape
    upstream = dot_t(upg_ref[...], up_ref[...])
    unit, scale = normalised(hidden_ref[...])
    part, gain_part = norm_back(unit, scale, fgain_ref[...], upstream)
    fgg_ref[...] = gain_part
    total = grad_ref[...] + part
    hg_ref[...] = total
    low = total.astype(BF16)
    mixed_grad = dot_t(low, wo_ref[...]).astype(BF16)
    mg_ref[...] = mixed_grad
    mgt_ref[...] = jnp.transpose(mixed_grad)
    core = lax.axis_index("batch") & 1
    half, step = wide // 2, 512
    for place, ref in ((1 - core, sent_ref), (core, kept_ref)):
        for at in range(0, half, step):
            grad = upg_ref[:, pl.ds(pl.multiple_of(place * half + at, step), step)]
            ref[at * width // step : (at + step) * width // step] = dot(nht_ref[...], grad).astype(BF16)
        rows = pl.ds(pl.multiple_of(place * (width // 2), width // 2), width // 2)
        ref[half * width // step :] = dot(mixt_ref[rows], low).astype(BF16)


def attend_back(pair, tile, w_ref, mg_ref, mgt_ref, q_ref, values, keys_t, dq_ref, dks, dvs):
    seen = before_diagonal()
    lanes = slice(pair * PAIR, (pair + 1) * PAIR)
    rows = slice(tile * TILE, (tile + 1) * TILE)
    upstream_t, upstream, query = mgt_ref[lanes, rows], mg_ref[rows, lanes], q_ref[rows, lanes]
    row = lax.broadcasted_iota(jnp.int32, (PAIR, TILE), 0)
    lane = lax.broadcasted_iota(jnp.int32, (TILE, PAIR), 1)
    none, none_t = jnp.zeros_like(upstream), jnp.zeros_like(upstream_t)
    for head in range(2):
        above_t = jnp.where(row // HEAD == head, upstream_t, none_t)
        first, middle_grad, last = [dot(block[:, lanes], above_t) for block in values]
        edge_grad = jnp.where(seen, last, first)
        weights = w_ref[2 * pair + head]
        edge, middle = weights[:TILE].astype(F32), weights[TILE:].astype(F32)
        centred = jnp.sum(edge * edge_grad + middle * middle_grad, axis=0, keepdims=True)
        edge = (edge * (edge_grad - centred)).astype(BF16)
        middle = (middle * (middle_grad - centred)).astype(BF16)
        left, right = halves(edge, seen)
        above = jnp.where(lane // HEAD == head, upstream, none)
        one = jnp.where(lane // HEAD == head, query, none)
        own = slice(pair * PAIR + head * HEAD, pair * PAIR + (head + 1) * HEAD)
        grad = dot(keys_t[0][own], left) + dot(keys_t[1][own], middle) + dot(keys_t[2][own], right)
        inside = (pair * PAIR + head * HEAD) % dq_ref.shape[0]
        dq_ref[inside : inside + HEAD, rows] = grad
        w_left, w_right = halves(weights[:TILE], seen)
        for place, part in enumerate((left, middle, right)):
            dks[place] = dks[place] + dot(part, one)
        for place, part in enumerate((w_left, weights[TILE:], w_right)):
            dvs[place] = dvs[place] + dot(part, above)


def rows_of(*smalls):
    rows = [s[:, at : at + TILE] for s in smalls for at in range(0, s.shape[1], TILE)]
    rows.append(jnp.zeros((128 - len(rows), TILE), F32))
    return jnp.concatenate(rows, axis=0).astype(BF16)


def attention_kernel(
    part, final, w0_ref, w1_ref, mg_ref, mgt_ref, q_ref, sv0_ref, sv1_ref, v_ref, skt0_ref, skt1_ref, kt_ref,
    cos_ref, sin_ref, nt_ref, snt0_ref, snt1_ref, wq_ref, wk_ref, wv_ref, *rest,
):
    if final:
        x_ref, memory_ref, side0_ref, side1_ref, gain_ref, hg_ref, up_ref, sup_ref, ig_ref, sg_ref, grads_ref, dq_ref = rest
    else:
        bog_ref, fgg_ref, nup_ref, nsup_ref, grads_ref, dq_ref = rest
    block, width = q_ref.shape
    pairs = width // PAIR // 2
    values = (sv0_ref, sv1_ref, v_ref.at[:TILE], v_ref.at[TILE:])
    keys_t = (skt0_ref, skt1_ref, kt_ref.at[:, :TILE], kt_ref.at[:, TILE:])
    dk_parts, dv_parts = [[] for _ in range(4)], [[] for _ in range(4)]
    for pair in range(part * pairs, (part + 1) * pairs):
        dk, dv = [0.0] * 4, [0.0] * 4
        for tile, w_ref in ((1, w1_ref), (0, w0_ref)):
            dks, dvs = dk[tile : tile + 3], dv[tile : tile + 3]
            attend_back(
                pair, tile, w_ref, mg_ref, mgt_ref, q_ref, values[tile : tile + 3], keys_t[tile : tile + 3],
                dq_ref, dks, dvs,
            )
            dk[tile : tile + 3], dv[tile : tile + 3] = dks, dvs
        for place in range(4):
            dk_parts[place].append(dk[place])
            dv_parts[place].append(dv[place])
    dk = [jnp.concatenate(p, axis=1) for p in dk_parts]
    dv = [jnp.concatenate(p, axis=1).astype(BF16) for p in dv_parts]
    lanes = slice(part * (width // 2), (part + 1) * (width // 2))
    scale = 1.0 / math.sqrt(HEAD)
    cosine, sine = cos_ref[...], -sin_ref[...]
    dq = turned(jnp.transpose(dq_ref[...]) * scale, cosine[block:], sine[block:]).astype(BF16)
    dk = [
        turned(p, cosine[i * TILE : (i + 1) * TILE], sine[i * TILE : (i + 1) * TILE]).astype(BF16)
        for i, p in enumerate(dk)
    ]
    own_k, own_v = jnp.concatenate(dk[2:], axis=0), jnp.concatenate(dv[2:], axis=0)
    side_k, side_v = jnp.concatenate(dk[:2], axis=0), jnp.concatenate(dv[:2], axis=0)
    rows_t = nt_ref[...]
    side_t = jnp.concatenate([snt0_ref[...], snt1_ref[...]], axis=1)
    grads_ref[:width] = dot(rows_t, dq).astype(BF16)
    grads_ref[width : 2 * width] = (dot(rows_t, own_k) + dot(side_t, side_k)).astype(BF16)
    grads_ref[2 * width : 3 * width] = (dot(rows_t, own_v) + dot(side_t, side_v)).astype(BF16)
    wk, wv = wk_ref[:, lanes], wv_ref[:, lanes]
    upstream = dot_t(dq, wq_ref[:, lanes]) + dot_t(own_k, wk) + dot_t(own_v, wv)
    side_up = dot_t(side_k, wk) + dot_t(side_v, wv)
    if not final:
        grads_ref[3 * width :] = rows_of(bog_ref[...], fgg_ref[...])
        nup_ref[...] = upstream
        nsup_ref[...] = side_up
        return
    upstream = upstream + up_ref[...]
    side_up = side_up + sup_ref[...]
    unit, spread = normalised(x_ref[...].astype(F32))
    back, gain_part = norm_back(unit, spread, gain_ref[...], upstream)
    ig_ref[...] = hg_ref[...] + back
    for i, ref in enumerate((side0_ref, side1_ref)):
        at = slice(i * TILE, (i + 1) * TILE)
        unit, spread = normalised(side_rows(memory_ref.at[at], ref))
        back, side_gain = norm_back(unit, spread, gain_ref[...], side_up[at])
        sg_ref[at] = back.astype(BF16)
        gain_part = gain_part + side_gain
    grads_ref[3 * width :] = rows_of(gain_part)


def places(own_ref, other_ref):
    core = lax.axis_index("batch") & 1
    return ((core, own_ref), (1 - core, other_ref))


def tall_final(own_ref, other_ref, out_ref):
    half = own_ref.shape[0]
    for place, ref in places(own_ref, other_ref):
        out_ref[pl.ds(pl.multiple_of(place * half, half), half)] = ref[...].astype(F32)


def wide_final(own_ref, other_ref, out_ref, *more):
    width, wide = out_ref.shape
    step = own_ref.shape[1]
    for place, ref in places(own_ref, other_ref):
        for at in range(wide // 2 // step):
            lanes = pl.ds(pl.multiple_of(place * (wide // 2) + at * step, step), step)
            out_ref[:, lanes] = ref[at * width : (at + 1) * width].astype(F32)
        for extra in more:
            half = extra.shape[0] // 2
            extra[pl.ds(pl.multiple_of(place * half, half), half)] = ref[wide // 2 // step * width :].astype(F32)


def rest_final(own_ref, other_ref, q_ref, k_ref, v_ref, bog_ref, fgg_ref, gg_ref):
    width = q_ref.shape[0]
    half = width // 2
    for place, ref in places(own_ref, other_ref):
        lanes = pl.ds(pl.multiple_of(place * half, half), half)
        for at, out in enumerate((q_ref, k_ref, v_ref)):
            out[:, lanes] = ref[at * width : (at + 1) * width].astype(F32)

    own, other = (ref[3 * width : 3 * width + 16].astype(F32) for ref in (own_ref, other_ref))
    core = lax.axis_index("batch") & 1
    zero, one = jnp.where(core == 0, own, other), jnp.where(core == 0, other, own)
    count = bog_ref.shape[0] // half
    for out, rows, first in ((bog_ref, zero, 0), (fgg_ref, zero, count), (gg_ref, one, 0)):
        for at in range(out.shape[0] // half):
            out[at * half : (at + 1) * half] = rows[first + at]


def add_back_kernel(part_ref, returned_ref, out_ref):
    out_ref[...] = part_ref[...] + returned_ref[...].astype(F32)


def call(kernel, operands, results, scratch=(), limit=6):
    nbytes = sum(a.size * a.dtype.itemsize for a in operands) + sum(
        math.prod(s) * jnp.dtype(d).itemsize for s, d in results
    )
    return pl.pallas_call(
        kernel,
        out_shape=tuple(jax.ShapeDtypeStruct(s, d) for s, d in results),
        in_specs=[VMEM] * len(operands),
        out_specs=tuple(VMEM for _ in results),
        scratch_shapes=list(scratch),
        compiler_params=pltpu.CompilerParams(vmem_limit_bytes=limit * MEGA),
        cost_estimate=pl.CostEstimate(flops=STEP_FLOPS, bytes_accessed=nbytes, transcendentals=0),
    )(*operands)


def exchanges(batches, blocks):
    number = batches * blocks

    def pairs(partner):
        return [
            (d, p[0] * blocks + p[1])
            for d in range(number)
            for p in [partner(d // blocks, d % blocks)]
        ]

    flips = {
        "x": (lambda b, s: (b, s ^ 1), lambda b, s: s),
        "y": (lambda b, s: (b ^ 2, s), lambda b, s: (b & 2) // 2),
        "z": (lambda b, s: (b ^ 4, s), lambda b, s: (b & 4) // 4),
    }

    def flip(place):
        return (pairs(lambda b, s: (b ^ place, s)), lambda b, s: (b & place) // place)

    def mixed(way):
        (first, first_bit), (second, second_bit) = (flips[axis] for axis in way)
        return (
            pairs(lambda b, s: second(b, s) if b % 2 else first(b, s)),
            lambda b, s: jnp.where(b & 1 == 0, first_bit(b, s), second_bit(b, s)),
        )

    found = {way: mixed(way) for way in ("xy", "yx", "zy", "yz", "xz", "zx", "xx", "yy", "zz")}
    found["core"] = flip(1)
    rest = []
    place = 8
    while place < batches:
        rest.append(flip(place))
        place *= 2
    return found, rest


def added(left, right, rows):
    return (left[rows].astype(F32) + right[rows].astype(F32)).astype(BF16)


def halve_kernel(bit, kept_ref, arrived_ref, sent_ref, left_ref):
    half, mine = sent_ref.shape[0], bit(lax.axis_index("batch"), lax.axis_index("seq"))
    step = 16 * math.gcd(half // 16, 8)
    for place, ref in ((1 - mine, sent_ref), (mine, left_ref)):
        for at in range(0, half, step):
            rows = pl.ds(pl.multiple_of(place * half + at, 16), step)
            ref[at : at + step] = added(kept_ref, arrived_ref, rows)


def add_kernel(kept_ref, arrived_ref, out_ref):
    half = out_ref.shape[0]
    step = 16 * math.gcd(half // 16, 8)
    for at in range(0, half, step):
        out_ref[at : at + step] = added(kept_ref, arrived_ref, slice(at, at + step))


def double_kernel(bit, kept_ref, arrived_ref, out_ref):
    half, mine = kept_ref.shape[0], bit(lax.axis_index("batch"), lax.axis_index("seq"))
    for place, ref in ((mine, kept_ref), (1 - mine, arrived_ref)):
        out_ref[pl.ds(pl.multiple_of(place * half, 16), half)] = ref[...]


def choose_kernel(bit, kept0_ref, arrived0_ref, kept1_ref, arrived1_ref, sent_ref, left_ref):
    mine = bit(lax.axis_index("batch"), lax.axis_index("seq"))
    step = 128
    for at in range(0, sent_ref.shape[0], step):
        rows = slice(at, at + step)
        zero, one = added(kept0_ref, arrived0_ref, rows), added(kept1_ref, arrived1_ref, rows)
        left_ref[rows] = jnp.where(mine == 0, zero, one)
        sent_ref[rows] = jnp.where(mine == 0, one, zero)


def pick_kernel(bit, zero_ref, one_ref, sent_ref, left_ref):
    mine = bit(lax.axis_index("batch"), lax.axis_index("seq"))

    @pl.when(mine == 0)
    def _():
        left_ref[...] = zero_ref[...]
        sent_ref[...] = one_ref[...]

    @pl.when(mine != 0)
    def _():
        left_ref[...] = one_ref[...]
        sent_ref[...] = zero_ref[...]


class Sum:
    def __init__(self, halvings, fulls, sent, kept, finish):
        self.halvings, self.fulls, self.finish = halvings, fulls, finish
        self.sent, self.kept, self.arrived, self.at = sent, kept, None, 0

    def start(self, exchange):
        self.arrived = lax.ppermute(self.sent, AXES, exchange[0])

    def add(self):
        (self.kept,) = call(add_kernel, (self.kept, self.arrived), [(self.kept.shape, BF16)])
        self.sent = self.kept

    def advance(self, *after):
        count, at = len(self.halvings), self.at
        self.at += 1
        if at == 0:
            self.sent = fence(self.sent, *after)[0]
            self.start(self.halvings[0])
            return self.sent
        self.kept = fence(self.kept, *after)[0]
        rows, columns = self.kept.shape
        if at < count:
            self.sent, self.kept = call(
                functools.partial(halve_kernel, self.halvings[at][1]),
                (self.kept, self.arrived),
                [((rows // 2, columns), BF16)] * 2,
            )
            self.start(self.halvings[at])
        elif at == count:
            self.add()
            self.start(self.fulls[0])
        elif at == count + 1:
            for exchange in self.fulls[1:]:
                self.add()
                self.start(exchange)
            self.add()
            self.start(self.halvings[-1])
        elif at <= 2 * count:
            (self.kept,) = call(
                functools.partial(double_kernel, self.halvings[2 * count + 1 - at + 0][1]),
                (self.kept, self.arrived),
                [((rows * 2, columns), BF16)],
            )
            self.sent = self.kept
            self.start(self.halvings[2 * count - at])
        else:
            self.result = self.finish(self.kept, self.arrived)
            return self.result[0]
        return self.sent


def fence(*arrays):
    return lax.optimization_barrier(arrays)


def body(
    inputs,
    memory,
    cotangent,
    labels,
    attention_gain,
    query_weight,
    key_weight,
    value_weight,
    out_weight,
    forward_gain,
    up_weight,
    down_weight,
    boundary_hidden,
    boundary_out,
):
    group, block, width = inputs.shape
    wide, hidden_wide = up_weight.shape[1], boundary_hidden.shape[1]
    batches, blocks = (lax.axis_size("batch"), lax.axis_size("seq"))
    found, fulls = exchanges(batches, blocks)
    column = lax.axis_index("seq")
    core = lax.axis_index("batch") % 2
    rows = inputs.reshape(block, width)
    memory_rows = memory.reshape(block, width)
    onward = [(i, i + 1) for i in range(blocks - 1)]
    side1 = lax.ppermute(rows[TILE:], "seq", onward)
    side0 = lax.ppermute(rows[:TILE], "seq", onward)
    tables = rotary_tables(-block, (blocks + 1) * block)
    cosine, sine = (
        lax.dynamic_slice_in_dim(jnp.asarray(t), column * block, 2 * block) for t in tables
    )
    gain = attention_gain.reshape(1, width)
    square, side_shape = (block, width), (TILE, width)
    turned_square, turned_side = (width, block), (width, TILE)
    normed_t, queries, queries_t, keys, keys_t, values, values_t = call(
        own_kernel,
        (rows, gain, query_weight, key_weight, value_weight, cosine, sine),
        [(turned_square, BF16), (square, BF16), (turned_square, BF16)]
        + [(square, BF16), (turned_square, BF16)] * 2,
    )
    side_results = [
        (turned_side, BF16), (side_shape, BF16), (turned_side, BF16), (side_shape, BF16), (turned_side, BF16),
        ((HEADS, 2 * TILE, TILE), BF16), (turned_side, BF16),
    ]
    sn_t1, sk1, sk_t1, sv1, sv_t1, weights1, mix1 = call(
        late_kernel,
        (memory_rows, side1, gain, key_weight, value_weight, cosine, sine, queries_t, keys, values_t),
        side_results,
    )
    sn_t0, sk0, sk_t0, sv0, sv_t0, weights0, mix0 = call(
        early_kernel,
        (memory_rows, side0, gain, key_weight, value_weight, cosine, sine, queries_t, keys, values_t, sk1, sv_t1),
        side_results,
    )
    bh_half = (hidden_wide // 2 * width // 512, 512)
    (
        mixed_t, hidden, normed_hidden_t, gated, slope, outputs, probe_grad, hidden_sent, hidden_kept,
        boundary_out_grad,
    ) = call(
        forward_kernel,
        (
            rows, mix0, mix1, out_weight, forward_gain.reshape(1, width), up_weight, down_weight,
            boundary_hidden, boundary_out.reshape(1, hidden_wide), labels,
        ),
        [
            (turned_square, BF16), (square, F32), (turned_square, BF16), ((block, wide), BF16),
            ((block, wide), BF16), (square, BF16), ((block, hidden_wide), BF16),
            (bh_half, BF16), (bh_half, BF16), ((1, hidden_wide), F32),
        ],
        [
            pltpu.VMEM((block, hidden_wide), BF16),
            pltpu.VMEM((block, hidden_wide), BF16),
            pltpu.VMEM((width, block), BF16),
        ],
        limit=18,
    )
    sums, made = {}, {}

    def add_sum(name, way, sent, kept, finish):
        sums[name] = Sum([found[w] for w in way], fulls, sent, kept, finish)

    add_sum(
        "hidden", ("core", "xy", "yx", "zz"), hidden_sent, hidden_kept,
        lambda own, other: call(wide_final, (own, other), [((width, hidden_wide), F32)]),
    )
    up_half = (wide // 2 * width // 512 + width // 2, 512)
    grads_shape = ((3 * width + 128, width // 2), BF16)
    work = [pltpu.VMEM((width // 2, block), F32)]
    shared = (
        queries, sv0, sv1, values, sk_t0, sk_t1, keys_t,
        cosine, sine, normed_t, sn_t0, sn_t1, query_weight, key_weight, value_weight,
    )

    def down_part(*after):
        grad = fence(probe_grad, *after)[0]
        final_grad, up_grad, sent, kept = call(
            down_kernel,
            (grad, boundary_hidden, cotangent.reshape(square), gated, slope, down_weight),
            [(square, F32), ((block, wide), BF16), ((wide // 2, width), BF16), ((wide // 2, width), BF16)],
        )
        made["down"] = (final_grad, up_grad)
        add_sum(
            "down", ("core", "xy", "yx", "zz"), sent, kept,
            lambda own, other: call(tall_final, (own, other), [((wide, width), F32)]),
        )
        return up_grad

    def up_part(*after):
        final_grad, up_grad = made["down"]
        up_grad = fence(up_grad, *after)[0]
        hidden_grad, mixed_grad, mixed_grad_t, gain_part, sent, kept = call(
            up_kernel,
            (
                normed_hidden_t, up_grad, up_weight, hidden, forward_gain.reshape(1, width), final_grad,
                mixed_t, out_weight,
            ),
            [
                (square, F32), (square, BF16), (turned_square, BF16), ((1, width), F32),
                (up_half, BF16), (up_half, BF16),
            ],
        )
        made["up"] = (hidden_grad, (weights0, weights1, mixed_grad, mixed_grad_t) + shared, gain_part)
        add_sum(
            "up", ("core", "xy", "yx", "zz"), sent, kept,
            lambda own, other: call(
                wide_final, (own, other), [((width, wide), F32), ((width, width), F32)]
            ),
        )
        return mixed_grad

    def attention0(*after):
        hidden_grad, operands, gain_part = made["up"]
        operands = (fence(weights0, *after)[0],) + operands[1:]
        made["attention"] = call(
            functools.partial(attention_kernel, 0, False),
            operands + (boundary_out_grad, gain_part),
            [(square, F32), (square, F32), grads_shape],
            work,
            limit=10,
        )
        return made["attention"][0]

    def attention1(*after):
        hidden_grad, operands, _ = made["up"]
        upstream, side_upstream, grads0 = made["attention"]
        upstream = fence(upstream, *after)[0]
        input_part, side_grad, grads1 = call(
            functools.partial(attention_kernel, 1, True),
            operands + (rows, memory_rows, side0, side1, gain, hidden_grad, upstream, side_upstream),
            [(square, F32), (square, BF16), grads_shape],
            work,
            limit=10,
        )
        made["input"] = (input_part, side_grad)
        picked = call(
            functools.partial(pick_kernel, found["core"][1]), (grads0, grads1), [grads_shape] * 2
        )
        add_sum(
            "rest", ("core", "xy", "yx", "zz"), *picked,
            lambda own, other: call(
                rest_final, (own, other), [((width, width), F32)] * 3 + [((hidden_wide,), F32), ((width,), F32), ((width,), F32)]
            ),
        )
        return picked[0]

    def send_back(*after):
        input_part, side_grad = made["input"]
        side_grad = fence(side_grad, *after)[0]
        made["returned"] = lax.ppermute(side_grad, "seq", [(i + 1, i) for i in range(blocks - 1)])
        return side_grad

    def add_back(*after):
        input_part = fence(made["input"][0], *after)[0]
        (made["input_grad"],) = call(add_back_kernel, (input_part, made["returned"]), [(square, F32)])
        return made["input_grad"]

    parts = {
        "a": down_part, "b": up_part, "c": attention0, "d": attention1, "r": send_back, "s": add_back,
    }
    names = {"H": "hidden", "D": "down", "U": "up", "T": "rest"}
    token = hidden_kept
    for letter in ORDER:
        token = parts[letter](token) if letter in parts else sums[names[letter]].advance(token)
    (hidden_total,), (down_total,) = (sums["hidden"].result, sums["down"].result)
    up_total, out_total = sums["up"].result
    query_total, key_total, value_total, boundary_out_total, forward_gain_total, gain_total = sums["rest"].result
    input_grad = made["input_grad"]
    return (
        outputs.reshape(inputs.shape),
        input_grad.reshape(inputs.shape),
        gain_total,
        query_total,
        key_total,
        value_total,
        out_total,
        forward_gain_total,
        up_total,
        down_total,
        hidden_total,
        boundary_out_total,
    )


def solution(mesh):
    placed = (
        P("batch", "seq", None),
        P("batch", None, None),
        P("batch", "seq", None),
        P("batch", "seq"),
        P(),
        P(),
        P(),
        P(),
        P(),
        P(),
        P(),
        P(),
        P(),
        P(),
    )
    return jax.shard_map(
        body,
        mesh=mesh,
        in_specs=placed,
        out_specs=(
            P("batch", "seq", None),
            P("batch", "seq", None),
            P(),
            P(),
            P(),
            P(),
            P(),
            P(),
            P(),
            P(),
            P(),
            P(),
        ),
        check_vma=False,
    )
```

```python
import functools
import math

import jax
import jax.numpy as jnp
import numpy as np
from jax import lax
from jax.experimental import pallas as pl
from jax.experimental.pallas import tpu as pltpu
from jax.sharding import PartitionSpec as P

HEADS = 8
HEAD = 64
PAIR = 2 * HEAD
TILE = 256
EPS = 1e-05
BASE = 10000.0
AXES = ("batch", "seq")
F32, BF16 = jnp.float32, jnp.bfloat16
VMEM = pl.BlockSpec(memory_space=pltpu.VMEM)
HBM = pl.BlockSpec(memory_space=pl.ANY)
STEP_FLOPS = int(2e10)
MEGA = 1024 * 1024
ORDER = "HaDHbDUcHUDdTHUDTHrDUTHDUsHTDHTUDHTUHDTUDTUTUT"


def dot(left, right):
    return jnp.dot(left, right, preferred_element_type=F32)


def dot_t(left, right):
    return lax.dot_general(left, right, (((1,), (1,)), ((), ())), preferred_element_type=F32)


def t_dot(left, right):
    return lax.dot_general(left, right, (((0,), (0,)), ((), ())), preferred_element_type=F32)


def normalised(values):
    centre = values - jnp.mean(values, axis=-1, keepdims=True)
    spread = jnp.mean(centre * centre, axis=-1, keepdims=True)
    scale = lax.rsqrt(spread + EPS)
    return centre * scale, scale


def norm_back(unit, scale, gain, upstream):
    product = upstream * unit
    inner = upstream * gain
    mean = jnp.mean(inner, axis=-1, keepdims=True)
    along = jnp.mean(inner * unit, axis=-1, keepdims=True)
    return scale * (inner - mean - unit * along), jnp.sum(product, axis=0, keepdims=True)


def gelu_both(value):
    factor = math.sqrt(2.0 / math.pi)
    square = value * value
    half = 0.5 + 0.5 * jnp.tanh(value * (factor + (factor * 0.044715) * square))
    result = value * half
    bend = (result - result * half) * (2.0 * factor + (6.0 * factor * 0.044715) * square)
    return result, half + bend


def turned(values, cosine, sine):
    front = lax.broadcasted_iota(jnp.int32, (values.shape[0], PAIR), 1) % HEAD < HEAD // 2
    parts = []
    for at in range(0, values.shape[1], PAIR):
        part = values[:, at : at + PAIR]
        other = jnp.where(
            front, pltpu.roll(part, PAIR - HEAD // 2, 1), pltpu.roll(part, HEAD // 2, 1)
        )
        parts.append(part * cosine + other * sine)
    return jnp.concatenate(parts, axis=1)


def rotary_tables(first, count):
    positions = np.arange(first, first + count, dtype=np.float32)
    half = HEAD // 2
    freqs = np.float32(BASE) ** (-(np.arange(half, dtype=np.float32) * np.float32(2.0 / HEAD)))
    angles = (positions[:, None] * freqs[None, :].astype(np.float32)).astype(np.float64)
    cosine, sine = (np.cos(angles), np.sin(angles))
    return (
        np.concatenate([cosine] * 4, axis=1).astype(np.float32),
        np.concatenate([-sine, sine] * 2, axis=1).astype(np.float32),
    )


def own_kernel(
    x_ref, gain_ref, wq_ref, wk_ref, wv_ref, cos_ref, sin_ref,
    nt_ref, q_ref, qt_ref, k_ref, kt_ref, v_ref, vt_ref,
):
    unit, _ = normalised(x_ref[...].astype(F32))
    low = (unit * gain_ref[...]).astype(BF16)
    nt_ref[...] = jnp.transpose(low)
    block = low.shape[0]
    cosine, sine = cos_ref[block:], sin_ref[block:]
    scale = 1.0 / math.sqrt(HEAD)
    query = turned(dot(low, wq_ref[...]), cosine, sine).astype(BF16).astype(F32) * scale
    query = query.astype(BF16)
    q_ref[...] = query
    qt_ref[...] = jnp.transpose(query)
    key = turned(dot(low, wk_ref[...]), cosine, sine).astype(BF16)
    k_ref[...] = key
    kt_ref[...] = jnp.transpose(key)
    value = dot(low, wv_ref[...]).astype(BF16)
    v_ref[...] = value
    vt_ref[...] = jnp.transpose(value)


def before_diagonal():
    key = lax.broadcasted_iota(jnp.int32, (TILE, TILE), 0)
    return key <= lax.broadcasted_iota(jnp.int32, (TILE, TILE), 1)


def halves(array, seen):
    none = jnp.zeros_like(array)
    return jnp.where(seen, none, array), jnp.where(seen, array, none)


def attend(q_t, keys, values_t, w_ref, mix_ref):
    seen = before_diagonal()
    pairs = mix_ref.shape[0] // PAIR

    def one_pair(pair, carry):
        lanes = pl.ds(pl.multiple_of(pair * PAIR, PAIR), PAIR)
        both = q_t(lanes)
        row = lax.broadcasted_iota(jnp.int32, both.shape, 0)
        for head in range(2):
            query = jnp.where(row // HEAD == head, both, jnp.zeros_like(both))
            first, middle, last = [dot(block(lanes), query) for block in keys]
            edge = jnp.where(seen, last, first)
            peak = jnp.maximum(
                jnp.max(edge, axis=0, keepdims=True), jnp.max(middle, axis=0, keepdims=True)
            )
            edge, middle = jnp.exp(edge - peak), jnp.exp(middle - peak)
            total = jnp.sum(edge + middle, axis=0, keepdims=True)
            edge, middle = (edge / total).astype(BF16), (middle / total).astype(BF16)
            w_ref[2 * pair + head, :TILE] = edge
            w_ref[2 * pair + head, TILE:] = middle
            own = pl.ds(pl.multiple_of(pair * PAIR + head * HEAD, HEAD), HEAD)
            left, right = halves(edge, seen)
            mix = dot(values_t[0](own), left) + dot(values_t[1](own), middle)
            mix_ref[own] = (mix + dot(values_t[2](own), right)).astype(BF16)
        return carry

    lax.fori_loop(0, pairs, one_pair, 0, unroll=pairs)


def side_rows(memory_ref, received_ref):
    return jnp.where(lax.axis_index("seq") == 0, memory_ref[...], received_ref[...]).astype(F32)


def side_part(memory_ref, received_ref, gain_ref, wk_ref, wv_ref, cos_ref, sin_ref, sn_ref, k_ref, v_ref, vt_ref):
    unit, _ = normalised(side_rows(memory_ref, received_ref))
    low = (unit * gain_ref[...]).astype(BF16)
    sn_ref[...] = low
    key = turned(dot(low, wk_ref[...]), cos_ref[...], sin_ref[...]).astype(BF16)
    k_ref[...] = key
    value = dot(low, wv_ref[...]).astype(BF16)
    v_ref[...] = value
    vt_ref[...] = jnp.transpose(value)


def late_kernel(
    memory_ref, received_ref, gain_ref, wk_ref, wv_ref, cos_ref, sin_ref, qt_ref, ok_ref, ovt_ref,
    sn_ref, k_ref, v_ref, vt_ref, w_ref, mix_ref,
):
    side_part(
        memory_ref.at[TILE:], received_ref, gain_ref, wk_ref, wv_ref, cos_ref.at[TILE : 2 * TILE], sin_ref.at[TILE : 2 * TILE],
        sn_ref, k_ref, v_ref, vt_ref,
    )
    attend(
        lambda at: qt_ref[at, TILE:],
        (lambda at: k_ref[:, at], lambda at: ok_ref[:TILE, at], lambda at: ok_ref[TILE:, at]),
        (lambda at: vt_ref[at], lambda at: ovt_ref[at, :TILE], lambda at: ovt_ref[at, TILE:]),
        w_ref,
        mix_ref,
    )


def early_kernel(
    memory_ref, received_ref, gain_ref, wk_ref, wv_ref, cos_ref, sin_ref, qt_ref, ok_ref, ovt_ref, sk_ref, svt_ref,
    sn_ref, k_ref, v_ref, vt_ref, w_ref, mix_ref,
):
    side_part(
        memory_ref.at[:TILE], received_ref, gain_ref, wk_ref, wv_ref, cos_ref.at[:TILE], sin_ref.at[:TILE],
        sn_ref, k_ref, v_ref, vt_ref,
    )
    attend(
        lambda at: qt_ref[at, :TILE],
        (lambda at: k_ref[:, at], lambda at: sk_ref[:, at], lambda at: ok_ref[:TILE, at]),
        (lambda at: vt_ref[at], lambda at: svt_ref[at], lambda at: ovt_ref[at, :TILE]),
        w_ref,
        mix_ref,
    )


def forward_kernel(
    x_ref, mix0_ref, mix1_ref, wo_ref, fgain_ref, up_ref, down_ref, bh_ref, bo_ref, labels_ref,
    hidden_ref, nh_ref, gated_ref, slope_ref, out_ref, pg_ref, sent_ref, kept_ref, probe_ref, signal_ref,
    pslope_ref, turn_ref,
):
    block, width = x_ref.shape
    mixed = jnp.concatenate([jnp.transpose(mix0_ref[...]), jnp.transpose(mix1_ref[...])], axis=0)
    hidden = x_ref[...].astype(F32) + dot(mixed, wo_ref[...])
    hidden_ref[...] = hidden
    unit, _ = normalised(hidden)
    low = (unit * fgain_ref[...]).astype(BF16)
    nh_ref[...] = low
    step = 1024

    def feed_forward(tile, carry):
        rows = pl.ds(pl.multiple_of(tile * TILE, TILE), TILE)
        low, final = nh_ref[rows], hidden_ref[rows]
        for at in range(0, up_ref.shape[1], step):
            gated, slope = gelu_both(dot(low, up_ref[:, at : at + step]))
            gated = gated.astype(BF16)
            gated_ref[rows, at : at + step] = gated
            slope_ref[rows, at : at + step] = slope.astype(BF16)
            final = final + dot(gated, down_ref[at : at + step])
        out = final.astype(BF16)
        out_ref[rows] = out
        logit = jnp.zeros((TILE, 1), F32)
        for at in range(0, bh_ref.shape[1], step):
            probe, slope = gelu_both(dot(out, bh_ref[:, at : at + step]))
            probe = probe.astype(BF16)
            probe_ref[rows, at : at + step] = probe
            pslope_ref[rows, at : at + step] = slope.astype(BF16)
            logit = logit + jnp.sum(
                probe.astype(F32) * bo_ref[:, at : at + step].astype(F32), axis=-1, keepdims=True
            )
        signal_ref[rows] = jnp.broadcast_to(logit, (TILE, PAIR))
        return carry

    lax.fori_loop(0, block // TILE, feed_forward, 0)
    turn_ref[...] = jnp.transpose(out_ref[...])
    logits = signal_ref[:, :1]
    targets = jnp.transpose(jnp.broadcast_to(labels_ref[...].astype(F32), (PAIR, block)))[:, :1]
    signal = (jax.nn.sigmoid(logits) - targets).astype(BF16).astype(F32)
    step = 512
    half = bh_ref.shape[1] // 2
    core = lax.axis_index("batch") & 1
    for at in range(0, bh_ref.shape[1], step):
        grad = pslope_ref[:, at : at + step].astype(F32) * (
            signal * bo_ref[:, at : at + step].astype(F32)
        )
        pg_ref[:, at : at + step] = grad.astype(BF16)
    for place, ref in ((1 - core, sent_ref), (core, kept_ref)):
        for at in range(0, half, step):
            grad = pg_ref[:, pl.ds(pl.multiple_of(place * half + at, step), step)]
            ref[at * width // step : (at + step) * width // step] = dot(turn_ref[...], grad).astype(BF16)
    signal_ref[...] = jnp.broadcast_to(signal, signal_ref.shape)


def down_kernel(
    pg_ref, bh_ref, cot_ref, gated_ref, slope_ref, down_ref, probe_ref, signal_ref, sn0_ref, sn1_ref, sk0_ref, sk1_ref,
    grad_ref, upg_ref, sent_ref, kept_ref, bog_ref, snt0_ref, snt1_ref, skt0_ref, skt1_ref,
):
    final = cot_ref[...].astype(F32) + dot_t(pg_ref[...], bh_ref[...])
    grad_ref[...] = final
    low = final.astype(BF16)
    step = 512
    half = down_ref.shape[0] // 2
    core = lax.axis_index("batch") & 1
    for at in range(0, half, step):
        rows = pl.ds(pl.multiple_of((1 - core) * half + at, step), step)
        sent_ref[at : at + step] = t_dot(gated_ref[:, rows], low).astype(BF16)
    for at in range(0, half, step):
        rows = pl.ds(pl.multiple_of(core * half + at, step), step)
        kept_ref[at : at + step] = t_dot(gated_ref[:, rows], low).astype(BF16)
    for at in range(0, down_ref.shape[0], step):
        part = slope_ref[:, at : at + step].astype(F32) * dot_t(low, down_ref[at : at + step])
        upg_ref[:, at : at + step] = part.astype(BF16)
    signal = signal_ref[:, :1]
    for at in range(0, bog_ref.shape[1], step):
        bog_ref[:, at : at + step] = jnp.sum(
            signal * probe_ref[:, at : at + step].astype(F32), axis=0, keepdims=True
        )
    for ref, turned_ref in (
        (sn0_ref, snt0_ref), (sn1_ref, snt1_ref), (sk0_ref, skt0_ref), (sk1_ref, skt1_ref)
    ):
        turned_ref[...] = jnp.transpose(ref[...])


def up_kernel(
    nh_ref, upg_ref, up_ref, hidden_ref, fgain_ref, grad_ref, mix0_ref, mix1_ref, wo_ref,
    hg_ref, mg_ref, mgt_ref, fgg_ref, sent_ref, kept_ref, nht_ref, mixt_ref,
):
    width, wide = up_ref.shape
    nht_ref[...] = jnp.transpose(nh_ref[...])
    mixt_ref[:, :TILE] = mix0_ref[...]
    mixt_ref[:, TILE:] = mix1_ref[...]
    upstream = dot_t(upg_ref[...], up_ref[...])
    unit, scale = normalised(hidden_ref[...])
    part, gain_part = norm_back(unit, scale, fgain_ref[...], upstream)
    fgg_ref[...] = gain_part
    total = grad_ref[...] + part
    hg_ref[...] = total
    low = total.astype(BF16)
    mixed_grad = dot_t(low, wo_ref[...]).astype(BF16)
    mg_ref[...] = mixed_grad
    mgt_ref[...] = jnp.transpose(mixed_grad)
    core = lax.axis_index("batch") & 1
    half, step = wide // 2, 512
    for place, ref in ((1 - core, sent_ref), (core, kept_ref)):
        for at in range(0, half, step):
            grad = upg_ref[:, pl.ds(pl.multiple_of(place * half + at, step), step)]
            ref[at * width // step : (at + step) * width // step] = dot(nht_ref[...], grad).astype(BF16)
        rows = pl.ds(pl.multiple_of(place * (width // 2), width // 2), width // 2)
        ref[half * width // step :] = dot(mixt_ref[rows], low).astype(BF16)


def attend_back(start, pair, tile, w_ref, mg_ref, mgt_ref, q_ref, values, keys_t, dq_ref, dks, dvs):
    seen = before_diagonal()
    lanes = pl.ds(pl.multiple_of((start + pair) * PAIR, PAIR), PAIR)
    rows = slice(tile * TILE, (tile + 1) * TILE)
    upstream_t, upstream, query = mgt_ref[lanes, rows], mg_ref[rows, lanes], q_ref[rows, lanes]
    row = lax.broadcasted_iota(jnp.int32, (PAIR, TILE), 0)
    lane = lax.broadcasted_iota(jnp.int32, (TILE, PAIR), 1)
    none, none_t = jnp.zeros_like(upstream), jnp.zeros_like(upstream_t)
    for head in range(2):
        above_t = jnp.where(row // HEAD == head, upstream_t, none_t)
        first, middle_grad, last = [dot(block[:, lanes], above_t) for block in values]
        edge_grad = jnp.where(seen, last, first)
        weights = w_ref[2 * (start + pair) + head]
        edge, middle = weights[:TILE].astype(F32), weights[TILE:].astype(F32)
        centred = jnp.sum(edge * edge_grad + middle * middle_grad, axis=0, keepdims=True)
        edge = (edge * (edge_grad - centred)).astype(BF16)
        middle = (middle * (middle_grad - centred)).astype(BF16)
        left, right = halves(edge, seen)
        above = jnp.where(lane // HEAD == head, upstream, none)
        one = jnp.where(lane // HEAD == head, query, none)
        own = pl.ds(pl.multiple_of((start + pair) * PAIR + head * HEAD, HEAD), HEAD)
        grad = dot(keys_t[0][own], left) + dot(keys_t[1][own], middle) + dot(keys_t[2][own], right)
        dq_ref[pl.ds(pl.multiple_of(pair * PAIR + head * HEAD, HEAD), HEAD), rows] = grad
        w_left, w_right = halves(weights[:TILE], seen)
        for place, part in enumerate((left, middle, right)):
            dks[place] = dks[place] + dot(part, one)
        for place, part in enumerate((w_left, weights[TILE:], w_right)):
            dvs[place] = dvs[place] + dot(part, above)


def rows_of(*smalls):
    rows = [s[:, at : at + TILE] for s in smalls for at in range(0, s.shape[1], TILE)]
    rows.append(jnp.zeros((128 - len(rows), TILE), F32))
    return jnp.concatenate(rows, axis=0).astype(BF16)


def attention_kernel(
    part, final, w0_ref, w1_ref, mg_ref, mgt_ref, q_ref, sv0_ref, sv1_ref, v_ref, skt0_ref, skt1_ref, kt_ref,
    cos_ref, sin_ref, nt_ref, snt0_ref, snt1_ref, wq_ref, wk_ref, wv_ref, *rest,
):
    if final:
        x_ref, memory_ref, side0_ref, side1_ref, gain_ref, hg_ref, up_ref, sup_ref, ig_ref, sg_ref, grads_ref, dq_ref, dk_ref, dv_ref = rest
    else:
        bog_ref, fgg_ref, nup_ref, nsup_ref, grads_ref, dq_ref, dk_ref, dv_ref = rest
    block, width = q_ref.shape
    pairs = width // PAIR // 2
    values = (sv0_ref, sv1_ref, v_ref.at[:TILE], v_ref.at[TILE:])
    keys_t = (skt0_ref, skt1_ref, kt_ref.at[:, :TILE], kt_ref.at[:, TILE:])

    def one_pair(pair, carry):
        dk, dv = [0.0] * 4, [0.0] * 4
        for tile, w_ref in ((1, w1_ref), (0, w0_ref)):
            dks, dvs = dk[tile : tile + 3], dv[tile : tile + 3]
            attend_back(
                part * pairs, pair, tile, w_ref, mg_ref, mgt_ref, q_ref, values[tile : tile + 3],
                keys_t[tile : tile + 3], dq_ref, dks, dvs,
            )
            dk[tile : tile + 3], dv[tile : tile + 3] = dks, dvs
        inside = pl.ds(pl.multiple_of(pair * PAIR, PAIR), PAIR)
        for place in range(4):
            dk_ref[place * TILE : (place + 1) * TILE, inside] = dk[place]
            dv_ref[place * TILE : (place + 1) * TILE, inside] = dv[place].astype(BF16)
        return carry

    lax.fori_loop(0, pairs, one_pair, 0)
    dk = [dk_ref[place * TILE : (place + 1) * TILE] for place in range(4)]
    dv = [dv_ref[place * TILE : (place + 1) * TILE] for place in range(4)]
    lanes = slice(part * (width // 2), (part + 1) * (width // 2))
    scale = 1.0 / math.sqrt(HEAD)
    cosine, sine = cos_ref[...], -sin_ref[...]
    dq = turned(jnp.transpose(dq_ref[...]) * scale, cosine[block:], sine[block:]).astype(BF16)
    dk = [
        turned(p, cosine[i * TILE : (i + 1) * TILE], sine[i * TILE : (i + 1) * TILE]).astype(BF16)
        for i, p in enumerate(dk)
    ]
    own_k, own_v = jnp.concatenate(dk[2:], axis=0), jnp.concatenate(dv[2:], axis=0)
    side_k, side_v = jnp.concatenate(dk[:2], axis=0), jnp.concatenate(dv[:2], axis=0)
    rows_t = nt_ref[...]
    side_t = jnp.concatenate([snt0_ref[...], snt1_ref[...]], axis=1)
    grads_ref[:width] = dot(rows_t, dq).astype(BF16)
    grads_ref[width : 2 * width] = (dot(rows_t, own_k) + dot(side_t, side_k)).astype(BF16)
    grads_ref[2 * width : 3 * width] = (dot(rows_t, own_v) + dot(side_t, side_v)).astype(BF16)
    wk, wv = wk_ref[:, lanes], wv_ref[:, lanes]
    upstream = dot_t(dq, wq_ref[:, lanes]) + dot_t(own_k, wk) + dot_t(own_v, wv)
    side_up = dot_t(side_k, wk) + dot_t(side_v, wv)
    if not final:
        grads_ref[3 * width :] = rows_of(bog_ref[...], fgg_ref[...])
        nup_ref[...] = upstream
        nsup_ref[...] = side_up
        return
    upstream = upstream + up_ref[...]
    side_up = side_up + sup_ref[...]
    unit, spread = normalised(x_ref[...].astype(F32))
    back, gain_part = norm_back(unit, spread, gain_ref[...], upstream)
    ig_ref[...] = hg_ref[...] + back
    for i, ref in enumerate((side0_ref, side1_ref)):
        at = slice(i * TILE, (i + 1) * TILE)
        unit, spread = normalised(side_rows(memory_ref.at[at], ref))
        back, side_gain = norm_back(unit, spread, gain_ref[...], side_up[at])
        sg_ref[at] = back.astype(BF16)
        gain_part = gain_part + side_gain
    grads_ref[3 * width :] = rows_of(gain_part)


def places(own_ref, other_ref):
    core = lax.axis_index("batch") & 1
    return ((core, own_ref), (1 - core, other_ref))


def tall_final(own_ref, other_ref, out_ref, work_ref, sems):
    half = own_ref.shape[0]
    copies = []
    for number, (place, ref) in enumerate(places(own_ref, other_ref)):
        for at in range(0, half, half // 2):
            rows = pl.ds(pl.multiple_of(place * half + at, half // 2), half // 2)
            work_ref[rows] = ref[at : at + half // 2].astype(F32)
            copies.append(pltpu.make_async_copy(work_ref.at[rows], out_ref.at[rows], sems.at[len(copies)]))
            copies[-1].start()
    for copy in copies:
        copy.wait()


def wide_final(own_ref, other_ref, out_ref, *more):
    work_ref, sems = more[-2:]
    width, wide = out_ref.shape
    step = own_ref.shape[1]
    copies = []
    for place, ref in places(own_ref, other_ref):
        for at in range(wide // 2 // step):
            lanes = pl.ds(pl.multiple_of(place * (wide // 2) + at * step, step), step)
            work_ref[:, lanes] = ref[at * width : (at + 1) * width].astype(F32)
            copies.append(pltpu.make_async_copy(work_ref.at[:, lanes], out_ref.at[:, lanes], sems.at[len(copies)]))
            copies[-1].start()
        if len(more) > 2:
            half = width // 2
            more[1][pl.ds(pl.multiple_of(place * half, half), half)] = ref[wide // 2 // step * width :].astype(F32)
    if len(more) > 2:
        copies.append(pltpu.make_async_copy(more[1], more[0], sems.at[len(copies)]))
        copies[-1].start()
    for copy in copies:
        copy.wait()


def rest_final(own_ref, other_ref, q_ref, k_ref, v_ref, bog_ref, fgg_ref, gg_ref):
    width = q_ref.shape[0]
    half = width // 2
    for place, ref in places(own_ref, other_ref):
        lanes = pl.ds(pl.multiple_of(place * half, half), half)
        for at, out in enumerate((q_ref, k_ref, v_ref)):
            out[:, lanes] = ref[at * width : (at + 1) * width].astype(F32)
    own, other = (ref[3 * width : 3 * width + 16].astype(F32) for ref in (own_ref, other_ref))
    core = lax.axis_index("batch") & 1
    zero, one = jnp.where(core == 0, own, other), jnp.where(core == 0, other, own)
    count = bog_ref.shape[0] // half
    for out, rows, first in ((bog_ref, zero, 0), (fgg_ref, zero, count), (gg_ref, one, 0)):
        for at in range(out.shape[0] // half):
            out[at * half : (at + 1) * half] = rows[first + at]


def add_back_kernel(part_ref, returned_ref, out_ref):
    out_ref[...] = part_ref[...] + returned_ref[...].astype(F32)


def call(kernel, operands, results, scratch=(), limit=6, outside=0):
    nbytes = sum(a.size * a.dtype.itemsize for a in operands) + sum(
        math.prod(s) * jnp.dtype(d).itemsize for s, d in results
    )
    return pl.pallas_call(
        kernel,
        out_shape=tuple(jax.ShapeDtypeStruct(s, d) for s, d in results),
        in_specs=[VMEM] * len(operands),
        out_specs=tuple(HBM if i < outside else VMEM for i in range(len(results))),
        scratch_shapes=list(scratch),
        compiler_params=pltpu.CompilerParams(vmem_limit_bytes=limit * MEGA),
        cost_estimate=pl.CostEstimate(flops=STEP_FLOPS, bytes_accessed=nbytes, transcendentals=0),
    )(*operands)


def exchanges(batches, blocks):
    number = batches * blocks

    def pairs(partner):
        return [
            (d, p[0] * blocks + p[1])
            for d in range(number)
            for p in [partner(d // blocks, d % blocks)]
        ]

    flips = {
        "x": (lambda b, s: (b, s ^ 1), lambda b, s: s),
        "y": (lambda b, s: (b ^ 2, s), lambda b, s: (b & 2) // 2),
        "z": (lambda b, s: (b ^ 4, s), lambda b, s: (b & 4) // 4),
    }

    def flip(place):
        return (pairs(lambda b, s: (b ^ place, s)), lambda b, s: (b & place) // place)

    def mixed(way):
        (first, first_bit), (second, second_bit) = (flips[axis] for axis in way)
        return (
            pairs(lambda b, s: second(b, s) if b % 2 else first(b, s)),
            lambda b, s: jnp.where(b & 1 == 0, first_bit(b, s), second_bit(b, s)),
        )

    found = {way: mixed(way) for way in ("xy", "yx", "zy", "yz", "xz", "zx", "xx", "yy", "zz")}
    found["core"] = flip(1)
    rest = []
    place = 8
    while place < batches:
        rest.append(flip(place))
        place *= 2
    return found, rest


def added(left, right, rows):
    return (left[rows].astype(F32) + right[rows].astype(F32)).astype(BF16)


def halve_kernel(bit, kept_ref, arrived_ref, sent_ref, left_ref):
    half, mine = sent_ref.shape[0], bit(lax.axis_index("batch"), lax.axis_index("seq"))
    step = 16 * math.gcd(half // 16, 8)
    for place, ref in ((1 - mine, sent_ref), (mine, left_ref)):
        for at in range(0, half, step):
            rows = pl.ds(pl.multiple_of(place * half + at, 16), step)
            ref[at : at + step] = added(kept_ref, arrived_ref, rows)


def add_kernel(kept_ref, arrived_ref, out_ref):
    half = out_ref.shape[0]
    step = 16 * math.gcd(half // 16, 8)
    for at in range(0, half, step):
        out_ref[at : at + step] = added(kept_ref, arrived_ref, slice(at, at + step))


def double_kernel(bit, kept_ref, arrived_ref, out_ref):
    half, mine = kept_ref.shape[0], bit(lax.axis_index("batch"), lax.axis_index("seq"))
    for place, ref in ((mine, kept_ref), (1 - mine, arrived_ref)):
        out_ref[pl.ds(pl.multiple_of(place * half, 16), half)] = ref[...]


def choose_kernel(bit, kept0_ref, arrived0_ref, kept1_ref, arrived1_ref, sent_ref, left_ref):
    mine = bit(lax.axis_index("batch"), lax.axis_index("seq"))
    step = 128
    for at in range(0, sent_ref.shape[0], step):
        rows = slice(at, at + step)
        zero, one = added(kept0_ref, arrived0_ref, rows), added(kept1_ref, arrived1_ref, rows)
        left_ref[rows] = jnp.where(mine == 0, zero, one)
        sent_ref[rows] = jnp.where(mine == 0, one, zero)


def pick_kernel(bit, zero_ref, one_ref, sent_ref, left_ref):
    mine = bit(lax.axis_index("batch"), lax.axis_index("seq"))

    @pl.when(mine == 0)
    def _():
        left_ref[...] = zero_ref[...]
        sent_ref[...] = one_ref[...]

    @pl.when(mine != 0)
    def _():
        left_ref[...] = one_ref[...]
        sent_ref[...] = zero_ref[...]


class Sum:
    def __init__(self, halvings, fulls, sent, kept, finish):
        self.halvings, self.fulls, self.finish = halvings, fulls, finish
        self.sent, self.kept, self.arrived, self.at = sent, kept, None, 0

    def start(self, exchange):
        self.arrived = lax.ppermute(self.sent, AXES, exchange[0])

    def add(self):
        (self.kept,) = call(add_kernel, (self.kept, self.arrived), [(self.kept.shape, BF16)])
        self.sent = self.kept

    def advance(self, *after):
        count, at = len(self.halvings), self.at
        self.at += 1
        if at == 0:
            self.sent = fence(self.sent, *after)[0]
            self.start(self.halvings[0])
            return self.sent
        self.kept = fence(self.kept, *after)[0]
        rows, columns = self.kept.shape
        if at < count:
            self.sent, self.kept = call(
                functools.partial(halve_kernel, self.halvings[at][1]),
                (self.kept, self.arrived),
                [((rows // 2, columns), BF16)] * 2,
            )
            self.start(self.halvings[at])
        elif at == count:
            self.add()
            self.start(self.fulls[0])
        elif at == count + 1:
            for exchange in self.fulls[1:]:
                self.add()
                self.start(exchange)
            self.add()
            self.start(self.halvings[-1])
        elif at <= 2 * count:
            (self.kept,) = call(
                functools.partial(double_kernel, self.halvings[2 * count + 1 - at + 0][1]),
                (self.kept, self.arrived),
                [((rows * 2, columns), BF16)],
            )
            self.sent = self.kept
            self.start(self.halvings[2 * count - at])
        else:
            self.result = self.finish(self.kept, self.arrived)
            return self.result[0]
        return self.sent


def fence(*arrays):
    return lax.optimization_barrier(arrays)


def body(
    inputs,
    memory,
    cotangent,
    labels,
    attention_gain,
    query_weight,
    key_weight,
    value_weight,
    out_weight,
    forward_gain,
    up_weight,
    down_weight,
    boundary_hidden,
    boundary_out,
):
    group, block, width = inputs.shape
    wide, hidden_wide = up_weight.shape[1], boundary_hidden.shape[1]
    batches, blocks = (lax.axis_size("batch"), lax.axis_size("seq"))
    found, fulls = exchanges(batches, blocks)
    column = lax.axis_index("seq")
    core = lax.axis_index("batch") % 2
    rows = inputs.reshape(block, width)
    memory_rows = memory.reshape(block, width)
    onward = [(i, i + 1) for i in range(blocks - 1)]
    side1 = lax.ppermute(rows[TILE:], "seq", onward)
    tables = rotary_tables(-block, (blocks + 1) * block)
    cosine, sine = (
        lax.dynamic_slice_in_dim(jnp.asarray(t), column * block, 2 * block) for t in tables
    )
    gain = attention_gain.reshape(1, width)
    square, side_shape = (block, width), (TILE, width)
    turned_square, turned_side = (width, block), (width, TILE)
    normed_t, queries, queries_t, keys, keys_t, values, values_t = call(
        own_kernel,
        (rows, gain, query_weight, key_weight, value_weight, cosine, sine),
        [(turned_square, BF16), (square, BF16), (turned_square, BF16)]
        + [(square, BF16), (turned_square, BF16)] * 2,
    )
    side0 = lax.ppermute(fence(rows, queries)[0][:TILE], "seq", onward)
    side_results = [
        (side_shape, BF16), (side_shape, BF16), (side_shape, BF16), (turned_side, BF16),
        ((HEADS, 2 * TILE, TILE), BF16), (turned_side, BF16),
    ]
    sn1, sk1, sv1, sv_t1, weights1, mix1 = call(
        late_kernel,
        (memory_rows, side1, gain, key_weight, value_weight, cosine, sine, queries_t, keys, values_t),
        side_results,
    )
    sn0, sk0, sv0, sv_t0, weights0, mix0 = call(
        early_kernel,
        (memory_rows, side0, gain, key_weight, value_weight, cosine, sine, queries_t, keys, values_t, sk1, sv_t1),
        side_results,
    )
    bh_half = (hidden_wide // 2 * width // 512, 512)
    (
        hidden, normed_hidden, gated, slope, outputs, probe_grad, hidden_sent, hidden_kept, probe, signal,
    ) = call(
        forward_kernel,
        (
            rows, mix0, mix1, out_weight, forward_gain.reshape(1, width), up_weight, down_weight,
            boundary_hidden, boundary_out.reshape(1, hidden_wide), labels,
        ),
        [
            (square, F32), (square, BF16), ((block, wide), BF16),
            ((block, wide), BF16), (square, BF16), ((block, hidden_wide), BF16),
            (bh_half, BF16), (bh_half, BF16), ((block, hidden_wide), BF16), ((block, PAIR), F32),
        ],
        [
            pltpu.VMEM((block, hidden_wide), BF16),
            pltpu.VMEM((width, block), BF16),
        ],
        limit=18,
    )
    sums, made = {}, {}

    def add_sum(name, way, sent, kept, finish):
        sums[name] = Sum([found[w] for w in way], fulls, sent, kept, finish)

    add_sum(
        "hidden", ("core", "xy", "yx", "zz"), hidden_sent, hidden_kept,
        lambda own, other: call(
            wide_final, (own, other), [((width, hidden_wide), F32)],
            [pltpu.VMEM((width, hidden_wide), F32), pltpu.SemaphoreType.DMA((4,))], outside=1,
        ),
    )
    up_half = (wide // 2 * width // 512 + width // 2, 512)
    grads_shape = ((3 * width + 128, width // 2), BF16)
    work = [
        pltpu.VMEM((width // 2, block), F32),
        pltpu.VMEM((2 * block, width // 2), F32),
        pltpu.VMEM((2 * block, width // 2), BF16),
    ]
    def down_part(*after):
        grad = fence(probe_grad, *after)[0]
        final_grad, up_grad, sent, kept, boundary_out_grad, sn_t0, sn_t1, sk_t0, sk_t1 = call(
            down_kernel,
            (
                grad, boundary_hidden, cotangent.reshape(square), gated, slope, down_weight, probe, signal,
                sn0, sn1, sk0, sk1,
            ),
            [(square, F32), ((block, wide), BF16), ((wide // 2, width), BF16), ((wide // 2, width), BF16)]
            + [((1, hidden_wide), F32)] + [(turned_side, BF16)] * 4,
        )
        made["down"] = (final_grad, up_grad, boundary_out_grad)
        made["shared"] = (
            queries, sv0, sv1, values, sk_t0, sk_t1, keys_t,
            cosine, sine, normed_t, sn_t0, sn_t1, query_weight, key_weight, value_weight,
        )
        add_sum(
            "down", ("core", "xy", "yx", "zz"), sent, kept,
            lambda own, other: call(
                tall_final, (own, other), [((wide, width), F32)],
                [pltpu.VMEM((wide, width), F32), pltpu.SemaphoreType.DMA((4,))], outside=1,
            ),
        )
        return up_grad

    def up_part(*after):
        final_grad, up_grad, _ = made["down"]
        up_grad = fence(up_grad, *after)[0]
        hidden_grad, mixed_grad, mixed_grad_t, gain_part, sent, kept = call(
            up_kernel,
            (
                normed_hidden, up_grad, up_weight, hidden, forward_gain.reshape(1, width), final_grad,
                mix0, mix1, out_weight,
            ),
            [
                (square, F32), (square, BF16), (turned_square, BF16), ((1, width), F32),
                (up_half, BF16), (up_half, BF16),
            ],
            [pltpu.VMEM((width, block), BF16), pltpu.VMEM((width, block), BF16)],
        )
        made["up"] = (hidden_grad, (weights0, weights1, mixed_grad, mixed_grad_t) + made["shared"], gain_part)
        add_sum(
            "up", ("core", "xy", "yx", "zz"), sent, kept,
            lambda own, other: call(
                wide_final, (own, other), [((width, wide), F32), ((width, width), F32)],
                [pltpu.VMEM((width, width), F32), pltpu.VMEM((width, wide), F32), pltpu.SemaphoreType.DMA((5,))],
                outside=2,
            ),
        )
        return mixed_grad

    def attention0(*after):
        hidden_grad, operands, gain_part = made["up"]
        operands = (fence(weights0, *after)[0],) + operands[1:]
        made["attention"] = call(
            functools.partial(attention_kernel, 0, False),
            operands + (made["down"][2], gain_part),
            [(square, F32), (square, F32), grads_shape],
            work,
            limit=10,
        )
        return made["attention"][0]

    def attention1(*after):
        hidden_grad, operands, _ = made["up"]
        upstream, side_upstream, grads0 = made["attention"]
        upstream = fence(upstream, *after)[0]
        input_part, side_grad, grads1 = call(
            functools.partial(attention_kernel, 1, True),
            operands + (rows, memory_rows, side0, side1, gain, hidden_grad, upstream, side_upstream),
            [(square, F32), (square, BF16), grads_shape],
            work,
            limit=10,
        )
        made["input"] = (input_part, side_grad)
        picked = call(
            functools.partial(pick_kernel, found["core"][1]), (grads0, grads1), [grads_shape] * 2
        )
        add_sum(
            "rest", ("core", "xy", "yx", "zz"), *picked,
            lambda own, other: call(
                rest_final, (own, other), [((width, width), F32)] * 3 + [((hidden_wide,), F32), ((width,), F32), ((width,), F32)],
            ),
        )
        return picked[0]

    def send_back(*after):
        input_part, side_grad = made["input"]
        side_grad = fence(side_grad, *after)[0]
        made["returned"] = lax.ppermute(side_grad, "seq", [(i + 1, i) for i in range(blocks - 1)])
        return side_grad

    def add_back(*after):
        input_part = fence(made["input"][0], *after)[0]
        (made["input_grad"],) = call(add_back_kernel, (input_part, made["returned"]), [(square, F32)])
        return made["input_grad"]

    parts = {
        "a": down_part, "b": up_part, "c": attention0, "d": attention1, "r": send_back, "s": add_back,
    }
    names = {"H": "hidden", "D": "down", "U": "up", "T": "rest"}
    token = hidden_kept
    for letter in ORDER:
        token = parts[letter](token) if letter in parts else sums[names[letter]].advance(token)
    (hidden_total,), (down_total,) = (sums["hidden"].result, sums["down"].result)
    up_total, out_total = sums["up"].result
    query_total, key_total, value_total, boundary_out_total, forward_gain_total, gain_total = sums["rest"].result
    input_grad = made["input_grad"]
    return (
        outputs.reshape(inputs.shape),
        input_grad.reshape(inputs.shape),
        gain_total,
        query_total,
        key_total,
        value_total,
        out_total,
        forward_gain_total,
        up_total,
        down_total,
        hidden_total,
        boundary_out_total,
    )


def solution(mesh):
    placed = (
        P("batch", "seq", None),
        P("batch", None, None),
        P("batch", "seq", None),
        P("batch", "seq"),
        P(),
        P(),
        P(),
        P(),
        P(),
        P(),
        P(),
        P(),
        P(),
        P(),
    )
    return jax.shard_map(
        body,
        mesh=mesh,
        in_specs=placed,
        out_specs=(
            P("batch", "seq", None),
            P("batch", "seq", None),
            P(),
            P(),
            P(),
            P(),
            P(),
            P(),
            P(),
            P(),
            P(),
            P(),
        ),
        check_vma=False,
    )
```

```python
import functools
import math

import jax
import jax.numpy as jnp
import numpy as np
from jax import lax
from jax.experimental import pallas as pl
from jax.experimental.pallas import tpu as pltpu
from jax.sharding import PartitionSpec as P

HEADS = 8
HEAD = 64
PAIR = 2 * HEAD
TILE = 256
EPS = 1e-05
BASE = 10000.0
AXES = ("batch", "seq")
F32, BF16 = jnp.float32, jnp.bfloat16
VMEM = pl.BlockSpec(memory_space=pltpu.VMEM)
HBM = pl.BlockSpec(memory_space=pl.ANY)
STEP_FLOPS = int(2e10)
MEGA = 1024 * 1024
ORDER = "HaDHbDUcHUDdTHUDTHrDUTHDUsHTDHTUDHTUHDTUDTUTUT"


def dot(left, right):
    return jnp.dot(left, right, preferred_element_type=F32)


def dot_t(left, right):
    return lax.dot_general(left, right, (((1,), (1,)), ((), ())), preferred_element_type=F32)


def t_dot(left, right):
    return lax.dot_general(left, right, (((0,), (0,)), ((), ())), preferred_element_type=F32)


def normalised(values):
    centre = values - jnp.mean(values, axis=-1, keepdims=True)
    spread = jnp.mean(centre * centre, axis=-1, keepdims=True)
    scale = lax.rsqrt(spread + EPS)
    return centre * scale, scale


def norm_back(unit, scale, gain, upstream):
    product = upstream * unit
    inner = upstream * gain
    mean = jnp.mean(inner, axis=-1, keepdims=True)
    along = jnp.mean(inner * unit, axis=-1, keepdims=True)
    return scale * (inner - mean - unit * along), jnp.sum(product, axis=0, keepdims=True)


def gelu_both(value):
    factor = math.sqrt(2.0 / math.pi)
    square = value * value
    half = 0.5 + 0.5 * jnp.tanh(value * (factor + (factor * 0.044715) * square))
    result = value * half
    bend = (result - result * half) * (2.0 * factor + (6.0 * factor * 0.044715) * square)
    return result, half + bend


def turned(values, cosine, sine):
    front = lax.broadcasted_iota(jnp.int32, (values.shape[0], PAIR), 1) % HEAD < HEAD // 2
    parts = []
    for at in range(0, values.shape[1], PAIR):
        part = values[:, at : at + PAIR]
        other = jnp.where(
            front, pltpu.roll(part, PAIR - HEAD // 2, 1), pltpu.roll(part, HEAD // 2, 1)
        )
        parts.append(part * cosine + other * sine)
    return jnp.concatenate(parts, axis=1)


def rotary_tables(first, count):
    positions = np.arange(first, first + count, dtype=np.float32)
    half = HEAD // 2
    freqs = np.float32(BASE) ** (-(np.arange(half, dtype=np.float32) * np.float32(2.0 / HEAD)))
    angles = (positions[:, None] * freqs[None, :].astype(np.float32)).astype(np.float64)
    cosine, sine = (np.cos(angles), np.sin(angles))
    return (
        np.concatenate([cosine] * 4, axis=1).astype(np.float32),
        np.concatenate([-sine, sine] * 2, axis=1).astype(np.float32),
    )


def own_kernel(
    x_ref, gain_ref, wq_ref, wk_ref, wv_ref, cos_ref, sin_ref,
    nt_ref, q_ref, qt_ref, k_ref, kt_ref, v_ref, vt_ref,
):
    unit, _ = normalised(x_ref[...].astype(F32))
    low = (unit * gain_ref[...]).astype(BF16)
    nt_ref[...] = jnp.transpose(low)
    block = low.shape[0]
    cosine, sine = cos_ref[block:], sin_ref[block:]
    scale = 1.0 / math.sqrt(HEAD)
    query = turned(dot(low, wq_ref[...]), cosine, sine).astype(BF16).astype(F32) * scale
    query = query.astype(BF16)
    q_ref[...] = query
    qt_ref[...] = jnp.transpose(query)
    key = turned(dot(low, wk_ref[...]), cosine, sine).astype(BF16)
    k_ref[...] = key
    kt_ref[...] = jnp.transpose(key)
    value = dot(low, wv_ref[...]).astype(BF16)
    v_ref[...] = value
    vt_ref[...] = jnp.transpose(value)


def before_diagonal():
    key = lax.broadcasted_iota(jnp.int32, (TILE, TILE), 0)
    return key <= lax.broadcasted_iota(jnp.int32, (TILE, TILE), 1)


def halves(array, seen):
    none = jnp.zeros_like(array)
    return jnp.where(seen, none, array), jnp.where(seen, array, none)


def attend(q_t, keys, values_t, w_ref, mix_ref):
    seen = before_diagonal()
    pairs = mix_ref.shape[0] // PAIR

    def one_pair(pair, carry):
        lanes = pl.ds(pl.multiple_of(pair * PAIR, PAIR), PAIR)
        both = q_t(lanes)
        row = lax.broadcasted_iota(jnp.int32, both.shape, 0)
        for head in range(2):
            query = jnp.where(row // HEAD == head, both, jnp.zeros_like(both))
            first, middle, last = [dot(block(lanes), query) for block in keys]
            edge = jnp.where(seen, last, first)
            peak = jnp.maximum(
                jnp.max(edge, axis=0, keepdims=True), jnp.max(middle, axis=0, keepdims=True)
            )
            edge, middle = jnp.exp(edge - peak), jnp.exp(middle - peak)
            total = jnp.sum(edge + middle, axis=0, keepdims=True)
            edge, middle = (edge / total).astype(BF16), (middle / total).astype(BF16)
            w_ref[2 * pair + head, :TILE] = edge
            w_ref[2 * pair + head, TILE:] = middle
            own = pl.ds(pl.multiple_of(pair * PAIR + head * HEAD, HEAD), HEAD)
            left, right = halves(edge, seen)
            mix = dot(values_t[0](own), left) + dot(values_t[1](own), middle)
            mix_ref[own] = (mix + dot(values_t[2](own), right)).astype(BF16)
        return carry

    lax.fori_loop(0, pairs, one_pair, 0, unroll=pairs)


def side_rows(memory_ref, received_ref):
    return jnp.where(lax.axis_index("seq") == 0, memory_ref[...], received_ref[...]).astype(F32)


def side_part(memory_ref, received_ref, gain_ref, wk_ref, wv_ref, cos_ref, sin_ref, sn_ref, k_ref, v_ref, vt_ref):
    unit, _ = normalised(side_rows(memory_ref, received_ref))
    low = (unit * gain_ref[...]).astype(BF16)
    sn_ref[...] = low
    key = turned(dot(low, wk_ref[...]), cos_ref[...], sin_ref[...]).astype(BF16)
    k_ref[...] = key
    value = dot(low, wv_ref[...]).astype(BF16)
    v_ref[...] = value
    vt_ref[...] = jnp.transpose(value)


def late_kernel(
    memory_ref, received_ref, gain_ref, wk_ref, wv_ref, cos_ref, sin_ref, qt_ref, ok_ref, ovt_ref,
    sn_ref, k_ref, v_ref, vt_ref, w_ref, mix_ref,
):
    side_part(
        memory_ref.at[TILE:], received_ref, gain_ref, wk_ref, wv_ref, cos_ref.at[TILE : 2 * TILE], sin_ref.at[TILE : 2 * TILE],
        sn_ref, k_ref, v_ref, vt_ref,
    )
    attend(
        lambda at: qt_ref[at, TILE:],
        (lambda at: k_ref[:, at], lambda at: ok_ref[:TILE, at], lambda at: ok_ref[TILE:, at]),
        (lambda at: vt_ref[at], lambda at: ovt_ref[at, :TILE], lambda at: ovt_ref[at, TILE:]),
        w_ref,
        mix_ref,
    )


def early_kernel(
    memory_ref, received_ref, gain_ref, wk_ref, wv_ref, cos_ref, sin_ref, qt_ref, ok_ref, ovt_ref, sk_ref, svt_ref,
    sn_ref, k_ref, v_ref, vt_ref, w_ref, mix_ref,
):
    side_part(
        memory_ref.at[:TILE], received_ref, gain_ref, wk_ref, wv_ref, cos_ref.at[:TILE], sin_ref.at[:TILE],
        sn_ref, k_ref, v_ref, vt_ref,
    )
    attend(
        lambda at: qt_ref[at, :TILE],
        (lambda at: k_ref[:, at], lambda at: sk_ref[:, at], lambda at: ok_ref[:TILE, at]),
        (lambda at: vt_ref[at], lambda at: svt_ref[at], lambda at: ovt_ref[at, :TILE]),
        w_ref,
        mix_ref,
    )


def forward_kernel(
    x_ref, mix0_ref, mix1_ref, wo_ref, fgain_ref, up_ref, down_ref, bh_ref, bo_ref, labels_ref,
    hidden_ref, nh_ref, gated_ref, slope_ref, out_ref, pg_ref, sent_ref, kept_ref, probe_ref, signal_ref,
    pslope_ref, turn_ref,
):
    block, width = x_ref.shape
    mixed = jnp.concatenate([jnp.transpose(mix0_ref[...]), jnp.transpose(mix1_ref[...])], axis=0)
    hidden = x_ref[...].astype(F32) + dot(mixed, wo_ref[...])
    hidden_ref[...] = hidden
    unit, _ = normalised(hidden)
    low = (unit * fgain_ref[...]).astype(BF16)
    nh_ref[...] = low
    step = 1024
    tops = [slice(top, top + TILE) for top in range(0, block, TILE)]
    for part_rows in tops:
        part = hidden[part_rows]
        for at in range(0, up_ref.shape[1], step):
            gated, slope = gelu_both(dot(low[part_rows], up_ref[:, at : at + step]))
            gated = gated.astype(BF16)
            gated_ref[part_rows, at : at + step] = gated
            slope_ref[part_rows, at : at + step] = slope.astype(BF16)
            part = part + dot(gated, down_ref[at : at + step])
        out_ref[part_rows] = part.astype(BF16)
    out = out_ref[...]
    turn_ref[...] = jnp.transpose(out)
    logits = []
    for part_rows in tops:
        logit = jnp.zeros((TILE, 1), F32)
        for at in range(0, bh_ref.shape[1], step):
            probe, slope = gelu_both(dot(out[part_rows], bh_ref[:, at : at + step]))
            probe = probe.astype(BF16)
            probe_ref[part_rows, at : at + step] = probe
            pslope_ref[part_rows, at : at + step] = slope.astype(BF16)
            logit = logit + jnp.sum(
                probe.astype(F32) * bo_ref[:, at : at + step].astype(F32), axis=-1, keepdims=True
            )
        logits.append(logit)
    logits = jnp.concatenate(logits, axis=0)
    targets = jnp.transpose(jnp.broadcast_to(labels_ref[...].astype(F32), (PAIR, block)))[:, :1]
    signal = (jax.nn.sigmoid(logits) - targets).astype(BF16).astype(F32)
    step = 512
    half = bh_ref.shape[1] // 2
    core = lax.axis_index("batch") & 1
    for at in range(0, bh_ref.shape[1], step):
        grad = pslope_ref[:, at : at + step].astype(F32) * (
            signal * bo_ref[:, at : at + step].astype(F32)
        )
        pg_ref[:, at : at + step] = grad.astype(BF16)
    for place, ref in ((1 - core, sent_ref), (core, kept_ref)):
        for at in range(0, half, step):
            grad = pg_ref[:, pl.ds(pl.multiple_of(place * half + at, step), step)]
            ref[at * width // step : (at + step) * width // step] = dot(turn_ref[...], grad).astype(BF16)
    signal_ref[...] = jnp.broadcast_to(signal, signal_ref.shape)


def down_kernel(
    pg_ref, bh_ref, cot_ref, gated_ref, slope_ref, down_ref, probe_ref, signal_ref, sn0_ref, sn1_ref, sk0_ref, sk1_ref,
    grad_ref, upg_ref, sent_ref, kept_ref, bog_ref, snt0_ref, snt1_ref, skt0_ref, skt1_ref,
):
    final = cot_ref[...].astype(F32) + dot_t(pg_ref[...], bh_ref[...])
    grad_ref[...] = final
    low = final.astype(BF16)
    step = 512
    half = down_ref.shape[0] // 2
    core = lax.axis_index("batch") & 1
    for at in range(0, half, step):
        rows = pl.ds(pl.multiple_of((1 - core) * half + at, step), step)
        sent_ref[at : at + step] = t_dot(gated_ref[:, rows], low).astype(BF16)
    for at in range(0, half, step):
        rows = pl.ds(pl.multiple_of(core * half + at, step), step)
        kept_ref[at : at + step] = t_dot(gated_ref[:, rows], low).astype(BF16)
    for at in range(0, down_ref.shape[0], step):
        part = slope_ref[:, at : at + step].astype(F32) * dot_t(low, down_ref[at : at + step])
        upg_ref[:, at : at + step] = part.astype(BF16)
    signal = signal_ref[:, :1]
    for at in range(0, bog_ref.shape[1], step):
        bog_ref[:, at : at + step] = jnp.sum(
            signal * probe_ref[:, at : at + step].astype(F32), axis=0, keepdims=True
        )
    for ref, turned_ref in (
        (sn0_ref, snt0_ref), (sn1_ref, snt1_ref), (sk0_ref, skt0_ref), (sk1_ref, skt1_ref)
    ):
        turned_ref[...] = jnp.transpose(ref[...])


def up_kernel(
    nh_ref, upg_ref, up_ref, hidden_ref, fgain_ref, grad_ref, mix0_ref, mix1_ref, wo_ref,
    hg_ref, mg_ref, mgt_ref, fgg_ref, sent_ref, kept_ref, nht_ref, mixt_ref,
):
    width, wide = up_ref.shape
    nht_ref[...] = jnp.transpose(nh_ref[...])
    mixt_ref[:, :TILE] = mix0_ref[...]
    mixt_ref[:, TILE:] = mix1_ref[...]
    upstream = dot_t(upg_ref[...], up_ref[...])
    unit, scale = normalised(hidden_ref[...])
    part, gain_part = norm_back(unit, scale, fgain_ref[...], upstream)
    fgg_ref[...] = gain_part
    total = grad_ref[...] + part
    hg_ref[...] = total
    low = total.astype(BF16)
    mixed_grad = dot_t(low, wo_ref[...]).astype(BF16)
    mg_ref[...] = mixed_grad
    mgt_ref[...] = jnp.transpose(mixed_grad)
    core = lax.axis_index("batch") & 1
    half, step = wide // 2, 512
    for place, ref in ((1 - core, sent_ref), (core, kept_ref)):
        for at in range(0, half, step):
            grad = upg_ref[:, pl.ds(pl.multiple_of(place * half + at, step), step)]
            ref[at * width // step : (at + step) * width // step] = dot(nht_ref[...], grad).astype(BF16)
        rows = pl.ds(pl.multiple_of(place * (width // 2), width // 2), width // 2)
        ref[half * width // step :] = dot(mixt_ref[rows], low).astype(BF16)


def attend_back(start, pair, tile, w_ref, mg_ref, mgt_ref, q_ref, values, keys_t, dq_ref, dks, dvs):
    seen = before_diagonal()
    lanes = pl.ds(pl.multiple_of((start + pair) * PAIR, PAIR), PAIR)
    rows = slice(tile * TILE, (tile + 1) * TILE)
    upstream_t, upstream, query = mgt_ref[lanes, rows], mg_ref[rows, lanes], q_ref[rows, lanes]
    row = lax.broadcasted_iota(jnp.int32, (PAIR, TILE), 0)
    lane = lax.broadcasted_iota(jnp.int32, (TILE, PAIR), 1)
    none, none_t = jnp.zeros_like(upstream), jnp.zeros_like(upstream_t)
    for head in range(2):
        above_t = jnp.where(row // HEAD == head, upstream_t, none_t)
        first, middle_grad, last = [dot(block[:, lanes], above_t) for block in values]
        edge_grad = jnp.where(seen, last, first)
        weights = w_ref[2 * (start + pair) + head]
        edge, middle = weights[:TILE].astype(F32), weights[TILE:].astype(F32)
        centred = jnp.sum(edge * edge_grad + middle * middle_grad, axis=0, keepdims=True)
        edge = (edge * (edge_grad - centred)).astype(BF16)
        middle = (middle * (middle_grad - centred)).astype(BF16)
        left, right = halves(edge, seen)
        above = jnp.where(lane // HEAD == head, upstream, none)
        one = jnp.where(lane // HEAD == head, query, none)
        own = pl.ds(pl.multiple_of((start + pair) * PAIR + head * HEAD, HEAD), HEAD)
        grad = dot(keys_t[0][own], left) + dot(keys_t[1][own], middle) + dot(keys_t[2][own], right)
        dq_ref[pl.ds(pl.multiple_of(pair * PAIR + head * HEAD, HEAD), HEAD), rows] = grad
        w_left, w_right = halves(weights[:TILE], seen)
        for place, part in enumerate((left, middle, right)):
            dks[place] = dks[place] + dot(part, one)
        for place, part in enumerate((w_left, weights[TILE:], w_right)):
            dvs[place] = dvs[place] + dot(part, above)


def rows_of(*smalls):
    rows = [s[:, at : at + TILE] for s in smalls for at in range(0, s.shape[1], TILE)]
    rows.append(jnp.zeros((128 - len(rows), TILE), F32))
    return jnp.concatenate(rows, axis=0).astype(BF16)


def attention_kernel(
    part, final, w0_ref, w1_ref, mg_ref, mgt_ref, q_ref, sv0_ref, sv1_ref, v_ref, skt0_ref, skt1_ref, kt_ref,
    cos_ref, sin_ref, nt_ref, snt0_ref, snt1_ref, wq_ref, wk_ref, wv_ref, *rest,
):
    if final:
        x_ref, memory_ref, side0_ref, side1_ref, gain_ref, hg_ref, up_ref, sup_ref, ig_ref, sg_ref, grads_ref, dq_ref, dk_ref, dv_ref = rest
    else:
        bog_ref, fgg_ref, nup_ref, nsup_ref, grads_ref, dq_ref, dk_ref, dv_ref = rest
    block, width = q_ref.shape
    pairs = width // PAIR // 2
    values = (sv0_ref, sv1_ref, v_ref.at[:TILE], v_ref.at[TILE:])
    keys_t = (skt0_ref, skt1_ref, kt_ref.at[:, :TILE], kt_ref.at[:, TILE:])

    def one_pair(pair, carry):
        dk, dv = [0.0] * 4, [0.0] * 4
        for tile, w_ref in ((1, w1_ref), (0, w0_ref)):
            dks, dvs = dk[tile : tile + 3], dv[tile : tile + 3]
            attend_back(
                part * pairs, pair, tile, w_ref, mg_ref, mgt_ref, q_ref, values[tile : tile + 3],
                keys_t[tile : tile + 3], dq_ref, dks, dvs,
            )
            dk[tile : tile + 3], dv[tile : tile + 3] = dks, dvs
        inside = pl.ds(pl.multiple_of(pair * PAIR, PAIR), PAIR)
        for place in range(4):
            dk_ref[place * TILE : (place + 1) * TILE, inside] = dk[place]
            dv_ref[place * TILE : (place + 1) * TILE, inside] = dv[place].astype(BF16)
        return carry

    lax.fori_loop(0, pairs, one_pair, 0)
    dk = [dk_ref[place * TILE : (place + 1) * TILE] for place in range(4)]
    dv = [dv_ref[place * TILE : (place + 1) * TILE] for place in range(4)]
    lanes = slice(part * (width // 2), (part + 1) * (width // 2))
    scale = 1.0 / math.sqrt(HEAD)
    cosine, sine = cos_ref[...], -sin_ref[...]
    dq = turned(jnp.transpose(dq_ref[...]) * scale, cosine[block:], sine[block:]).astype(BF16)
    dk = [
        turned(p, cosine[i * TILE : (i + 1) * TILE], sine[i * TILE : (i + 1) * TILE]).astype(BF16)
        for i, p in enumerate(dk)
    ]
    own_k, own_v = jnp.concatenate(dk[2:], axis=0), jnp.concatenate(dv[2:], axis=0)
    side_k, side_v = jnp.concatenate(dk[:2], axis=0), jnp.concatenate(dv[:2], axis=0)
    rows_t = nt_ref[...]
    side_t = jnp.concatenate([snt0_ref[...], snt1_ref[...]], axis=1)
    grads_ref[:width] = dot(rows_t, dq).astype(BF16)
    grads_ref[width : 2 * width] = (dot(rows_t, own_k) + dot(side_t, side_k)).astype(BF16)
    grads_ref[2 * width : 3 * width] = (dot(rows_t, own_v) + dot(side_t, side_v)).astype(BF16)
    wk, wv = wk_ref[:, lanes], wv_ref[:, lanes]
    upstream = dot_t(dq, wq_ref[:, lanes]) + dot_t(own_k, wk) + dot_t(own_v, wv)
    side_up = dot_t(side_k, wk) + dot_t(side_v, wv)
    if not final:
        grads_ref[3 * width :] = rows_of(bog_ref[...], fgg_ref[...])
        nup_ref[...] = upstream
        nsup_ref[...] = side_up
        return
    upstream = upstream + up_ref[...]
    side_up = side_up + sup_ref[...]
    unit, spread = normalised(x_ref[...].astype(F32))
    back, gain_part = norm_back(unit, spread, gain_ref[...], upstream)
    ig_ref[...] = hg_ref[...] + back
    for i, ref in enumerate((side0_ref, side1_ref)):
        at = slice(i * TILE, (i + 1) * TILE)
        unit, spread = normalised(side_rows(memory_ref.at[at], ref))
        back, side_gain = norm_back(unit, spread, gain_ref[...], side_up[at])
        sg_ref[at] = back.astype(BF16)
        gain_part = gain_part + side_gain
    grads_ref[3 * width :] = rows_of(gain_part)


def places(own_ref, other_ref):
    core = lax.axis_index("batch") & 1
    return ((core, own_ref), (1 - core, other_ref))


def tall_final(own_ref, other_ref, out_ref, work_ref, sems):
    half = own_ref.shape[0]
    copies = []
    for number, (place, ref) in enumerate(places(own_ref, other_ref)):
        for at in range(0, half, half // 2):
            rows = pl.ds(pl.multiple_of(place * half + at, half // 2), half // 2)
            work_ref[rows] = ref[at : at + half // 2].astype(F32)
            copies.append(pltpu.make_async_copy(work_ref.at[rows], out_ref.at[rows], sems.at[len(copies)]))
            copies[-1].start()
    for copy in copies:
        copy.wait()


def wide_final(own_ref, other_ref, out_ref, *more):
    work_ref, sems = more[-2:]
    width, wide = out_ref.shape
    step = own_ref.shape[1]
    copies = []
    for place, ref in places(own_ref, other_ref):
        for at in range(wide // 2 // step):
            lanes = pl.ds(pl.multiple_of(place * (wide // 2) + at * step, step), step)
            work_ref[:, lanes] = ref[at * width : (at + 1) * width].astype(F32)
            copies.append(pltpu.make_async_copy(work_ref.at[:, lanes], out_ref.at[:, lanes], sems.at[len(copies)]))
            copies[-1].start()
        if len(more) > 2:
            half = width // 2
            more[1][pl.ds(pl.multiple_of(place * half, half), half)] = ref[wide // 2 // step * width :].astype(F32)
    if len(more) > 2:
        copies.append(pltpu.make_async_copy(more[1], more[0], sems.at[len(copies)]))
        copies[-1].start()
    for copy in copies:
        copy.wait()


def rest_final(own_ref, other_ref, q_ref, k_ref, v_ref, bog_ref, fgg_ref, gg_ref):
    width = q_ref.shape[0]
    half = width // 2
    for place, ref in places(own_ref, other_ref):
        lanes = pl.ds(pl.multiple_of(place * half, half), half)
        for at, out in enumerate((q_ref, k_ref, v_ref)):
            out[:, lanes] = ref[at * width : (at + 1) * width].astype(F32)
    own, other = (ref[3 * width : 3 * width + 16].astype(F32) for ref in (own_ref, other_ref))
    core = lax.axis_index("batch") & 1
    zero, one = jnp.where(core == 0, own, other), jnp.where(core == 0, other, own)
    count = bog_ref.shape[0] // half
    for out, rows, first in ((bog_ref, zero, 0), (fgg_ref, zero, count), (gg_ref, one, 0)):
        for at in range(out.shape[0] // half):
            out[at * half : (at + 1) * half] = rows[first + at]


def add_back_kernel(part_ref, returned_ref, out_ref):
    out_ref[...] = part_ref[...] + returned_ref[...].astype(F32)


def call(kernel, operands, results, scratch=(), limit=6, outside=0):
    nbytes = sum(a.size * a.dtype.itemsize for a in operands) + sum(
        math.prod(s) * jnp.dtype(d).itemsize for s, d in results
    )
    return pl.pallas_call(
        kernel,
        out_shape=tuple(jax.ShapeDtypeStruct(s, d) for s, d in results),
        in_specs=[VMEM] * len(operands),
        out_specs=tuple(HBM if i < outside else VMEM for i in range(len(results))),
        scratch_shapes=list(scratch),
        compiler_params=pltpu.CompilerParams(vmem_limit_bytes=limit * MEGA),
        cost_estimate=pl.CostEstimate(flops=STEP_FLOPS, bytes_accessed=nbytes, transcendentals=0),
    )(*operands)


def exchanges(batches, blocks):
    number = batches * blocks

    def pairs(partner):
        return [
            (d, p[0] * blocks + p[1])
            for d in range(number)
            for p in [partner(d // blocks, d % blocks)]
        ]

    flips = {
        "x": (lambda b, s: (b, s ^ 1), lambda b, s: s),
        "y": (lambda b, s: (b ^ 2, s), lambda b, s: (b & 2) // 2),
        "z": (lambda b, s: (b ^ 4, s), lambda b, s: (b & 4) // 4),
    }

    def flip(place):
        return (pairs(lambda b, s: (b ^ place, s)), lambda b, s: (b & place) // place)

    def mixed(way):
        (first, first_bit), (second, second_bit) = (flips[axis] for axis in way)
        return (
            pairs(lambda b, s: second(b, s) if b % 2 else first(b, s)),
            lambda b, s: jnp.where(b & 1 == 0, first_bit(b, s), second_bit(b, s)),
        )

    found = {way: mixed(way) for way in ("xy", "yx", "zy", "yz", "xz", "zx", "xx", "yy", "zz")}
    found["core"] = flip(1)
    rest = []
    place = 8
    while place < batches:
        rest.append(flip(place))
        place *= 2
    return found, rest


def added(left, right, rows):
    return (left[rows].astype(F32) + right[rows].astype(F32)).astype(BF16)


def halve_kernel(bit, kept_ref, arrived_ref, sent_ref, left_ref):
    half, mine = sent_ref.shape[0], bit(lax.axis_index("batch"), lax.axis_index("seq"))
    step = 16 * math.gcd(half // 16, 8)
    for place, ref in ((1 - mine, sent_ref), (mine, left_ref)):
        for at in range(0, half, step):
            rows = pl.ds(pl.multiple_of(place * half + at, 16), step)
            ref[at : at + step] = added(kept_ref, arrived_ref, rows)


def add_kernel(kept_ref, arrived_ref, out_ref):
    half = out_ref.shape[0]
    step = 16 * math.gcd(half // 16, 8)
    for at in range(0, half, step):
        out_ref[at : at + step] = added(kept_ref, arrived_ref, slice(at, at + step))


def double_kernel(bit, kept_ref, arrived_ref, out_ref):
    half, mine = kept_ref.shape[0], bit(lax.axis_index("batch"), lax.axis_index("seq"))
    for place, ref in ((mine, kept_ref), (1 - mine, arrived_ref)):
        out_ref[pl.ds(pl.multiple_of(place * half, 16), half)] = ref[...]


def choose_kernel(bit, kept0_ref, arrived0_ref, kept1_ref, arrived1_ref, sent_ref, left_ref):
    mine = bit(lax.axis_index("batch"), lax.axis_index("seq"))
    step = 128
    for at in range(0, sent_ref.shape[0], step):
        rows = slice(at, at + step)
        zero, one = added(kept0_ref, arrived0_ref, rows), added(kept1_ref, arrived1_ref, rows)
        left_ref[rows] = jnp.where(mine == 0, zero, one)
        sent_ref[rows] = jnp.where(mine == 0, one, zero)


def pick_kernel(bit, zero_ref, one_ref, sent_ref, left_ref):
    mine = bit(lax.axis_index("batch"), lax.axis_index("seq"))

    @pl.when(mine == 0)
    def _():
        left_ref[...] = zero_ref[...]
        sent_ref[...] = one_ref[...]

    @pl.when(mine != 0)
    def _():
        left_ref[...] = one_ref[...]
        sent_ref[...] = zero_ref[...]


class Sum:
    def __init__(self, halvings, fulls, sent, kept, finish):
        self.halvings, self.fulls, self.finish = halvings, fulls, finish
        self.sent, self.kept, self.arrived, self.at = sent, kept, None, 0

    def start(self, exchange):
        self.arrived = lax.ppermute(self.sent, AXES, exchange[0])

    def add(self):
        (self.kept,) = call(add_kernel, (self.kept, self.arrived), [(self.kept.shape, BF16)])
        self.sent = self.kept

    def advance(self, *after):
        count, at = len(self.halvings), self.at
        self.at += 1
        if at == 0:
            self.sent = fence(self.sent, *after)[0]
            self.start(self.halvings[0])
            return self.sent
        self.kept = fence(self.kept, *after)[0]
        rows, columns = self.kept.shape
        if at < count:
            self.sent, self.kept = call(
                functools.partial(halve_kernel, self.halvings[at][1]),
                (self.kept, self.arrived),
                [((rows // 2, columns), BF16)] * 2,
            )
            self.start(self.halvings[at])
        elif at == count:
            self.add()
            self.start(self.fulls[0])
        elif at == count + 1:
            for exchange in self.fulls[1:]:
                self.add()
                self.start(exchange)
            self.add()
            self.start(self.halvings[-1])
        elif at <= 2 * count:
            (self.kept,) = call(
                functools.partial(double_kernel, self.halvings[2 * count + 1 - at + 0][1]),
                (self.kept, self.arrived),
                [((rows * 2, columns), BF16)],
            )
            self.sent = self.kept
            self.start(self.halvings[2 * count - at])
        else:
            self.result = self.finish(self.kept, self.arrived)
            return self.result[0]
        return self.sent


def fence(*arrays):
    return lax.optimization_barrier(arrays)


def body(
    inputs,
    memory,
    cotangent,
    labels,
    attention_gain,
    query_weight,
    key_weight,
    value_weight,
    out_weight,
    forward_gain,
    up_weight,
    down_weight,
    boundary_hidden,
    boundary_out,
):
    group, block, width = inputs.shape
    wide, hidden_wide = up_weight.shape[1], boundary_hidden.shape[1]
    batches, blocks = (lax.axis_size("batch"), lax.axis_size("seq"))
    found, fulls = exchanges(batches, blocks)
    column = lax.axis_index("seq")
    core = lax.axis_index("batch") % 2
    rows = inputs.reshape(block, width)
    memory_rows = memory.reshape(block, width)
    onward = [(i, i + 1) for i in range(blocks - 1)]
    side1 = lax.ppermute(rows[TILE:], "seq", onward)
    tables = rotary_tables(-block, (blocks + 1) * block)
    cosine, sine = (
        lax.dynamic_slice_in_dim(jnp.asarray(t), column * block, 2 * block) for t in tables
    )
    gain = attention_gain.reshape(1, width)
    square, side_shape = (block, width), (TILE, width)
    turned_square, turned_side = (width, block), (width, TILE)
    normed_t, queries, queries_t, keys, keys_t, values, values_t = call(
        own_kernel,
        (rows, gain, query_weight, key_weight, value_weight, cosine, sine),
        [(turned_square, BF16), (square, BF16), (turned_square, BF16)]
        + [(square, BF16), (turned_square, BF16)] * 2,
    )
    side0 = lax.ppermute(fence(rows, queries)[0][:TILE], "seq", onward)
    side_results = [
        (side_shape, BF16), (side_shape, BF16), (side_shape, BF16), (turned_side, BF16),
        ((HEADS, 2 * TILE, TILE), BF16), (turned_side, BF16),
    ]
    sn1, sk1, sv1, sv_t1, weights1, mix1 = call(
        late_kernel,
        (memory_rows, side1, gain, key_weight, value_weight, cosine, sine, queries_t, keys, values_t),
        side_results,
    )
    sn0, sk0, sv0, sv_t0, weights0, mix0 = call(
        early_kernel,
        (memory_rows, side0, gain, key_weight, value_weight, cosine, sine, queries_t, keys, values_t, sk1, sv_t1),
        side_results,
    )
    bh_half = (hidden_wide // 2 * width // 512, 512)
    (
        hidden, normed_hidden, gated, slope, outputs, probe_grad, hidden_sent, hidden_kept, probe, signal,
    ) = call(
        forward_kernel,
        (
            rows, mix0, mix1, out_weight, forward_gain.reshape(1, width), up_weight, down_weight,
            boundary_hidden, boundary_out.reshape(1, hidden_wide), labels,
        ),
        [
            (square, F32), (square, BF16), ((block, wide), BF16),
            ((block, wide), BF16), (square, BF16), ((block, hidden_wide), BF16),
            (bh_half, BF16), (bh_half, BF16), ((block, hidden_wide), BF16), ((block, PAIR), F32),
        ],
        [
            pltpu.VMEM((block, hidden_wide), BF16),
            pltpu.VMEM((width, block), BF16),
        ],
        limit=18,
    )
    sums, made = {}, {}

    def add_sum(name, way, sent, kept, finish):
        sums[name] = Sum([found[w] for w in way], fulls, sent, kept, finish)

    add_sum(
        "hidden", ("core", "xy", "yx", "zz"), hidden_sent, hidden_kept,
        lambda own, other: call(
            wide_final, (own, other), [((width, hidden_wide), F32)],
            [pltpu.VMEM((width, hidden_wide), F32), pltpu.SemaphoreType.DMA((4,))], outside=1,
        ),
    )
    up_half = (wide // 2 * width // 512 + width // 2, 512)
    grads_shape = ((3 * width + 128, width // 2), BF16)
    work = [
        pltpu.VMEM((width // 2, block), F32),
        pltpu.VMEM((2 * block, width // 2), F32),
        pltpu.VMEM((2 * block, width // 2), BF16),
    ]
    def down_part(*after):
        grad = fence(probe_grad, *after)[0]
        final_grad, up_grad, sent, kept, boundary_out_grad, sn_t0, sn_t1, sk_t0, sk_t1 = call(
            down_kernel,
            (
                grad, boundary_hidden, cotangent.reshape(square), gated, slope, down_weight, probe, signal,
                sn0, sn1, sk0, sk1,
            ),
            [(square, F32), ((block, wide), BF16), ((wide // 2, width), BF16), ((wide // 2, width), BF16)]
            + [((1, hidden_wide), F32)] + [(turned_side, BF16)] * 4,
        )
        made["down"] = (final_grad, up_grad, boundary_out_grad)
        made["shared"] = (
            queries, sv0, sv1, values, sk_t0, sk_t1, keys_t,
            cosine, sine, normed_t, sn_t0, sn_t1, query_weight, key_weight, value_weight,
        )
        add_sum(
            "down", ("core", "xy", "yx", "zz"), sent, kept,
            lambda own, other: call(
                tall_final, (own, other), [((wide, width), F32)],
                [pltpu.VMEM((wide, width), F32), pltpu.SemaphoreType.DMA((4,))], outside=1,
            ),
        )
        return up_grad

    def up_part(*after):
        final_grad, up_grad, _ = made["down"]
        up_grad = fence(up_grad, *after)[0]
        hidden_grad, mixed_grad, mixed_grad_t, gain_part, sent, kept = call(
            up_kernel,
            (
                normed_hidden, up_grad, up_weight, hidden, forward_gain.reshape(1, width), final_grad,
                mix0, mix1, out_weight,
            ),
            [
                (square, F32), (square, BF16), (turned_square, BF16), ((1, width), F32),
                (up_half, BF16), (up_half, BF16),
            ],
            [pltpu.VMEM((width, block), BF16), pltpu.VMEM((width, block), BF16)],
        )
        made["up"] = (hidden_grad, (weights0, weights1, mixed_grad, mixed_grad_t) + made["shared"], gain_part)
        add_sum(
            "up", ("core", "xy", "yx", "zz"), sent, kept,
            lambda own, other: call(
                wide_final, (own, other), [((width, wide), F32), ((width, width), F32)],
                [pltpu.VMEM((width, width), F32), pltpu.VMEM((width, wide), F32), pltpu.SemaphoreType.DMA((5,))],
                outside=2,
            ),
        )
        return mixed_grad

    def attention0(*after):
        hidden_grad, operands, gain_part = made["up"]
        operands = (fence(weights0, *after)[0],) + operands[1:]
        made["attention"] = call(
            functools.partial(attention_kernel, 0, False),
            operands + (made["down"][2], gain_part),
            [(square, F32), (square, F32), grads_shape],
            work,
            limit=10,
        )
        return made["attention"][0]

    def attention1(*after):
        hidden_grad, operands, _ = made["up"]
        upstream, side_upstream, grads0 = made["attention"]
        upstream = fence(upstream, *after)[0]
        input_part, side_grad, grads1 = call(
            functools.partial(attention_kernel, 1, True),
            operands + (rows, memory_rows, side0, side1, gain, hidden_grad, upstream, side_upstream),
            [(square, F32), (square, BF16), grads_shape],
            work,
            limit=10,
        )
        made["input"] = (input_part, side_grad)
        picked = call(
            functools.partial(pick_kernel, found["core"][1]), (grads0, grads1), [grads_shape] * 2
        )
        add_sum(
            "rest", ("core", "xy", "yx", "zz"), *picked,
            lambda own, other: call(
                rest_final, (own, other), [((width, width), F32)] * 3 + [((hidden_wide,), F32), ((width,), F32), ((width,), F32)],
            ),
        )
        return picked[0]

    def send_back(*after):
        input_part, side_grad = made["input"]
        side_grad = fence(side_grad, *after)[0]
        made["returned"] = lax.ppermute(side_grad, "seq", [(i + 1, i) for i in range(blocks - 1)])
        return side_grad

    def add_back(*after):
        input_part = fence(made["input"][0], *after)[0]
        (made["input_grad"],) = call(add_back_kernel, (input_part, made["returned"]), [(square, F32)])
        return made["input_grad"]

    parts = {
        "a": down_part, "b": up_part, "c": attention0, "d": attention1, "r": send_back, "s": add_back,
    }
    names = {"H": "hidden", "D": "down", "U": "up", "T": "rest"}
    token = hidden_kept
    for letter in ORDER:
        token = parts[letter](token) if letter in parts else sums[names[letter]].advance(token)
    (hidden_total,), (down_total,) = (sums["hidden"].result, sums["down"].result)
    up_total, out_total = sums["up"].result
    query_total, key_total, value_total, boundary_out_total, forward_gain_total, gain_total = sums["rest"].result
    input_grad = made["input_grad"]
    return (
        outputs.reshape(inputs.shape),
        input_grad.reshape(inputs.shape),
        gain_total,
        query_total,
        key_total,
        value_total,
        out_total,
        forward_gain_total,
        up_total,
        down_total,
        hidden_total,
        boundary_out_total,
    )


def solution(mesh):
    placed = (
        P("batch", "seq", None),
        P("batch", None, None),
        P("batch", "seq", None),
        P("batch", "seq"),
        P(),
        P(),
        P(),
        P(),
        P(),
        P(),
        P(),
        P(),
        P(),
        P(),
    )
    return jax.shard_map(
        body,
        mesh=mesh,
        in_specs=placed,
        out_specs=(
            P("batch", "seq", None),
            P("batch", "seq", None),
            P(),
            P(),
            P(),
            P(),
            P(),
            P(),
            P(),
            P(),
            P(),
            P(),
        ),
        check_vma=False,
    )
```

```python
import functools
import math

import jax
import jax.numpy as jnp
import numpy as np
from jax import lax
from jax.experimental import pallas as pl
from jax.experimental.pallas import tpu as pltpu
from jax.sharding import PartitionSpec as P

HEADS = 8
HEAD = 64
PAIR = 2 * HEAD
TILE = 256
EPS = 1e-05
BASE = 10000.0
AXES = ("batch", "seq")
F32, BF16 = jnp.float32, jnp.bfloat16
VMEM = pl.BlockSpec(memory_space=pltpu.VMEM)
HBM = pl.BlockSpec(memory_space=pl.ANY)
STEP_FLOPS = int(2e10)
MEGA = 1024 * 1024
ORDER = "HaHDbUcUDHdUTHDTHDUTDrHUTDHTUDHTUDTUHTsDHUDTUT"


def dot(left, right):
    return jnp.dot(left, right, preferred_element_type=F32)


def dot_t(left, right):
    return lax.dot_general(left, right, (((1,), (1,)), ((), ())), preferred_element_type=F32)


def t_dot(left, right):
    return lax.dot_general(left, right, (((0,), (0,)), ((), ())), preferred_element_type=F32)


def normalised(values):
    centre = values - jnp.mean(values, axis=-1, keepdims=True)
    spread = jnp.mean(centre * centre, axis=-1, keepdims=True)
    scale = lax.rsqrt(spread + EPS)
    return centre * scale, scale


def norm_back(unit, scale, gain, upstream):
    product = upstream * unit
    inner = upstream * gain
    mean = jnp.mean(inner, axis=-1, keepdims=True)
    along = jnp.mean(inner * unit, axis=-1, keepdims=True)
    return scale * (inner - mean - unit * along), jnp.sum(product, axis=0, keepdims=True)


def gelu_both(value):
    factor = math.sqrt(2.0 / math.pi)
    square = value * value
    half = 0.5 + 0.5 * jnp.tanh(value * (factor + (factor * 0.044715) * square))
    result = value * half
    bend = (result - result * half) * (2.0 * factor + (6.0 * factor * 0.044715) * square)
    return result, half + bend


def turned(values, cosine, sine):
    front = lax.broadcasted_iota(jnp.int32, (values.shape[0], PAIR), 1) % HEAD < HEAD // 2
    parts = []
    for at in range(0, values.shape[1], PAIR):
        part = values[:, at : at + PAIR]
        other = jnp.where(
            front, pltpu.roll(part, PAIR - HEAD // 2, 1), pltpu.roll(part, HEAD // 2, 1)
        )
        parts.append(part * cosine + other * sine)
    return jnp.concatenate(parts, axis=1)


def rotary_tables(first, count):
    positions = np.arange(first, first + count, dtype=np.float32)
    half = HEAD // 2
    freqs = np.float32(BASE) ** (-(np.arange(half, dtype=np.float32) * np.float32(2.0 / HEAD)))
    angles = (positions[:, None] * freqs[None, :].astype(np.float32)).astype(np.float64)
    cosine, sine = (np.cos(angles), np.sin(angles))
    return (
        np.concatenate([cosine] * 4, axis=1).astype(np.float32),
        np.concatenate([-sine, sine] * 2, axis=1).astype(np.float32),
    )


def own_kernel(
    x_ref, gain_ref, wq_ref, wk_ref, wv_ref, cos_ref, sin_ref,
    nt_ref, q_ref, qt_ref, k_ref, kt_ref, v_ref, vt_ref,
):
    unit, _ = normalised(x_ref[...].astype(F32))
    low = (unit * gain_ref[...]).astype(BF16)
    nt_ref[...] = jnp.transpose(low)
    block = low.shape[0]
    cosine, sine = cos_ref[block:], sin_ref[block:]
    scale = 1.0 / math.sqrt(HEAD)
    query = turned(dot(low, wq_ref[...]), cosine, sine).astype(BF16).astype(F32) * scale
    query = query.astype(BF16)
    q_ref[...] = query
    qt_ref[...] = jnp.transpose(query)
    key = turned(dot(low, wk_ref[...]), cosine, sine).astype(BF16)
    k_ref[...] = key
    kt_ref[...] = jnp.transpose(key)
    value = dot(low, wv_ref[...]).astype(BF16)
    v_ref[...] = value
    vt_ref[...] = jnp.transpose(value)


def before_diagonal():
    key = lax.broadcasted_iota(jnp.int32, (TILE, TILE), 0)
    return key <= lax.broadcasted_iota(jnp.int32, (TILE, TILE), 1)


def halves(array, seen):
    none = jnp.zeros_like(array)
    return jnp.where(seen, none, array), jnp.where(seen, array, none)


def attend(q_t, keys, values_t, w_ref, mix_ref):
    seen = before_diagonal()
    pairs = mix_ref.shape[0] // PAIR

    def one_pair(pair, carry):
        lanes = pl.ds(pl.multiple_of(pair * PAIR, PAIR), PAIR)
        both = q_t(lanes)
        row = lax.broadcasted_iota(jnp.int32, both.shape, 0)
        for head in range(2):
            query = jnp.where(row // HEAD == head, both, jnp.zeros_like(both))
            first, middle, last = [dot(block(lanes), query) for block in keys]
            edge = jnp.where(seen, last, first)
            peak = jnp.maximum(
                jnp.max(edge, axis=0, keepdims=True), jnp.max(middle, axis=0, keepdims=True)
            )
            edge, middle = jnp.exp(edge - peak), jnp.exp(middle - peak)
            total = jnp.sum(edge + middle, axis=0, keepdims=True)
            edge, middle = (edge / total).astype(BF16), (middle / total).astype(BF16)
            w_ref[2 * pair + head, :TILE] = edge
            w_ref[2 * pair + head, TILE:] = middle
            own = pl.ds(pl.multiple_of(pair * PAIR + head * HEAD, HEAD), HEAD)
            left, right = halves(edge, seen)
            mix = dot(values_t[0](own), left) + dot(values_t[1](own), middle)
            mix_ref[own] = (mix + dot(values_t[2](own), right)).astype(BF16)
        return carry

    lax.fori_loop(0, pairs, one_pair, 0, unroll=pairs)


def side_rows(memory_ref, received_ref):
    return jnp.where(lax.axis_index("seq") == 0, memory_ref[...], received_ref[...]).astype(F32)


def side_part(memory_ref, received_ref, gain_ref, wk_ref, wv_ref, cos_ref, sin_ref, sn_ref, k_ref, v_ref, vt_ref):
    unit, _ = normalised(side_rows(memory_ref, received_ref))
    low = (unit * gain_ref[...]).astype(BF16)
    sn_ref[...] = low
    key = turned(dot(low, wk_ref[...]), cos_ref[...], sin_ref[...]).astype(BF16)
    k_ref[...] = key
    value = dot(low, wv_ref[...]).astype(BF16)
    v_ref[...] = value
    vt_ref[...] = jnp.transpose(value)


def late_kernel(
    memory_ref, received_ref, gain_ref, wk_ref, wv_ref, cos_ref, sin_ref, qt_ref, ok_ref, ovt_ref,
    sn_ref, k_ref, v_ref, vt_ref, w_ref, mix_ref,
):
    side_part(
        memory_ref.at[TILE:], received_ref, gain_ref, wk_ref, wv_ref, cos_ref.at[TILE : 2 * TILE], sin_ref.at[TILE : 2 * TILE],
        sn_ref, k_ref, v_ref, vt_ref,
    )
    attend(
        lambda at: qt_ref[at, TILE:],
        (lambda at: k_ref[:, at], lambda at: ok_ref[:TILE, at], lambda at: ok_ref[TILE:, at]),
        (lambda at: vt_ref[at], lambda at: ovt_ref[at, :TILE], lambda at: ovt_ref[at, TILE:]),
        w_ref,
        mix_ref,
    )


def early_kernel(
    memory_ref, received_ref, gain_ref, wk_ref, wv_ref, cos_ref, sin_ref, qt_ref, ok_ref, ovt_ref, sk_ref, svt_ref,
    sn_ref, k_ref, v_ref, vt_ref, w_ref, mix_ref,
):
    side_part(
        memory_ref.at[:TILE], received_ref, gain_ref, wk_ref, wv_ref, cos_ref.at[:TILE], sin_ref.at[:TILE],
        sn_ref, k_ref, v_ref, vt_ref,
    )
    attend(
        lambda at: qt_ref[at, :TILE],
        (lambda at: k_ref[:, at], lambda at: sk_ref[:, at], lambda at: ok_ref[:TILE, at]),
        (lambda at: vt_ref[at], lambda at: svt_ref[at], lambda at: ovt_ref[at, :TILE]),
        w_ref,
        mix_ref,
    )


def forward_kernel(
    x_ref, mix0_ref, mix1_ref, wo_ref, fgain_ref, up_ref, down_ref, bh_ref, bo_ref, labels_ref,
    hidden_ref, nh_ref, gated_ref, slope_ref, out_ref, pg_ref, sent_ref, kept_ref, probe_ref, signal_ref,
    pslope_ref, turn_ref,
):
    block, width = x_ref.shape
    mixed = jnp.concatenate([jnp.transpose(mix0_ref[...]), jnp.transpose(mix1_ref[...])], axis=0)
    hidden = x_ref[...].astype(F32) + dot(mixed, wo_ref[...])
    hidden_ref[...] = hidden
    unit, _ = normalised(hidden)
    low = (unit * fgain_ref[...]).astype(BF16)
    nh_ref[...] = low
    step = 1024
    tops = [slice(top, top + TILE) for top in range(0, block, TILE)]
    for part_rows in tops:
        part = hidden[part_rows]
        for at in range(0, up_ref.shape[1], step):
            gated, slope = gelu_both(dot(low[part_rows], up_ref[:, at : at + step]))
            gated = gated.astype(BF16)
            gated_ref[part_rows, at : at + step] = gated
            slope_ref[part_rows, at : at + step] = slope.astype(BF16)
            part = part + dot(gated, down_ref[at : at + step])
        out_ref[part_rows] = part.astype(BF16)
    out = out_ref[...]
    turn_ref[...] = jnp.transpose(out)
    logits = []
    for part_rows in tops:
        logit = jnp.zeros((TILE, 1), F32)
        for at in range(0, bh_ref.shape[1], step):
            probe, slope = gelu_both(dot(out[part_rows], bh_ref[:, at : at + step]))
            probe = probe.astype(BF16)
            probe_ref[part_rows, at : at + step] = probe
            pslope_ref[part_rows, at : at + step] = slope.astype(BF16)
            logit = logit + jnp.sum(
                probe.astype(F32) * bo_ref[:, at : at + step].astype(F32), axis=-1, keepdims=True
            )
        logits.append(logit)
    logits = jnp.concatenate(logits, axis=0)
    targets = jnp.transpose(jnp.broadcast_to(labels_ref[...].astype(F32), (PAIR, block)))[:, :1]
    signal = (jax.nn.sigmoid(logits) - targets).astype(BF16).astype(F32)
    step = 512
    half = bh_ref.shape[1] // 2
    core = lax.axis_index("batch") & 1
    for at in range(0, bh_ref.shape[1], step):
        grad = pslope_ref[:, at : at + step].astype(F32) * (
            signal * bo_ref[:, at : at + step].astype(F32)
        )
        pg_ref[:, at : at + step] = grad.astype(BF16)
    for place, ref in ((1 - core, sent_ref), (core, kept_ref)):
        for at in range(0, half, step):
            grad = pg_ref[:, pl.ds(pl.multiple_of(place * half + at, step), step)]
            ref[at * width // step : (at + step) * width // step] = dot(turn_ref[...], grad).astype(BF16)
    signal_ref[...] = jnp.broadcast_to(signal, signal_ref.shape)


def down_kernel(
    pg_ref, bh_ref, cot_ref, gated_ref, slope_ref, down_ref, probe_ref, signal_ref, sn0_ref, sn1_ref, sk0_ref, sk1_ref,
    grad_ref, upg_ref, sent_ref, kept_ref, bog_ref, snt0_ref, snt1_ref, skt0_ref, skt1_ref,
):
    final = cot_ref[...].astype(F32) + dot_t(pg_ref[...], bh_ref[...])
    grad_ref[...] = final
    low = final.astype(BF16)
    step = 512
    half = down_ref.shape[0] // 2
    core = lax.axis_index("batch") & 1
    for at in range(0, half, step):
        rows = pl.ds(pl.multiple_of((1 - core) * half + at, step), step)
        sent_ref[at : at + step] = t_dot(gated_ref[:, rows], low).astype(BF16)
    for at in range(0, half, step):
        rows = pl.ds(pl.multiple_of(core * half + at, step), step)
        kept_ref[at : at + step] = t_dot(gated_ref[:, rows], low).astype(BF16)
    for at in range(0, down_ref.shape[0], step):
        part = slope_ref[:, at : at + step].astype(F32) * dot_t(low, down_ref[at : at + step])
        upg_ref[:, at : at + step] = part.astype(BF16)
    signal = signal_ref[:, :1]
    for at in range(0, bog_ref.shape[1], step):
        bog_ref[:, at : at + step] = jnp.sum(
            signal * probe_ref[:, at : at + step].astype(F32), axis=0, keepdims=True
        )
    for ref, turned_ref in (
        (sn0_ref, snt0_ref), (sn1_ref, snt1_ref), (sk0_ref, skt0_ref), (sk1_ref, skt1_ref)
    ):
        turned_ref[...] = jnp.transpose(ref[...])


def up_kernel(
    nh_ref, upg_ref, up_ref, hidden_ref, fgain_ref, grad_ref, mix0_ref, mix1_ref, wo_ref,
    hg_ref, mg_ref, mgt_ref, fgg_ref, sent_ref, kept_ref, nht_ref, mixt_ref,
):
    width, wide = up_ref.shape
    nht_ref[...] = jnp.transpose(nh_ref[...])
    mixt_ref[:, :TILE] = mix0_ref[...]
    mixt_ref[:, TILE:] = mix1_ref[...]
    upstream = dot_t(upg_ref[...], up_ref[...])
    unit, scale = normalised(hidden_ref[...])
    part, gain_part = norm_back(unit, scale, fgain_ref[...], upstream)
    fgg_ref[...] = gain_part
    total = grad_ref[...] + part
    hg_ref[...] = total
    low = total.astype(BF16)
    mixed_grad = dot_t(low, wo_ref[...]).astype(BF16)
    mg_ref[...] = mixed_grad
    mgt_ref[...] = jnp.transpose(mixed_grad)
    core = lax.axis_index("batch") & 1
    half, step = wide // 2, 512
    for place, ref in ((1 - core, sent_ref), (core, kept_ref)):
        for at in range(0, half, step):
            grad = upg_ref[:, pl.ds(pl.multiple_of(place * half + at, step), step)]
            ref[at * width // step : (at + step) * width // step] = dot(nht_ref[...], grad).astype(BF16)
        rows = pl.ds(pl.multiple_of(place * (width // 2), width // 2), width // 2)
        ref[half * width // step :] = dot(mixt_ref[rows], low).astype(BF16)


def attend_back(start, pair, tile, w_ref, mg_ref, mgt_ref, q_ref, values, keys_t, dq_ref, dks, dvs):
    seen = before_diagonal()
    lanes = pl.ds(pl.multiple_of((start + pair) * PAIR, PAIR), PAIR)
    rows = slice(tile * TILE, (tile + 1) * TILE)
    upstream_t, upstream, query = mgt_ref[lanes, rows], mg_ref[rows, lanes], q_ref[rows, lanes]
    row = lax.broadcasted_iota(jnp.int32, (PAIR, TILE), 0)
    lane = lax.broadcasted_iota(jnp.int32, (TILE, PAIR), 1)
    none, none_t = jnp.zeros_like(upstream), jnp.zeros_like(upstream_t)
    for head in range(2):
        above_t = jnp.where(row // HEAD == head, upstream_t, none_t)
        first, middle_grad, last = [dot(block[:, lanes], above_t) for block in values]
        edge_grad = jnp.where(seen, last, first)
        weights = w_ref[2 * (start + pair) + head]
        edge, middle = weights[:TILE].astype(F32), weights[TILE:].astype(F32)
        centred = jnp.sum(edge * edge_grad + middle * middle_grad, axis=0, keepdims=True)
        edge = (edge * (edge_grad - centred)).astype(BF16)
        middle = (middle * (middle_grad - centred)).astype(BF16)
        left, right = halves(edge, seen)
        above = jnp.where(lane // HEAD == head, upstream, none)
        one = jnp.where(lane // HEAD == head, query, none)
        own = pl.ds(pl.multiple_of((start + pair) * PAIR + head * HEAD, HEAD), HEAD)
        grad = dot(keys_t[0][own], left) + dot(keys_t[1][own], middle) + dot(keys_t[2][own], right)
        dq_ref[pl.ds(pl.multiple_of(pair * PAIR + head * HEAD, HEAD), HEAD), rows] = grad
        w_left, w_right = halves(weights[:TILE], seen)
        for place, part in enumerate((left, middle, right)):
            dks[place] = dks[place] + dot(part, one)
        for place, part in enumerate((w_left, weights[TILE:], w_right)):
            dvs[place] = dvs[place] + dot(part, above)


def rows_of(*smalls):
    rows = [s[:, at : at + TILE] for s in smalls for at in range(0, s.shape[1], TILE)]
    rows.append(jnp.zeros((128 - len(rows), TILE), F32))
    return jnp.concatenate(rows, axis=0).astype(BF16)


def attention_kernel(
    part, final, w0_ref, w1_ref, mg_ref, mgt_ref, q_ref, sv0_ref, sv1_ref, v_ref, skt0_ref, skt1_ref, kt_ref,
    cos_ref, sin_ref, nt_ref, snt0_ref, snt1_ref, wq_ref, wk_ref, wv_ref, *rest,
):
    if final:
        x_ref, memory_ref, side0_ref, side1_ref, gain_ref, hg_ref, up_ref, sup_ref, ig_ref, sg_ref, grads_ref, dq_ref, dk_ref, dv_ref = rest
    else:
        bog_ref, fgg_ref, nup_ref, nsup_ref, grads_ref, dq_ref, dk_ref, dv_ref = rest
    block, width = q_ref.shape
    pairs = width // PAIR // 2
    values = (sv0_ref, sv1_ref, v_ref.at[:TILE], v_ref.at[TILE:])
    keys_t = (skt0_ref, skt1_ref, kt_ref.at[:, :TILE], kt_ref.at[:, TILE:])

    def one_pair(pair, carry):
        dk, dv = [0.0] * 4, [0.0] * 4
        for tile, w_ref in ((1, w1_ref), (0, w0_ref)):
            dks, dvs = dk[tile : tile + 3], dv[tile : tile + 3]
            attend_back(
                part * pairs, pair, tile, w_ref, mg_ref, mgt_ref, q_ref, values[tile : tile + 3],
                keys_t[tile : tile + 3], dq_ref, dks, dvs,
            )
            dk[tile : tile + 3], dv[tile : tile + 3] = dks, dvs
        inside = pl.ds(pl.multiple_of(pair * PAIR, PAIR), PAIR)
        for place in range(4):
            dk_ref[place * TILE : (place + 1) * TILE, inside] = dk[place]
            dv_ref[place * TILE : (place + 1) * TILE, inside] = dv[place].astype(BF16)
        return carry

    lax.fori_loop(0, pairs, one_pair, 0)
    dk = [dk_ref[place * TILE : (place + 1) * TILE] for place in range(4)]
    dv = [dv_ref[place * TILE : (place + 1) * TILE] for place in range(4)]
    lanes = slice(part * (width // 2), (part + 1) * (width // 2))
    scale = 1.0 / math.sqrt(HEAD)
    cosine, sine = cos_ref[...], -sin_ref[...]
    dq = turned(jnp.transpose(dq_ref[...]) * scale, cosine[block:], sine[block:]).astype(BF16)
    dk = [
        turned(p, cosine[i * TILE : (i + 1) * TILE], sine[i * TILE : (i + 1) * TILE]).astype(BF16)
        for i, p in enumerate(dk)
    ]
    own_k, own_v = jnp.concatenate(dk[2:], axis=0), jnp.concatenate(dv[2:], axis=0)
    side_k, side_v = jnp.concatenate(dk[:2], axis=0), jnp.concatenate(dv[:2], axis=0)
    rows_t = nt_ref[...]
    side_t = jnp.concatenate([snt0_ref[...], snt1_ref[...]], axis=1)
    grads_ref[:width] = dot(rows_t, dq).astype(BF16)
    grads_ref[width : 2 * width] = (dot(rows_t, own_k) + dot(side_t, side_k)).astype(BF16)
    grads_ref[2 * width : 3 * width] = (dot(rows_t, own_v) + dot(side_t, side_v)).astype(BF16)
    wk, wv = wk_ref[:, lanes], wv_ref[:, lanes]
    upstream = dot_t(dq, wq_ref[:, lanes]) + dot_t(own_k, wk) + dot_t(own_v, wv)
    side_up = dot_t(side_k, wk) + dot_t(side_v, wv)
    if not final:
        grads_ref[3 * width :] = rows_of(bog_ref[...], fgg_ref[...])
        nup_ref[...] = upstream
        nsup_ref[...] = side_up
        return
    upstream = upstream + up_ref[...]
    side_up = side_up + sup_ref[...]
    unit, spread = normalised(x_ref[...].astype(F32))
    back, gain_part = norm_back(unit, spread, gain_ref[...], upstream)
    ig_ref[...] = hg_ref[...] + back
    for i, ref in enumerate((side0_ref, side1_ref)):
        at = slice(i * TILE, (i + 1) * TILE)
        unit, spread = normalised(side_rows(memory_ref.at[at], ref))
        back, side_gain = norm_back(unit, spread, gain_ref[...], side_up[at])
        sg_ref[at] = back.astype(BF16)
        gain_part = gain_part + side_gain
    grads_ref[3 * width :] = rows_of(gain_part)


def places(own_ref, other_ref):
    core = lax.axis_index("batch") & 1
    return ((core, own_ref), (1 - core, other_ref))


def tall_final(own_ref, other_ref, out_ref, work_ref, sems):
    half = own_ref.shape[0]
    copies = []
    for number, (place, ref) in enumerate(places(own_ref, other_ref)):
        for at in range(0, half, half // 2):
            rows = pl.ds(pl.multiple_of(place * half + at, half // 2), half // 2)
            work_ref[rows] = ref[at : at + half // 2].astype(F32)
            copies.append(pltpu.make_async_copy(work_ref.at[rows], out_ref.at[rows], sems.at[len(copies)]))
            copies[-1].start()
    for copy in copies:
        copy.wait()


def wide_final(own_ref, other_ref, out_ref, *more):
    work_ref, sems = more[-2:]
    width, wide = out_ref.shape
    step = own_ref.shape[1]
    copies = []
    for place, ref in places(own_ref, other_ref):
        for at in range(wide // 2 // step):
            lanes = pl.ds(pl.multiple_of(place * (wide // 2) + at * step, step), step)
            work_ref[:, lanes] = ref[at * width : (at + 1) * width].astype(F32)
            copies.append(pltpu.make_async_copy(work_ref.at[:, lanes], out_ref.at[:, lanes], sems.at[len(copies)]))
            copies[-1].start()
        if len(more) > 2:
            half = width // 2
            more[1][pl.ds(pl.multiple_of(place * half, half), half)] = ref[wide // 2 // step * width :].astype(F32)
    if len(more) > 2:
        copies.append(pltpu.make_async_copy(more[1], more[0], sems.at[len(copies)]))
        copies[-1].start()
    for copy in copies:
        copy.wait()


def rest_final(own_ref, other_ref, q_ref, k_ref, v_ref, bog_ref, fgg_ref, gg_ref):
    width = q_ref.shape[0]
    half = width // 2
    for place, ref in places(own_ref, other_ref):
        lanes = pl.ds(pl.multiple_of(place * half, half), half)
        for at, out in enumerate((q_ref, k_ref, v_ref)):
            out[:, lanes] = ref[at * width : (at + 1) * width].astype(F32)
    own, other = (ref[3 * width : 3 * width + 16].astype(F32) for ref in (own_ref, other_ref))
    core = lax.axis_index("batch") & 1
    zero, one = jnp.where(core == 0, own, other), jnp.where(core == 0, other, own)
    count = bog_ref.shape[0] // half
    for out, rows, first in ((bog_ref, zero, 0), (fgg_ref, zero, count), (gg_ref, one, 0)):
        for at in range(out.shape[0] // half):
            out[at * half : (at + 1) * half] = rows[first + at]


def add_back_kernel(part_ref, returned_ref, out_ref):
    out_ref[...] = part_ref[...] + returned_ref[...].astype(F32)


def call(kernel, operands, results, scratch=(), limit=6, outside=0):
    nbytes = sum(a.size * a.dtype.itemsize for a in operands) + sum(
        math.prod(s) * jnp.dtype(d).itemsize for s, d in results
    )
    return pl.pallas_call(
        kernel,
        out_shape=tuple(jax.ShapeDtypeStruct(s, d) for s, d in results),
        in_specs=[VMEM] * len(operands),
        out_specs=tuple(HBM if i < outside else VMEM for i in range(len(results))),
        scratch_shapes=list(scratch),
        compiler_params=pltpu.CompilerParams(vmem_limit_bytes=limit * MEGA),
        cost_estimate=pl.CostEstimate(flops=STEP_FLOPS, bytes_accessed=nbytes, transcendentals=0),
    )(*operands)


def exchanges(batches, blocks):
    number = batches * blocks

    def pairs(partner):
        return [
            (d, p[0] * blocks + p[1])
            for d in range(number)
            for p in [partner(d // blocks, d % blocks)]
        ]

    flips = {
        "x": (lambda b, s: (b, s ^ 1), lambda b, s: s),
        "y": (lambda b, s: (b ^ 2, s), lambda b, s: (b & 2) // 2),
        "z": (lambda b, s: (b ^ 4, s), lambda b, s: (b & 4) // 4),
    }

    def flip(place):
        return (pairs(lambda b, s: (b ^ place, s)), lambda b, s: (b & place) // place)

    def mixed(way):
        (first, first_bit), (second, second_bit) = (flips[axis] for axis in way)
        return (
            pairs(lambda b, s: second(b, s) if b % 2 else first(b, s)),
            lambda b, s: jnp.where(b & 1 == 0, first_bit(b, s), second_bit(b, s)),
        )

    found = {way: mixed(way) for way in ("xy", "yx", "zy", "yz", "xz", "zx", "xx", "yy", "zz")}
    found["core"] = flip(1)
    rest = []
    place = 8
    while place < batches:
        rest.append(flip(place))
        place *= 2
    return found, rest


def added(left, right, rows):
    return (left[rows].astype(F32) + right[rows].astype(F32)).astype(BF16)


def halve_kernel(bit, kept_ref, arrived_ref, sent_ref, left_ref):
    half, mine = sent_ref.shape[0], bit(lax.axis_index("batch"), lax.axis_index("seq"))
    step = 16 * math.gcd(half // 16, 8)
    for place, ref in ((1 - mine, sent_ref), (mine, left_ref)):
        for at in range(0, half, step):
            rows = pl.ds(pl.multiple_of(place * half + at, 16), step)
            ref[at : at + step] = added(kept_ref, arrived_ref, rows)


def add_kernel(kept_ref, arrived_ref, out_ref):
    half = out_ref.shape[0]
    step = 16 * math.gcd(half // 16, 8)
    for at in range(0, half, step):
        out_ref[at : at + step] = added(kept_ref, arrived_ref, slice(at, at + step))


def double_kernel(bit, kept_ref, arrived_ref, out_ref):
    half, mine = kept_ref.shape[0], bit(lax.axis_index("batch"), lax.axis_index("seq"))
    for place, ref in ((mine, kept_ref), (1 - mine, arrived_ref)):
        out_ref[pl.ds(pl.multiple_of(place * half, 16), half)] = ref[...]


def choose_kernel(bit, kept0_ref, arrived0_ref, kept1_ref, arrived1_ref, sent_ref, left_ref):
    mine = bit(lax.axis_index("batch"), lax.axis_index("seq"))
    step = 128
    for at in range(0, sent_ref.shape[0], step):
        rows = slice(at, at + step)
        zero, one = added(kept0_ref, arrived0_ref, rows), added(kept1_ref, arrived1_ref, rows)
        left_ref[rows] = jnp.where(mine == 0, zero, one)
        sent_ref[rows] = jnp.where(mine == 0, one, zero)


def pick_kernel(bit, zero_ref, one_ref, sent_ref, left_ref):
    mine = bit(lax.axis_index("batch"), lax.axis_index("seq"))

    @pl.when(mine == 0)
    def _():
        left_ref[...] = zero_ref[...]
        sent_ref[...] = one_ref[...]

    @pl.when(mine != 0)
    def _():
        left_ref[...] = one_ref[...]
        sent_ref[...] = zero_ref[...]


class Sum:
    def __init__(self, halvings, fulls, sent, kept, finish):
        self.halvings, self.fulls, self.finish = halvings, fulls, finish
        self.sent, self.kept, self.arrived, self.at = sent, kept, None, 0

    def start(self, exchange):
        self.arrived = lax.ppermute(self.sent, AXES, exchange[0])

    def add(self):
        (self.kept,) = call(add_kernel, (self.kept, self.arrived), [(self.kept.shape, BF16)])
        self.sent = self.kept

    def advance(self, *after):
        count, at = len(self.halvings), self.at
        self.at += 1
        if at == 0:
            self.sent = fence(self.sent, *after)[0]
            self.start(self.halvings[0])
            return self.sent
        self.kept = fence(self.kept, *after)[0]
        rows, columns = self.kept.shape
        if at < count:
            self.sent, self.kept = call(
                functools.partial(halve_kernel, self.halvings[at][1]),
                (self.kept, self.arrived),
                [((rows // 2, columns), BF16)] * 2,
            )
            self.start(self.halvings[at])
        elif at == count:
            self.add()
            self.start(self.fulls[0])
        elif at == count + 1:
            for exchange in self.fulls[1:]:
                self.add()
                self.start(exchange)
            self.add()
            self.start(self.halvings[-1])
        elif at <= 2 * count:
            (self.kept,) = call(
                functools.partial(double_kernel, self.halvings[2 * count + 1 - at + 0][1]),
                (self.kept, self.arrived),
                [((rows * 2, columns), BF16)],
            )
            self.sent = self.kept
            self.start(self.halvings[2 * count - at])
        else:
            self.result = self.finish(self.kept, self.arrived)
            return self.result[0]
        return self.sent


def fence(*arrays):
    return lax.optimization_barrier(arrays)


def body(
    inputs,
    memory,
    cotangent,
    labels,
    attention_gain,
    query_weight,
    key_weight,
    value_weight,
    out_weight,
    forward_gain,
    up_weight,
    down_weight,
    boundary_hidden,
    boundary_out,
):
    group, block, width = inputs.shape
    wide, hidden_wide = up_weight.shape[1], boundary_hidden.shape[1]
    batches, blocks = (lax.axis_size("batch"), lax.axis_size("seq"))
    found, fulls = exchanges(batches, blocks)
    column = lax.axis_index("seq")
    core = lax.axis_index("batch") % 2
    rows = inputs.reshape(block, width)
    memory_rows = memory.reshape(block, width)
    onward = [(i, i + 1) for i in range(blocks - 1)]
    side1 = lax.ppermute(rows[TILE:], "seq", onward)
    tables = rotary_tables(-block, (blocks + 1) * block)
    cosine, sine = (
        lax.dynamic_slice_in_dim(jnp.asarray(t), column * block, 2 * block) for t in tables
    )
    gain = attention_gain.reshape(1, width)
    square, side_shape = (block, width), (TILE, width)
    turned_square, turned_side = (width, block), (width, TILE)
    normed_t, queries, queries_t, keys, keys_t, values, values_t = call(
        own_kernel,
        (rows, gain, query_weight, key_weight, value_weight, cosine, sine),
        [(turned_square, BF16), (square, BF16), (turned_square, BF16)]
        + [(square, BF16), (turned_square, BF16)] * 2,
    )
    side0 = lax.ppermute(fence(rows, queries)[0][:TILE], "seq", onward)
    side_results = [
        (side_shape, BF16), (side_shape, BF16), (side_shape, BF16), (turned_side, BF16),
        ((HEADS, 2 * TILE, TILE), BF16), (turned_side, BF16),
    ]
    sn1, sk1, sv1, sv_t1, weights1, mix1 = call(
        late_kernel,
        (memory_rows, side1, gain, key_weight, value_weight, cosine, sine, queries_t, keys, values_t),
        side_results,
    )
    sn0, sk0, sv0, sv_t0, weights0, mix0 = call(
        early_kernel,
        (memory_rows, side0, gain, key_weight, value_weight, cosine, sine, queries_t, keys, values_t, sk1, sv_t1),
        side_results,
    )
    bh_half = (hidden_wide // 2 * width // 512, 512)
    (
        hidden, normed_hidden, gated, slope, outputs, probe_grad, hidden_sent, hidden_kept, probe, signal,
    ) = call(
        forward_kernel,
        (
            rows, mix0, mix1, out_weight, forward_gain.reshape(1, width), up_weight, down_weight,
            boundary_hidden, boundary_out.reshape(1, hidden_wide), labels,
        ),
        [
            (square, F32), (square, BF16), ((block, wide), BF16),
            ((block, wide), BF16), (square, BF16), ((block, hidden_wide), BF16),
            (bh_half, BF16), (bh_half, BF16), ((block, hidden_wide), BF16), ((block, PAIR), F32),
        ],
        [
            pltpu.VMEM((block, hidden_wide), BF16),
            pltpu.VMEM((width, block), BF16),
        ],
        limit=18,
    )
    sums, made = {}, {}

    def add_sum(name, way, sent, kept, finish):
        sums[name] = Sum([found[w] for w in way], fulls, sent, kept, finish)

    add_sum(
        "hidden", ("core", "xy", "yx", "zz"), hidden_sent, hidden_kept,
        lambda own, other: call(
            wide_final, (own, other), [((width, hidden_wide), F32)],
            [pltpu.VMEM((width, hidden_wide), F32), pltpu.SemaphoreType.DMA((4,))], outside=1,
        ),
    )
    up_half = (wide // 2 * width // 512 + width // 2, 512)
    grads_shape = ((3 * width + 128, width // 2), BF16)
    work = [
        pltpu.VMEM((width // 2, block), F32),
        pltpu.VMEM((2 * block, width // 2), F32),
        pltpu.VMEM((2 * block, width // 2), BF16),
    ]
    def down_part(*after):
        grad = fence(probe_grad, *after)[0]
        final_grad, up_grad, sent, kept, boundary_out_grad, sn_t0, sn_t1, sk_t0, sk_t1 = call(
            down_kernel,
            (
                grad, boundary_hidden, cotangent.reshape(square), gated, slope, down_weight, probe, signal,
                sn0, sn1, sk0, sk1,
            ),
            [(square, F32), ((block, wide), BF16), ((wide // 2, width), BF16), ((wide // 2, width), BF16)]
            + [((1, hidden_wide), F32)] + [(turned_side, BF16)] * 4,
        )
        made["down"] = (final_grad, up_grad, boundary_out_grad)
        made["shared"] = (
            queries, sv0, sv1, values, sk_t0, sk_t1, keys_t,
            cosine, sine, normed_t, sn_t0, sn_t1, query_weight, key_weight, value_weight,
        )
        add_sum(
            "down", ("core", "zz", "xy", "yx"), sent, kept,
            lambda own, other: call(
                tall_final, (own, other), [((wide, width), F32)],
                [pltpu.VMEM((wide, width), F32), pltpu.SemaphoreType.DMA((4,))], outside=1,
            ),
        )
        return up_grad

    def up_part(*after):
        final_grad, up_grad, _ = made["down"]
        up_grad = fence(up_grad, *after)[0]
        hidden_grad, mixed_grad, mixed_grad_t, gain_part, sent, kept = call(
            up_kernel,
            (
                normed_hidden, up_grad, up_weight, hidden, forward_gain.reshape(1, width), final_grad,
                mix0, mix1, out_weight,
            ),
            [
                (square, F32), (square, BF16), (turned_square, BF16), ((1, width), F32),
                (up_half, BF16), (up_half, BF16),
            ],
            [pltpu.VMEM((width, block), BF16), pltpu.VMEM((width, block), BF16)],
        )
        made["up"] = (hidden_grad, (weights0, weights1, mixed_grad, mixed_grad_t) + made["shared"], gain_part)
        add_sum(
            "up", ("core", "xy", "yx", "zz"), sent, kept,
            lambda own, other: call(
                wide_final, (own, other), [((width, wide), F32), ((width, width), F32)],
                [pltpu.VMEM((width, width), F32), pltpu.VMEM((width, wide), F32), pltpu.SemaphoreType.DMA((5,))],
                outside=2,
            ),
        )
        return mixed_grad

    def attention0(*after):
        hidden_grad, operands, gain_part = made["up"]
        operands = (fence(weights0, *after)[0],) + operands[1:]
        made["attention"] = call(
            functools.partial(attention_kernel, 0, False),
            operands + (made["down"][2], gain_part),
            [(square, F32), (square, F32), grads_shape],
            work,
            limit=10,
        )
        return made["attention"][0]

    def attention1(*after):
        hidden_grad, operands, _ = made["up"]
        upstream, side_upstream, grads0 = made["attention"]
        upstream = fence(upstream, *after)[0]
        input_part, side_grad, grads1 = call(
            functools.partial(attention_kernel, 1, True),
            operands + (rows, memory_rows, side0, side1, gain, hidden_grad, upstream, side_upstream),
            [(square, F32), (square, BF16), grads_shape],
            work,
            limit=10,
        )
        made["input"] = (input_part, side_grad)
        picked = call(
            functools.partial(pick_kernel, found["core"][1]), (grads0, grads1), [grads_shape] * 2
        )
        add_sum(
            "rest", ("core", "xy", "yx", "zz"), *picked,
            lambda own, other: call(
                rest_final, (own, other), [((width, width), F32)] * 3 + [((hidden_wide,), F32), ((width,), F32), ((width,), F32)],
            ),
        )
        return picked[0]

    def send_back(*after):
        input_part, side_grad = made["input"]
        side_grad = fence(side_grad, *after)[0]
        made["returned"] = lax.ppermute(side_grad, "seq", [(i + 1, i) for i in range(blocks - 1)])
        return side_grad

    def add_back(*after):
        input_part = fence(made["input"][0], *after)[0]
        (made["input_grad"],) = call(add_back_kernel, (input_part, made["returned"]), [(square, F32)])
        return made["input_grad"]

    parts = {
        "a": down_part, "b": up_part, "c": attention0, "d": attention1, "r": send_back, "s": add_back,
    }
    names = {"H": "hidden", "D": "down", "U": "up", "T": "rest"}
    token = hidden_kept
    for letter in ORDER:
        token = parts[letter](token) if letter in parts else sums[names[letter]].advance(token)
    (hidden_total,), (down_total,) = (sums["hidden"].result, sums["down"].result)
    up_total, out_total = sums["up"].result
    query_total, key_total, value_total, boundary_out_total, forward_gain_total, gain_total = sums["rest"].result
    input_grad = made["input_grad"]
    return (
        outputs.reshape(inputs.shape),
        input_grad.reshape(inputs.shape),
        gain_total,
        query_total,
        key_total,
        value_total,
        out_total,
        forward_gain_total,
        up_total,
        down_total,
        hidden_total,
        boundary_out_total,
    )


def solution(mesh):
    placed = (
        P("batch", "seq", None),
        P("batch", None, None),
        P("batch", "seq", None),
        P("batch", "seq"),
        P(),
        P(),
        P(),
        P(),
        P(),
        P(),
        P(),
        P(),
        P(),
        P(),
    )
    return jax.shard_map(
        body,
        mesh=mesh,
        in_specs=placed,
        out_specs=(
            P("batch", "seq", None),
            P("batch", "seq", None),
            P(),
            P(),
            P(),
            P(),
            P(),
            P(),
            P(),
            P(),
            P(),
            P(),
        ),
        check_vma=False,
    )
```

```python
import functools
import math

import jax
import jax.numpy as jnp
import numpy as np
from jax import lax
from jax.experimental import pallas as pl
from jax.experimental.pallas import tpu as pltpu
from jax.sharding import PartitionSpec as P

HEADS = 8
HEAD = 64
PAIR = 2 * HEAD
TILE = 256
EPS = 1e-05
BASE = 10000.0
AXES = ("batch", "seq")
F32, BF16 = jnp.float32, jnp.bfloat16
VMEM = pl.BlockSpec(memory_space=pltpu.VMEM)
HBM = pl.BlockSpec(memory_space=pl.ANY)
STEP_FLOPS = int(2e10)
MEGA = 1024 * 1024
ORDER = "HaHDbUcUDHdUTHDTHDUTDrHUTDHTUDHUTDTUHTsDHUDTUT"


def dot(left, right):
    return jnp.dot(left, right, preferred_element_type=F32)


def dot_t(left, right):
    return lax.dot_general(left, right, (((1,), (1,)), ((), ())), preferred_element_type=F32)


def t_dot(left, right):
    return lax.dot_general(left, right, (((0,), (0,)), ((), ())), preferred_element_type=F32)


def normalised(values):
    centre = values - jnp.mean(values, axis=-1, keepdims=True)
    spread = jnp.mean(centre * centre, axis=-1, keepdims=True)
    scale = lax.rsqrt(spread + EPS)
    return centre * scale, scale


def norm_back(unit, scale, gain, upstream):
    product = upstream * unit
    inner = upstream * gain
    mean = jnp.mean(inner, axis=-1, keepdims=True)
    along = jnp.mean(inner * unit, axis=-1, keepdims=True)
    return scale * (inner - mean - unit * along), jnp.sum(product, axis=0, keepdims=True)


def gelu_both(value):
    factor = math.sqrt(2.0 / math.pi)
    square = value * value
    half = 0.5 + 0.5 * jnp.tanh(value * (factor + (factor * 0.044715) * square))
    result = value * half
    bend = (result - result * half) * (2.0 * factor + (6.0 * factor * 0.044715) * square)
    return result, half + bend


def turned(values, cosine, sine):
    front = lax.broadcasted_iota(jnp.int32, (values.shape[0], PAIR), 1) % HEAD < HEAD // 2
    parts = []
    for at in range(0, values.shape[1], PAIR):
        part = values[:, at : at + PAIR]
        other = jnp.where(
            front, pltpu.roll(part, PAIR - HEAD // 2, 1), pltpu.roll(part, HEAD // 2, 1)
        )
        parts.append(part * cosine + other * sine)
    return jnp.concatenate(parts, axis=1)


def rotary_tables(first, count):
    positions = np.arange(first, first + count, dtype=np.float32)
    half = HEAD // 2
    freqs = np.float32(BASE) ** (-(np.arange(half, dtype=np.float32) * np.float32(2.0 / HEAD)))
    angles = (positions[:, None] * freqs[None, :].astype(np.float32)).astype(np.float64)
    cosine, sine = (np.cos(angles), np.sin(angles))
    return (
        np.concatenate([cosine] * 4, axis=1).astype(np.float32),
        np.concatenate([-sine, sine] * 2, axis=1).astype(np.float32),
    )


def own_kernel(
    x_ref, gain_ref, wq_ref, wk_ref, wv_ref, cos_ref, sin_ref,
    nt_ref, q_ref, qt_ref, k_ref, kt_ref, v_ref, vt_ref,
):
    unit, _ = normalised(x_ref[...].astype(F32))
    low = (unit * gain_ref[...]).astype(BF16)
    nt_ref[...] = jnp.transpose(low)
    block = low.shape[0]
    cosine, sine = cos_ref[block:], sin_ref[block:]
    scale = 1.0 / math.sqrt(HEAD)
    query = turned(dot(low, wq_ref[...]), cosine, sine).astype(BF16).astype(F32) * scale
    query = query.astype(BF16)
    q_ref[...] = query
    qt_ref[...] = jnp.transpose(query)
    key = turned(dot(low, wk_ref[...]), cosine, sine).astype(BF16)
    k_ref[...] = key
    kt_ref[...] = jnp.transpose(key)
    value = dot(low, wv_ref[...]).astype(BF16)
    v_ref[...] = value
    vt_ref[...] = jnp.transpose(value)


def before_diagonal():
    key = lax.broadcasted_iota(jnp.int32, (TILE, TILE), 0)
    return key <= lax.broadcasted_iota(jnp.int32, (TILE, TILE), 1)


def halves(array, seen):
    none = jnp.zeros_like(array)
    return jnp.where(seen, none, array), jnp.where(seen, array, none)


def attend(q_t, keys, values_t, w_ref, mix_ref):
    seen = before_diagonal()
    pairs = mix_ref.shape[0] // PAIR

    def one_pair(pair, carry):
        lanes = pl.ds(pl.multiple_of(pair * PAIR, PAIR), PAIR)
        both = q_t(lanes)
        row = lax.broadcasted_iota(jnp.int32, both.shape, 0)
        for head in range(2):
            query = jnp.where(row // HEAD == head, both, jnp.zeros_like(both))
            first, middle, last = [dot(block(lanes), query) for block in keys]
            edge = jnp.where(seen, last, first)
            peak = jnp.maximum(
                jnp.max(edge, axis=0, keepdims=True), jnp.max(middle, axis=0, keepdims=True)
            )
            edge, middle = jnp.exp(edge - peak), jnp.exp(middle - peak)
            total = jnp.sum(edge + middle, axis=0, keepdims=True)
            edge, middle = (edge / total).astype(BF16), (middle / total).astype(BF16)
            w_ref[2 * pair + head, :TILE] = edge
            w_ref[2 * pair + head, TILE:] = middle
            own = pl.ds(pl.multiple_of(pair * PAIR + head * HEAD, HEAD), HEAD)
            left, right = halves(edge, seen)
            mix = dot(values_t[0](own), left) + dot(values_t[1](own), middle)
            mix_ref[own] = (mix + dot(values_t[2](own), right)).astype(BF16)
        return carry

    lax.fori_loop(0, pairs, one_pair, 0, unroll=pairs)


def side_rows(memory_ref, received_ref):
    return jnp.where(lax.axis_index("seq") == 0, memory_ref[...], received_ref[...]).astype(F32)


def side_part(memory_ref, received_ref, gain_ref, wk_ref, wv_ref, cos_ref, sin_ref, sn_ref, k_ref, v_ref, vt_ref):
    unit, _ = normalised(side_rows(memory_ref, received_ref))
    low = (unit * gain_ref[...]).astype(BF16)
    sn_ref[...] = low
    key = turned(dot(low, wk_ref[...]), cos_ref[...], sin_ref[...]).astype(BF16)
    k_ref[...] = key
    value = dot(low, wv_ref[...]).astype(BF16)
    v_ref[...] = value
    vt_ref[...] = jnp.transpose(value)


def late_kernel(
    memory_ref, received_ref, gain_ref, wk_ref, wv_ref, cos_ref, sin_ref, qt_ref, ok_ref, ovt_ref,
    sn_ref, k_ref, v_ref, vt_ref, w_ref, mix_ref,
):
    side_part(
        memory_ref.at[TILE:], received_ref, gain_ref, wk_ref, wv_ref, cos_ref.at[TILE : 2 * TILE], sin_ref.at[TILE : 2 * TILE],
        sn_ref, k_ref, v_ref, vt_ref,
    )
    attend(
        lambda at: qt_ref[at, TILE:],
        (lambda at: k_ref[:, at], lambda at: ok_ref[:TILE, at], lambda at: ok_ref[TILE:, at]),
        (lambda at: vt_ref[at], lambda at: ovt_ref[at, :TILE], lambda at: ovt_ref[at, TILE:]),
        w_ref,
        mix_ref,
    )


def early_kernel(
    memory_ref, received_ref, gain_ref, wk_ref, wv_ref, cos_ref, sin_ref, qt_ref, ok_ref, ovt_ref, sk_ref, svt_ref,
    sn_ref, k_ref, v_ref, vt_ref, w_ref, mix_ref,
):
    side_part(
        memory_ref.at[:TILE], received_ref, gain_ref, wk_ref, wv_ref, cos_ref.at[:TILE], sin_ref.at[:TILE],
        sn_ref, k_ref, v_ref, vt_ref,
    )
    attend(
        lambda at: qt_ref[at, :TILE],
        (lambda at: k_ref[:, at], lambda at: sk_ref[:, at], lambda at: ok_ref[:TILE, at]),
        (lambda at: vt_ref[at], lambda at: svt_ref[at], lambda at: ovt_ref[at, :TILE]),
        w_ref,
        mix_ref,
    )


def forward_kernel(
    x_ref, mix0_ref, mix1_ref, wo_ref, fgain_ref, up_ref, down_ref, bh_ref, bo_ref, labels_ref,
    hidden_ref, nh_ref, gated_ref, slope_ref, out_ref, pg_ref, sent_ref, kept_ref, probe_ref, signal_ref,
    pslope_ref, turn_ref,
):
    block, width = x_ref.shape
    mixed = jnp.concatenate([jnp.transpose(mix0_ref[...]), jnp.transpose(mix1_ref[...])], axis=0)
    hidden = x_ref[...].astype(F32) + dot(mixed, wo_ref[...])
    hidden_ref[...] = hidden
    unit, _ = normalised(hidden)
    low = (unit * fgain_ref[...]).astype(BF16)
    nh_ref[...] = low
    step = 1024
    tops = [slice(top, top + TILE) for top in range(0, block, TILE)]
    for part_rows in tops:
        part = hidden[part_rows]
        for at in range(0, up_ref.shape[1], step):
            gated, slope = gelu_both(dot(low[part_rows], up_ref[:, at : at + step]))
            gated = gated.astype(BF16)
            gated_ref[part_rows, at : at + step] = gated
            slope_ref[part_rows, at : at + step] = slope.astype(BF16)
            part = part + dot(gated, down_ref[at : at + step])
        out_ref[part_rows] = part.astype(BF16)
    out = out_ref[...]
    turn_ref[...] = jnp.transpose(out)
    logits = []
    for part_rows in tops:
        logit = jnp.zeros((TILE, 1), F32)
        for at in range(0, bh_ref.shape[1], step):
            probe, slope = gelu_both(dot(out[part_rows], bh_ref[:, at : at + step]))
            probe = probe.astype(BF16)
            probe_ref[part_rows, at : at + step] = probe
            pslope_ref[part_rows, at : at + step] = slope.astype(BF16)
            logit = logit + jnp.sum(
                probe.astype(F32) * bo_ref[:, at : at + step].astype(F32), axis=-1, keepdims=True
            )
        logits.append(logit)
    logits = jnp.concatenate(logits, axis=0)
    targets = jnp.transpose(jnp.broadcast_to(labels_ref[...].astype(F32), (PAIR, block)))[:, :1]
    signal = (jax.nn.sigmoid(logits) - targets).astype(BF16).astype(F32)
    step = 512
    half = bh_ref.shape[1] // 2
    core = lax.axis_index("batch") & 1
    for at in range(0, bh_ref.shape[1], step):
        grad = pslope_ref[:, at : at + step].astype(F32) * (
            signal * bo_ref[:, at : at + step].astype(F32)
        )
        pg_ref[:, at : at + step] = grad.astype(BF16)
    for place, ref in ((1 - core, sent_ref), (core, kept_ref)):
        for at in range(0, half, step):
            grad = pg_ref[:, pl.ds(pl.multiple_of(place * half + at, step), step)]
            ref[at * width // step : (at + step) * width // step] = dot(turn_ref[...], grad).astype(BF16)
    signal_ref[...] = jnp.broadcast_to(signal, signal_ref.shape)


def down_kernel(
    pg_ref, bh_ref, cot_ref, gated_ref, slope_ref, down_ref, probe_ref, signal_ref, sn0_ref, sn1_ref, sk0_ref, sk1_ref,
    grad_ref, upg_ref, sent_ref, kept_ref, bog_ref, snt0_ref, snt1_ref, skt0_ref, skt1_ref,
):
    final = cot_ref[...].astype(F32) + dot_t(pg_ref[...], bh_ref[...])
    grad_ref[...] = final
    low = final.astype(BF16)
    step = 512
    half = down_ref.shape[0] // 2
    core = lax.axis_index("batch") & 1
    for at in range(0, half, step):
        rows = pl.ds(pl.multiple_of((1 - core) * half + at, step), step)
        sent_ref[at : at + step] = t_dot(gated_ref[:, rows], low).astype(BF16)
    for at in range(0, half, step):
        rows = pl.ds(pl.multiple_of(core * half + at, step), step)
        kept_ref[at : at + step] = t_dot(gated_ref[:, rows], low).astype(BF16)
    for at in range(0, down_ref.shape[0], step):
        part = slope_ref[:, at : at + step].astype(F32) * dot_t(low, down_ref[at : at + step])
        upg_ref[:, at : at + step] = part.astype(BF16)
    signal = signal_ref[:, :1]
    for at in range(0, bog_ref.shape[1], step):
        bog_ref[:, at : at + step] = jnp.sum(
            signal * probe_ref[:, at : at + step].astype(F32), axis=0, keepdims=True
        )
    for ref, turned_ref in (
        (sn0_ref, snt0_ref), (sn1_ref, snt1_ref), (sk0_ref, skt0_ref), (sk1_ref, skt1_ref)
    ):
        turned_ref[...] = jnp.transpose(ref[...])


def up_kernel(
    nh_ref, upg_ref, up_ref, hidden_ref, fgain_ref, grad_ref, mix0_ref, mix1_ref, wo_ref,
    hg_ref, mg_ref, mgt_ref, fgg_ref, sent_ref, kept_ref, nht_ref, mixt_ref,
):
    width, wide = up_ref.shape
    nht_ref[...] = jnp.transpose(nh_ref[...])
    mixt_ref[:, :TILE] = mix0_ref[...]
    mixt_ref[:, TILE:] = mix1_ref[...]
    upstream = dot_t(upg_ref[...], up_ref[...])
    unit, scale = normalised(hidden_ref[...])
    part, gain_part = norm_back(unit, scale, fgain_ref[...], upstream)
    fgg_ref[...] = gain_part
    total = grad_ref[...] + part
    hg_ref[...] = total
    low = total.astype(BF16)
    mixed_grad = dot_t(low, wo_ref[...]).astype(BF16)
    mg_ref[...] = mixed_grad
    mgt_ref[...] = jnp.transpose(mixed_grad)
    core = lax.axis_index("batch") & 1
    half, step = wide // 2, 512
    for place, ref in ((1 - core, sent_ref), (core, kept_ref)):
        for at in range(0, half, step):
            grad = upg_ref[:, pl.ds(pl.multiple_of(place * half + at, step), step)]
            ref[at * width // step : (at + step) * width // step] = dot(nht_ref[...], grad).astype(BF16)
        rows = pl.ds(pl.multiple_of(place * (width // 2), width // 2), width // 2)
        ref[half * width // step :] = dot(mixt_ref[rows], low).astype(BF16)


def attend_back(start, pair, tile, w_ref, mg_ref, mgt_ref, q_ref, values, keys_t, dq_ref, dks, dvs):
    seen = before_diagonal()
    lanes = pl.ds(pl.multiple_of((start + pair) * PAIR, PAIR), PAIR)
    rows = slice(tile * TILE, (tile + 1) * TILE)
    upstream_t, upstream, query = mgt_ref[lanes, rows], mg_ref[rows, lanes], q_ref[rows, lanes]
    row = lax.broadcasted_iota(jnp.int32, (PAIR, TILE), 0)
    lane = lax.broadcasted_iota(jnp.int32, (TILE, PAIR), 1)
    none, none_t = jnp.zeros_like(upstream), jnp.zeros_like(upstream_t)
    for head in range(2):
        above_t = jnp.where(row // HEAD == head, upstream_t, none_t)
        first, middle_grad, last = [dot(block[:, lanes], above_t) for block in values]
        edge_grad = jnp.where(seen, last, first)
        weights = w_ref[2 * (start + pair) + head]
        edge, middle = weights[:TILE].astype(F32), weights[TILE:].astype(F32)
        centred = jnp.sum(edge * edge_grad + middle * middle_grad, axis=0, keepdims=True)
        edge = (edge * (edge_grad - centred)).astype(BF16)
        middle = (middle * (middle_grad - centred)).astype(BF16)
        left, right = halves(edge, seen)
        above = jnp.where(lane // HEAD == head, upstream, none)
        one = jnp.where(lane // HEAD == head, query, none)
        own = pl.ds(pl.multiple_of((start + pair) * PAIR + head * HEAD, HEAD), HEAD)
        grad = dot(keys_t[0][own], left) + dot(keys_t[1][own], middle) + dot(keys_t[2][own], right)
        dq_ref[pl.ds(pl.multiple_of(pair * PAIR + head * HEAD, HEAD), HEAD), rows] = grad
        w_left, w_right = halves(weights[:TILE], seen)
        for place, part in enumerate((left, middle, right)):
            dks[place] = dks[place] + dot(part, one)
        for place, part in enumerate((w_left, weights[TILE:], w_right)):
            dvs[place] = dvs[place] + dot(part, above)


def rows_of(*smalls):
    rows = [s[:, at : at + TILE] for s in smalls for at in range(0, s.shape[1], TILE)]
    rows.append(jnp.zeros((128 - len(rows), TILE), F32))
    return jnp.concatenate(rows, axis=0).astype(BF16)


def attention_kernel(
    part, final, w0_ref, w1_ref, mg_ref, mgt_ref, q_ref, sv0_ref, sv1_ref, v_ref, skt0_ref, skt1_ref, kt_ref,
    cos_ref, sin_ref, nt_ref, snt0_ref, snt1_ref, wq_ref, wk_ref, wv_ref, *rest,
):
    if final:
        x_ref, memory_ref, side0_ref, side1_ref, gain_ref, hg_ref, up_ref, sup_ref, ig_ref, sg_ref, grads_ref, dq_ref, dk_ref, dv_ref = rest
    else:
        bog_ref, fgg_ref, nup_ref, nsup_ref, grads_ref, dq_ref, dk_ref, dv_ref = rest
    block, width = q_ref.shape
    pairs = width // PAIR // 2
    values = (sv0_ref, sv1_ref, v_ref.at[:TILE], v_ref.at[TILE:])
    keys_t = (skt0_ref, skt1_ref, kt_ref.at[:, :TILE], kt_ref.at[:, TILE:])

    def one_pair(pair, carry):
        dk, dv = [0.0] * 4, [0.0] * 4
        for tile, w_ref in ((1, w1_ref), (0, w0_ref)):
            dks, dvs = dk[tile : tile + 3], dv[tile : tile + 3]
            attend_back(
                part * pairs, pair, tile, w_ref, mg_ref, mgt_ref, q_ref, values[tile : tile + 3],
                keys_t[tile : tile + 3], dq_ref, dks, dvs,
            )
            dk[tile : tile + 3], dv[tile : tile + 3] = dks, dvs
        inside = pl.ds(pl.multiple_of(pair * PAIR, PAIR), PAIR)
        for place in range(4):
            dk_ref[place * TILE : (place + 1) * TILE, inside] = dk[place]
            dv_ref[place * TILE : (place + 1) * TILE, inside] = dv[place].astype(BF16)
        return carry

    lax.fori_loop(0, pairs, one_pair, 0)
    dk = [dk_ref[place * TILE : (place + 1) * TILE] for place in range(4)]
    dv = [dv_ref[place * TILE : (place + 1) * TILE] for place in range(4)]
    lanes = slice(part * (width // 2), (part + 1) * (width // 2))
    scale = 1.0 / math.sqrt(HEAD)
    cosine, sine = cos_ref[...], -sin_ref[...]
    dq = turned(jnp.transpose(dq_ref[...]) * scale, cosine[block:], sine[block:]).astype(BF16)
    dk = [
        turned(p, cosine[i * TILE : (i + 1) * TILE], sine[i * TILE : (i + 1) * TILE]).astype(BF16)
        for i, p in enumerate(dk)
    ]
    own_k, own_v = jnp.concatenate(dk[2:], axis=0), jnp.concatenate(dv[2:], axis=0)
    side_k, side_v = jnp.concatenate(dk[:2], axis=0), jnp.concatenate(dv[:2], axis=0)
    rows_t = nt_ref[...]
    side_t = jnp.concatenate([snt0_ref[...], snt1_ref[...]], axis=1)
    grads_ref[:width] = dot(rows_t, dq).astype(BF16)
    grads_ref[width : 2 * width] = (dot(rows_t, own_k) + dot(side_t, side_k)).astype(BF16)
    grads_ref[2 * width : 3 * width] = (dot(rows_t, own_v) + dot(side_t, side_v)).astype(BF16)
    wk, wv = wk_ref[:, lanes], wv_ref[:, lanes]
    upstream = dot_t(dq, wq_ref[:, lanes]) + dot_t(own_k, wk) + dot_t(own_v, wv)
    side_up = dot_t(side_k, wk) + dot_t(side_v, wv)
    if not final:
        grads_ref[3 * width :] = rows_of(bog_ref[...], fgg_ref[...])
        nup_ref[...] = upstream
        nsup_ref[...] = side_up
        return
    upstream = upstream + up_ref[...]
    side_up = side_up + sup_ref[...]
    unit, spread = normalised(x_ref[...].astype(F32))
    back, gain_part = norm_back(unit, spread, gain_ref[...], upstream)
    ig_ref[...] = hg_ref[...] + back
    for i, ref in enumerate((side0_ref, side1_ref)):
        at = slice(i * TILE, (i + 1) * TILE)
        unit, spread = normalised(side_rows(memory_ref.at[at], ref))
        back, side_gain = norm_back(unit, spread, gain_ref[...], side_up[at])
        sg_ref[at] = back.astype(BF16)
        gain_part = gain_part + side_gain
    grads_ref[3 * width :] = rows_of(gain_part)


def places(own_ref, other_ref):
    core = lax.axis_index("batch") & 1
    return ((core, own_ref), (1 - core, other_ref))


def tall_final(own_ref, other_ref, out_ref, work_ref, sems):
    half = own_ref.shape[0]
    copies = []
    for number, (place, ref) in enumerate(places(own_ref, other_ref)):
        for at in range(0, half, half // 2):
            rows = pl.ds(pl.multiple_of(place * half + at, half // 2), half // 2)
            work_ref[rows] = ref[at : at + half // 2].astype(F32)
            copies.append(pltpu.make_async_copy(work_ref.at[rows], out_ref.at[rows], sems.at[len(copies)]))
            copies[-1].start()
    for copy in copies:
        copy.wait()


def wide_final(own_ref, other_ref, out_ref, *more):
    work_ref, sems = more[-2:]
    width, wide = out_ref.shape
    step = own_ref.shape[1]
    copies = []
    for place, ref in places(own_ref, other_ref):
        for at in range(wide // 2 // step):
            lanes = pl.ds(pl.multiple_of(place * (wide // 2) + at * step, step), step)
            work_ref[:, lanes] = ref[at * width : (at + 1) * width].astype(F32)
            copies.append(pltpu.make_async_copy(work_ref.at[:, lanes], out_ref.at[:, lanes], sems.at[len(copies)]))
            copies[-1].start()
        if len(more) > 2:
            half = width // 2
            more[1][pl.ds(pl.multiple_of(place * half, half), half)] = ref[wide // 2 // step * width :].astype(F32)
    if len(more) > 2:
        copies.append(pltpu.make_async_copy(more[1], more[0], sems.at[len(copies)]))
        copies[-1].start()
    for copy in copies:
        copy.wait()


def rest_final(own_ref, other_ref, q_ref, k_ref, v_ref, bog_ref, fgg_ref, gg_ref):
    width = q_ref.shape[0]
    half = width // 2
    for place, ref in places(own_ref, other_ref):
        lanes = pl.ds(pl.multiple_of(place * half, half), half)
        for at, out in enumerate((q_ref, k_ref, v_ref)):
            out[:, lanes] = ref[at * width : (at + 1) * width].astype(F32)
    own, other = (ref[3 * width : 3 * width + 16].astype(F32) for ref in (own_ref, other_ref))
    core = lax.axis_index("batch") & 1
    zero, one = jnp.where(core == 0, own, other), jnp.where(core == 0, other, own)
    count = bog_ref.shape[0] // half
    for out, rows, first in ((bog_ref, zero, 0), (fgg_ref, zero, count), (gg_ref, one, 0)):
        for at in range(out.shape[0] // half):
            out[at * half : (at + 1) * half] = rows[first + at]


def add_back_kernel(part_ref, returned_ref, out_ref):
    out_ref[...] = part_ref[...] + returned_ref[...].astype(F32)


def call(kernel, operands, results, scratch=(), limit=6, outside=0):
    nbytes = sum(a.size * a.dtype.itemsize for a in operands) + sum(
        math.prod(s) * jnp.dtype(d).itemsize for s, d in results
    )
    return pl.pallas_call(
        kernel,
        out_shape=tuple(jax.ShapeDtypeStruct(s, d) for s, d in results),
        in_specs=[VMEM] * len(operands),
        out_specs=tuple(HBM if i < outside else VMEM for i in range(len(results))),
        scratch_shapes=list(scratch),
        compiler_params=pltpu.CompilerParams(vmem_limit_bytes=limit * MEGA),
        cost_estimate=pl.CostEstimate(flops=STEP_FLOPS, bytes_accessed=nbytes, transcendentals=0),
    )(*operands)


def exchanges(batches, blocks):
    number = batches * blocks

    def pairs(partner):
        return [
            (d, p[0] * blocks + p[1])
            for d in range(number)
            for p in [partner(d // blocks, d % blocks)]
        ]

    flips = {
        "x": (lambda b, s: (b, s ^ 1), lambda b, s: s),
        "y": (lambda b, s: (b ^ 2, s), lambda b, s: (b & 2) // 2),
        "z": (lambda b, s: (b ^ 4, s), lambda b, s: (b & 4) // 4),
    }

    def flip(place):
        return (pairs(lambda b, s: (b ^ place, s)), lambda b, s: (b & place) // place)

    def mixed(way):
        (first, first_bit), (second, second_bit) = (flips[axis] for axis in way)
        return (
            pairs(lambda b, s: second(b, s) if b % 2 else first(b, s)),
            lambda b, s: jnp.where(b & 1 == 0, first_bit(b, s), second_bit(b, s)),
        )

    found = {way: mixed(way) for way in ("xy", "yx", "zy", "yz", "xz", "zx", "xx", "yy", "zz")}
    found["core"] = flip(1)
    rest = []
    place = 8
    while place < batches:
        rest.append(flip(place))
        place *= 2
    return found, rest


def added(left, right, rows):
    return (left[rows].astype(F32) + right[rows].astype(F32)).astype(BF16)


def halve_kernel(bit, kept_ref, arrived_ref, sent_ref, left_ref):
    half, mine = sent_ref.shape[0], bit(lax.axis_index("batch"), lax.axis_index("seq"))
    step = 16 * math.gcd(half // 16, 8)
    for place, ref in ((1 - mine, sent_ref), (mine, left_ref)):
        for at in range(0, half, step):
            rows = pl.ds(pl.multiple_of(place * half + at, 16), step)
            ref[at : at + step] = added(kept_ref, arrived_ref, rows)


def add_kernel(kept_ref, arrived_ref, out_ref):
    half = out_ref.shape[0]
    step = 16 * math.gcd(half // 16, 8)
    for at in range(0, half, step):
        out_ref[at : at + step] = added(kept_ref, arrived_ref, slice(at, at + step))


def double_kernel(bit, kept_ref, arrived_ref, out_ref):
    half, mine = kept_ref.shape[0], bit(lax.axis_index("batch"), lax.axis_index("seq"))
    for place, ref in ((mine, kept_ref), (1 - mine, arrived_ref)):
        out_ref[pl.ds(pl.multiple_of(place * half, 16), half)] = ref[...]


def choose_kernel(bit, kept0_ref, arrived0_ref, kept1_ref, arrived1_ref, sent_ref, left_ref):
    mine = bit(lax.axis_index("batch"), lax.axis_index("seq"))
    step = 128
    for at in range(0, sent_ref.shape[0], step):
        rows = slice(at, at + step)
        zero, one = added(kept0_ref, arrived0_ref, rows), added(kept1_ref, arrived1_ref, rows)
        left_ref[rows] = jnp.where(mine == 0, zero, one)
        sent_ref[rows] = jnp.where(mine == 0, one, zero)


def pick_kernel(bit, zero_ref, one_ref, sent_ref, left_ref):
    mine = bit(lax.axis_index("batch"), lax.axis_index("seq"))

    @pl.when(mine == 0)
    def _():
        left_ref[...] = zero_ref[...]
        sent_ref[...] = one_ref[...]

    @pl.when(mine != 0)
    def _():
        left_ref[...] = one_ref[...]
        sent_ref[...] = zero_ref[...]


class Sum:
    def __init__(self, halvings, fulls, sent, kept, finish):
        self.halvings, self.fulls, self.finish = halvings, fulls, finish
        self.sent, self.kept, self.arrived, self.at = sent, kept, None, 0

    def start(self, exchange):
        self.arrived = lax.ppermute(self.sent, AXES, exchange[0])

    def add(self):
        (self.kept,) = call(add_kernel, (self.kept, self.arrived), [(self.kept.shape, BF16)])
        self.sent = self.kept

    def advance(self, *after):
        count, at = len(self.halvings), self.at
        self.at += 1
        if at == 0:
            self.sent = fence(self.sent, *after)[0]
            self.start(self.halvings[0])
            return self.sent
        self.kept = fence(self.kept, *after)[0]
        rows, columns = self.kept.shape
        if at < count:
            self.sent, self.kept = call(
                functools.partial(halve_kernel, self.halvings[at][1]),
                (self.kept, self.arrived),
                [((rows // 2, columns), BF16)] * 2,
            )
            self.start(self.halvings[at])
        elif at == count:
            self.add()
            self.start(self.fulls[0])
        elif at == count + 1:
            for exchange in self.fulls[1:]:
                self.add()
                self.start(exchange)
            self.add()
            self.start(self.halvings[-1])
        elif at <= 2 * count:
            (self.kept,) = call(
                functools.partial(double_kernel, self.halvings[2 * count + 1 - at + 0][1]),
                (self.kept, self.arrived),
                [((rows * 2, columns), BF16)],
            )
            self.sent = self.kept
            self.start(self.halvings[2 * count - at])
        else:
            self.result = self.finish(self.kept, self.arrived)
            return self.result[0]
        return self.sent


def fence(*arrays):
    return lax.optimization_barrier(arrays)


def body(
    inputs,
    memory,
    cotangent,
    labels,
    attention_gain,
    query_weight,
    key_weight,
    value_weight,
    out_weight,
    forward_gain,
    up_weight,
    down_weight,
    boundary_hidden,
    boundary_out,
):
    group, block, width = inputs.shape
    wide, hidden_wide = up_weight.shape[1], boundary_hidden.shape[1]
    batches, blocks = (lax.axis_size("batch"), lax.axis_size("seq"))
    found, fulls = exchanges(batches, blocks)
    column = lax.axis_index("seq")
    core = lax.axis_index("batch") % 2
    rows = inputs.reshape(block, width)
    memory_rows = memory.reshape(block, width)
    onward = [(i, i + 1) for i in range(blocks - 1)]
    side1 = lax.ppermute(rows[TILE:], "seq", onward)
    tables = rotary_tables(-block, (blocks + 1) * block)
    cosine, sine = (
        lax.dynamic_slice_in_dim(jnp.asarray(t), column * block, 2 * block) for t in tables
    )
    gain = attention_gain.reshape(1, width)
    square, side_shape = (block, width), (TILE, width)
    turned_square, turned_side = (width, block), (width, TILE)
    normed_t, queries, queries_t, keys, keys_t, values, values_t = call(
        own_kernel,
        (rows, gain, query_weight, key_weight, value_weight, cosine, sine),
        [(turned_square, BF16), (square, BF16), (turned_square, BF16)]
        + [(square, BF16), (turned_square, BF16)] * 2,
    )
    side0 = lax.ppermute(fence(rows, queries)[0][:TILE], "seq", onward)
    side_results = [
        (side_shape, BF16), (side_shape, BF16), (side_shape, BF16), (turned_side, BF16),
        ((HEADS, 2 * TILE, TILE), BF16), (turned_side, BF16),
    ]
    sn1, sk1, sv1, sv_t1, weights1, mix1 = call(
        late_kernel,
        (memory_rows, side1, gain, key_weight, value_weight, cosine, sine, queries_t, keys, values_t),
        side_results,
    )
    sn0, sk0, sv0, sv_t0, weights0, mix0 = call(
        early_kernel,
        (memory_rows, side0, gain, key_weight, value_weight, cosine, sine, queries_t, keys, values_t, sk1, sv_t1),
        side_results,
    )
    bh_half = (hidden_wide // 2 * width // 512, 512)
    (
        hidden, normed_hidden, gated, slope, outputs, probe_grad, hidden_sent, hidden_kept, probe, signal,
    ) = call(
        forward_kernel,
        (
            rows, mix0, mix1, out_weight, forward_gain.reshape(1, width), up_weight, down_weight,
            boundary_hidden, boundary_out.reshape(1, hidden_wide), labels,
        ),
        [
            (square, F32), (square, BF16), ((block, wide), BF16),
            ((block, wide), BF16), (square, BF16), ((block, hidden_wide), BF16),
            (bh_half, BF16), (bh_half, BF16), ((block, hidden_wide), BF16), ((block, PAIR), F32),
        ],
        [
            pltpu.VMEM((block, hidden_wide), BF16),
            pltpu.VMEM((width, block), BF16),
        ],
        limit=18,
    )
    sums, made = {}, {}

    def add_sum(name, way, sent, kept, finish):
        sums[name] = Sum([found[w] for w in way], fulls, sent, kept, finish)

    add_sum(
        "hidden", ("core", "xy", "yx", "zz"), hidden_sent, hidden_kept,
        lambda own, other: call(
            wide_final, (own, other), [((width, hidden_wide), F32)],
            [pltpu.VMEM((width, hidden_wide), F32), pltpu.SemaphoreType.DMA((4,))], outside=1,
        ),
    )
    up_half = (wide // 2 * width // 512 + width // 2, 512)
    grads_shape = ((3 * width + 128, width // 2), BF16)
    work = [
        pltpu.VMEM((width // 2, block), F32),
        pltpu.VMEM((2 * block, width // 2), F32),
        pltpu.VMEM((2 * block, width // 2), BF16),
    ]
    def down_part(*after):
        grad = fence(probe_grad, *after)[0]
        final_grad, up_grad, sent, kept, boundary_out_grad, sn_t0, sn_t1, sk_t0, sk_t1 = call(
            down_kernel,
            (
                grad, boundary_hidden, cotangent.reshape(square), gated, slope, down_weight, probe, signal,
                sn0, sn1, sk0, sk1,
            ),
            [(square, F32), ((block, wide), BF16), ((wide // 2, width), BF16), ((wide // 2, width), BF16)]
            + [((1, hidden_wide), F32)] + [(turned_side, BF16)] * 4,
        )
        made["down"] = (final_grad, up_grad, boundary_out_grad)
        made["shared"] = (
            queries, sv0, sv1, values, sk_t0, sk_t1, keys_t,
            cosine, sine, normed_t, sn_t0, sn_t1, query_weight, key_weight, value_weight,
        )
        add_sum(
            "down", ("core", "zz", "xy", "yx"), sent, kept,
            lambda own, other: call(
                tall_final, (own, other), [((wide, width), F32)],
                [pltpu.VMEM((wide, width), F32), pltpu.SemaphoreType.DMA((4,))], outside=1,
            ),
        )
        return up_grad

    def up_part(*after):
        final_grad, up_grad, _ = made["down"]
        up_grad = fence(up_grad, *after)[0]
        hidden_grad, mixed_grad, mixed_grad_t, gain_part, sent, kept = call(
            up_kernel,
            (
                normed_hidden, up_grad, up_weight, hidden, forward_gain.reshape(1, width), final_grad,
                mix0, mix1, out_weight,
            ),
            [
                (square, F32), (square, BF16), (turned_square, BF16), ((1, width), F32),
                (up_half, BF16), (up_half, BF16),
            ],
            [pltpu.VMEM((width, block), BF16), pltpu.VMEM((width, block), BF16)],
        )
        made["up"] = (hidden_grad, (weights0, weights1, mixed_grad, mixed_grad_t) + made["shared"], gain_part)
        add_sum(
            "up", ("core", "xy", "yx", "zz"), sent, kept,
            lambda own, other: call(
                wide_final, (own, other), [((width, wide), F32), ((width, width), F32)],
                [pltpu.VMEM((width, width), F32), pltpu.VMEM((width, wide), F32), pltpu.SemaphoreType.DMA((5,))],
                outside=2,
            ),
        )
        return mixed_grad

    def attention0(*after):
        hidden_grad, operands, gain_part = made["up"]
        operands = (fence(weights0, *after)[0],) + operands[1:]
        made["attention"] = call(
            functools.partial(attention_kernel, 0, False),
            operands + (made["down"][2], gain_part),
            [(square, F32), (square, F32), grads_shape],
            work,
            limit=10,
        )
        return made["attention"][0]

    def attention1(*after):
        hidden_grad, operands, _ = made["up"]
        upstream, side_upstream, grads0 = made["attention"]
        upstream = fence(upstream, *after)[0]
        input_part, side_grad, grads1 = call(
            functools.partial(attention_kernel, 1, True),
            operands + (rows, memory_rows, side0, side1, gain, hidden_grad, upstream, side_upstream),
            [(square, F32), (square, BF16), grads_shape],
            work,
            limit=10,
        )
        made["input"] = (input_part, side_grad)
        picked = call(
            functools.partial(pick_kernel, found["core"][1]), (grads0, grads1), [grads_shape] * 2
        )
        add_sum(
            "rest", ("core", "xy", "yx", "zz"), *picked,
            lambda own, other: call(
                rest_final, (own, other), [((width, width), F32)] * 3 + [((hidden_wide,), F32), ((width,), F32), ((width,), F32)],
            ),
        )
        return picked[0]

    def send_back(*after):
        input_part, side_grad = made["input"]
        side_grad = fence(side_grad, *after)[0]
        made["returned"] = lax.ppermute(side_grad, "seq", [(i + 1, i) for i in range(blocks - 1)])
        return side_grad

    def add_back(*after):
        input_part = fence(made["input"][0], *after)[0]
        (made["input_grad"],) = call(add_back_kernel, (input_part, made["returned"]), [(square, F32)])
        return made["input_grad"]

    parts = {
        "a": down_part, "b": up_part, "c": attention0, "d": attention1, "r": send_back, "s": add_back,
    }
    names = {"H": "hidden", "D": "down", "U": "up", "T": "rest"}
    token = hidden_kept
    for letter in ORDER:
        token = parts[letter](token) if letter in parts else sums[names[letter]].advance(token)
    (hidden_total,), (down_total,) = (sums["hidden"].result, sums["down"].result)
    up_total, out_total = sums["up"].result
    query_total, key_total, value_total, boundary_out_total, forward_gain_total, gain_total = sums["rest"].result
    input_grad = made["input_grad"]
    return (
        outputs.reshape(inputs.shape),
        input_grad.reshape(inputs.shape),
        gain_total,
        query_total,
        key_total,
        value_total,
        out_total,
        forward_gain_total,
        up_total,
        down_total,
        hidden_total,
        boundary_out_total,
    )


def solution(mesh):
    placed = (
        P("batch", "seq", None),
        P("batch", None, None),
        P("batch", "seq", None),
        P("batch", "seq"),
        P(),
        P(),
        P(),
        P(),
        P(),
        P(),
        P(),
        P(),
        P(),
        P(),
    )
    return jax.shard_map(
        body,
        mesh=mesh,
        in_specs=placed,
        out_specs=(
            P("batch", "seq", None),
            P("batch", "seq", None),
            P(),
            P(),
            P(),
            P(),
            P(),
            P(),
            P(),
            P(),
            P(),
            P(),
        ),
        check_vma=False,
    )
```
